32 devices in a mesh: ens: 4 (over y, core), slab: 8 (over z, x).
Axes of the slice: x: 2, y: 2, z: 4, core: 2. Of those that a mesh axis runs over, the one named last changes fastest.
Arguments:
- tracer: float32 [32, 128, 4096], P('ens', 'slab'), may hold values from -6 to 6
- coefficients: float32 [4, 128, 4096], P(None, 'slab'), may hold values from -1.5 to 1.5, as said below
- parameters: float32 [32, 4096], P('ens'), may hold values from -6 to 6
- obs_index: int32 [16384], P('slab'), may hold values from 0 to 65535, as said below
- obs_values: float32 [32, 16384], P('ens', 'slab'), may hold values from -6 to 6
- obs_variance: float32 [16384], P('slab'), may hold values from 0.1 to 1
- member_group: int32 [32], replicated, may hold values from 0 to 7, as said below
Outputs:
- final_field: float32 [32, 128, 4096], P('ens', 'slab')
- updated_params: float32 [32, 4096], P('ens')
The draws below stay inside these ranges and needn't reach their ends.
Inputs may be any that keep to these rules, and one draw needn't show every extreme that they name: `obs_index`: every slab has an observation at flat index 0 and one at 65535; indices may repeat. `member_group`: every group holds exactly 4 members. `coefficients`: the Courant numbers lie within -0.3 to 0.3, the diffusion number within 0.02 to 0.1.
All inputs are finite; a program needn't handle non-finite values.
Results may differ from the reference program's by a relative error of at most 0.0003.
Values sent between devices are 32-bit elements; how exact they have to be, the bound alone decides.
No kernel may reach another device: no remote copies, remote signals or barrier semaphores. Data moves between devices by JAX's collectives and lax.ppermute only.
A program may use at most 128 MiB of HBM per device.

```python
import math
import jax
import jax.numpy as jnp
from jax import lax

P_SIZE = 4096
CX = 16
OBS_DEV = 2048
STEPS = 4
GROUPS = 8
MEMBERS = 32
NX = 128
NOBS = 16384
N_SLAB = 8


def draw_coefficients(key, part):
    subkeys = jax.random.split(key, 4)
    grid_shape = (NX, P_SIZE)
    speed_x = jax.random.uniform(subkeys[0], grid_shape, minval=-0.3, maxval=0.3)
    speed_y = jax.random.uniform(subkeys[1], grid_shape, minval=-0.3, maxval=0.3)
    diffusion = jnp.exp(jax.random.uniform(subkeys[2], grid_shape, minval=math.log(0.02), maxval=math.log(0.1)))
    pattern = 0.5 * jax.random.truncated_normal(subkeys[3], -3.0, 3.0, grid_shape)
    return jnp.stack([speed_x, speed_y, diffusion, pattern]).astype(jnp.float32)


def draw_obs_index(key, part):
    blocks = NOBS // OBS_DEV
    values = jax.random.randint(key, (blocks, OBS_DEV), 0, CX * P_SIZE, dtype=jnp.int32)
    values = values.at[:, 0].set(CX * P_SIZE - 1).at[:, 1].set(0)
    return values.reshape(NOBS)


def draw_member_group(key, part):
    shuffled = jax.random.permutation(key, MEMBERS)
    return (shuffled % GROUPS).astype(jnp.int32)


def block_scale(own_key, dims, cuts, smallest, top_value):
    gain, own = 1.0, jax.random.fold_in(own_key, 6)
    for dim, blocks in cuts:
        draws = jnp.exp(jax.random.uniform(jax.random.fold_in(own, dim), (blocks,), jnp.float32, smallest / len(cuts), top_value / len(cuts)))
        gain = gain * jnp.repeat(draws, dims[dim] // blocks).reshape([-1 if axis == dim else 1 for axis in range(len(dims))])
    return gain


def scatter_about(rng, extent, scale, reach, shards=(), kind=jnp.bfloat16):
    drawn = scale * jax.random.normal(rng, extent, jnp.float32)
    if shards:
        drawn = drawn * block_scale(rng, extent, shards, -0.22, 0.18)
    return jnp.clip(drawn, -reach, reach).astype(kind)


def setup_inputs(seed: int = 0) -> dict:
    streams_of = jax.random.split(jax.random.key(seed), 8)
    return {
        "tracer": scatter_about(streams_of[0], (MEMBERS, NX, P_SIZE), 1.0, 6.0, ((0, 4), (1, 8)), jnp.float32),
        "coefficients": draw_coefficients(jax.random.fold_in(streams_of[7], 71), 0),
        "parameters": scatter_about(streams_of[2], (MEMBERS, P_SIZE), 1.0, 6.0, ((0, 4),), jnp.float32),
        "obs_index": draw_obs_index(jax.random.fold_in(streams_of[7], 71), 0),
        "obs_values": scatter_about(streams_of[4], (MEMBERS, NOBS), 1.0, 6.0, ((0, 4), (1, 8)), jnp.float32),
        "obs_variance": jnp.clip(jnp.exp(math.log(1.0) - 2.3025851 * jax.random.uniform(streams_of[5], (NOBS,), jnp.float32) ** block_scale(streams_of[5], (NOBS,), ((0, 8),), -0.2, 0.2)), 0.1, 1.0),
        "member_group": draw_member_group(jax.random.fold_in(streams_of[7], 71), 0),
    }


def hdot(left, right):
    return jnp.dot(left.astype(jnp.float32), right.astype(jnp.float32), precision=lax.Precision.HIGHEST, preferred_element_type=jnp.float32)

def minmod(left, right):
    return jnp.where(left * right > 0.0, jnp.where(jnp.abs(left) < jnp.abs(right), left, right), 0.0)

def upwind(minus_two, minus_one, centre, plus_one, plus_two, speed):
    slope_back = minmod(minus_one - minus_two, centre - minus_one)
    slope_here = minmod(centre - minus_one, plus_one - centre)
    slope_next = minmod(plus_one - centre, plus_two - plus_one)
    forward = centre + 0.5 * slope_here - (minus_one + 0.5 * slope_back)
    backward = plus_one - 0.5 * slope_next - (centre - 0.5 * slope_here)
    return speed * jnp.where(speed > 0.0, forward, backward)

def advance(padded, coefficients, params):
    out_rows = padded.shape[-2] - 4
    along_x = [lax.slice_in_dim(padded, offset, offset + out_rows, axis=padded.ndim - 2) for offset in range(5)]
    centre = along_x[2]
    along_y = [jnp.roll(centre, shift, axis=-1) for shift in (2, 1, 0, -1, -2)]
    advection = upwind(*along_x, coefficients[0]) + upwind(*along_y, coefficients[1])
    laplace = along_x[1] + along_x[3] + along_y[1] + along_y[3] - 4.0 * centre
    source = jnp.expand_dims(params, -2) * coefficients[3]
    return centre - advection + coefficients[2] * laplace + source

def reference(tracer, coefficients, parameters, obs_index, obs_values, obs_variance, member_group):

    def one_member(item):
        field_now, row_params = item
        for step_index in range(STEPS):
            field_now = advance(jnp.pad(field_now, ((2, 2), (0, 0))), coefficients, row_params)
        return field_now
    final_field = lax.map(one_member, (tracer, parameters))
    flat_state = final_field.reshape(MEMBERS, N_SLAB, CX * P_SIZE)
    where_obs = jnp.broadcast_to(obs_index.reshape(1, N_SLAB, OBS_DEV), (MEMBERS, N_SLAB, OBS_DEV))
    predicted = jnp.take_along_axis(flat_state, where_obs, axis=2).reshape(MEMBERS, NOBS)
    weight = 1.0 / (obs_variance * NOBS)
    innovation = (obs_values - predicted) * weight[None, :]
    same_group = (member_group[:, None] == member_group[None, :]).astype(jnp.float32)
    per_group = MEMBERS // GROUPS
    spread = 1.0 / math.sqrt(per_group - 1)
    anomalies = (predicted - hdot(same_group, predicted) / per_group) * spread
    gram = hdot(anomalies * weight[None, :], anomalies.T)
    mixed = hdot(anomalies, innovation.T)
    system = jnp.eye(MEMBERS, dtype=jnp.float32) + same_group * gram
    factor = jnp.linalg.cholesky(system)
    solved = jax.scipy.linalg.solve_triangular(factor, same_group * mixed, lower=True)
    solved = jax.scipy.linalg.solve_triangular(factor.T, solved, lower=False)
    param_anomalies = (parameters - hdot(same_group, parameters) / per_group) * spread
    updated_params = parameters + hdot(solved.T, param_anomalies)
    return (final_field, updated_params)
```

```python
import functools
import math

import jax
import jax.numpy as jnp
from jax import lax
from jax.experimental import pallas as pl
from jax.experimental.pallas import tpu as pltpu
from jax.sharding import PartitionSpec as P

STEPS = 4
GROUPS = 8
HALO = 2 * STEPS
LANES = 128
SUBLANES = 8
ROWS = 16
GROUP = 4
LAG = 3
WIDE = 4
VMEM_LIMIT = 48 * 1024 * 1024
ANYWHERE = pl.BlockSpec(memory_space=pl.ANY)
IN_VMEM = pl.BlockSpec(memory_space=pltpu.VMEM)
IN_SMEM = pl.BlockSpec(memory_space=pltpu.SMEM)


def hdot(left, right):
    return jnp.dot(left, right, precision=lax.Precision.HIGHEST, preferred_element_type=jnp.float32)


def limited(left, right):
    return jnp.minimum(jnp.maximum(left, jnp.minimum(right, 0.0)), jnp.maximum(right, 0.0))


def block_at(block):
    return pl.ds(pl.multiple_of(block * LANES, LANES), LANES)


def wide(row):
    return jnp.broadcast_to(row, (SUBLANES, LANES))


def columns_pass(level, row, levels, coef, params, blocks):
    lane = lax.broadcasted_iota(jnp.int32, (SUBLANES, LANES), 1)
    first, last = lane == 0, lane == LANES - 1
    c, c_rolled, d, d_rolled, slope, twice, left, right, laplace = ({} for _ in range(9))
    for tick in range(blocks + 2 * LAG + 4):
        b = tick - 1
        if b <= blocks:
            c[b] = levels[level, row, :, block_at(b % blocks)]
            c_rolled[b] = pltpu.roll(c[b], LANES - 1, 1)
        b = tick - 2 if tick - 2 < blocks else tick - 2
        if -1 <= b <= blocks:
            c_next = jnp.where(last, c_rolled[b + 1], c_rolled[b]) if b < blocks else c_rolled[b]
            d[b] = c_next - c[b]
            d_rolled[b] = pltpu.roll(d[b], 1, 1)
        b = tick - 2 - LAG
        if -1 <= b <= blocks:
            d_back = jnp.where(first, d_rolled[b - 1], d_rolled[b]) if b >= 0 else d_rolled[b]
            slope[b] = limited(d_back, d[b])
            twice[b] = d[b] + d[b]
            laplace[b] = d[b] - d_back
            left[b] = pltpu.roll(twice[b] - slope[b], 1, 1)
            right[b] = pltpu.roll(slope[b], LANES - 1, 1)
        b = tick - 3 - 2 * LAG
        if 0 <= b < blocks:
            at = block_at(b)
            speed = wide(coef[1, row, :, at])
            forward = jnp.where(first, left[b - 1], left[b])
            backward = twice[b] - jnp.where(last, right[b + 1], right[b])
            value = c[b] - speed * (jnp.where(speed > 0.0, forward, backward) + slope[b])
            value = value + wide(coef[2, row, :, at]) * laplace[b]
            value = value + params[:, at] * wide(coef[3, row, :, at])
            levels[level + 1, row, :, at] = value


def rows_pass(level, row, levels, coef, at):
    c = [levels[level, row - 2 + i, :, at] for i in range(GROUP + 4)]
    d = [c[i + 1] - c[i] for i in range(GROUP + 3)]
    slope = [None] + [limited(d[i - 1], d[i]) for i in range(1, GROUP + 3)]
    twice = [None] + [d[i] + d[i] for i in range(1, GROUP + 2)]
    for i in range(2, GROUP + 2):
        here = row - 2 + i
        speed = wide(coef[0, here, :, at])
        forward = twice[i - 1] - slope[i - 1]
        backward = twice[i] - slope[i + 1]
        change = wide(coef[2, here, :, at]) * (d[i] - d[i - 1])
        change = change - speed * (jnp.where(speed > 0.0, forward, backward) + slope[i])
        levels[level + 1, here, :, at] = levels[level + 1, here, :, at] + change


def advance_group(level, row, levels, coef, params, blocks):
    @pl.loop(0, GROUP)
    def _(i):
        columns_pass(level, row + i, levels, coef, params, blocks)

    @pl.loop(0, blocks // WIDE)
    def _(wide_block):
        for i in range(WIDE):
            rows_pass(level, row, levels, coef, block_at(wide_block * WIDE + i))


class Copies:
    def __init__(self, sems):
        self.sems, self.used = sems, 0

    def start(self, source, target):
        copy = pltpu.make_async_copy(source, target, self.sems.at[self.used])
        self.used += 1
        copy.start()
        return copy


def place(row):
    return pl.ds(row + HALO, GROUP)


def to_rows_kernel(blocks, tracer, *rest):
    outs, (staged, sems) = rest[: ROWS // GROUP], rest[ROWS // GROUP :]

    def copy(block):
        return pltpu.make_async_copy(tracer.at[:, block_at(block)], staged.at[block], sems.at[block])

    @pl.loop(0, blocks)
    def _(block):
        copy(block).start()

    @pl.loop(0, blocks)
    def _(block):
        copy(block).wait()
        for row in range(ROWS):
            outs[row // GROUP][row % GROUP, :, block_at(block)] = staged[
                block, pl.ds(row, SUBLANES, stride=ROWS), :
            ]


def interior_kernel(blocks, own0, own1, own2, own3, own_coef, params, *rest):
    outs, (levels, coef, sems) = rest[:5], rest[5:]
    copies = Copies(sems)
    waits = [
        copies.start(own, levels.at[0, place(GROUP * i)])
        for i, own in enumerate((own0, own1, own2, own3))
    ]
    waits.append(copies.start(own_coef, coef.at[:, HALO : HALO + ROWS]))
    for copy in waits:
        copy.wait()
    for level, start, count in ((0, 2, 3), (1, 4, 2), (2, 6, 1)):
        @pl.loop(0, count)
        def _(i):
            advance_group(level, start + HALO + GROUP * i, levels, coef, params, blocks)

    waits = [
        copies.start(levels.at[level, place(row)], out)
        for out, (level, row) in zip(outs, ((1, 2), (1, 10), (2, 4), (2, 8), (3, 6)))
    ]
    for copy in waits:
        copy.wait()


def edge_steps(outer, blocks, copies, waits, levels, coef, params, ready):
    for level in range(STEPS):
        for copy in waits[level]:
            copy.wait()
        low, high = 2 * level - outer, ROWS + outer - GROUP - 2 * level

        @pl.loop(0, 2)
        def _(side):
            advance_group(
                level, low + HALO + side * (high - low), levels, coef, params, blocks
            )

        ready(level, low, high)


def load_coef(copies, own_coef, gathered, coef):
    return [
        copies.start(own_coef, coef.at[:, HALO : HALO + ROWS]),
        copies.start(gathered.at[:, 0:HALO], coef.at[:, 0:HALO]),
        copies.start(gathered.at[:, HALO : 2 * HALO], coef.at[:, HALO + ROWS :]),
    ]


def middle_kernel(blocks, *refs):
    sources, refs = refs[:9], refs[9:]
    own_coef, gathered, params = refs[:3]
    outs, (levels, coef, sems) = refs[3:11], refs[11:]
    copies = Copies(sems)
    places = ((0, -4), (0, 0), (0, 12), (0, 16), (1, 2), (1, 10), (2, 4), (2, 8), (3, 6))
    waits = [[] for _ in range(STEPS)]
    for source, (level, row) in zip(sources, places):
        waits[level].append(copies.start(source, levels.at[level, place(row)]))
    waits[0] += load_coef(copies, own_coef, gathered, coef)
    sends = []

    def ready(level, low, high):
        for row, out in ((low, outs[2 * level]), (high, outs[2 * level + 1])):
            sends.append(copies.start(levels.at[level + 1, place(row)], out))

    edge_steps(2, blocks, copies, waits, levels, coef, params, ready)
    for copy in sends:
        copy.wait()


def last_kernel(blocks, *refs):
    sources, refs = refs[:12], refs[12:]
    own_coef, gathered, params, row_of, offset_of, shift_of = refs[:6]
    out, predicted, levels, coef, staged, sems, out_sems = refs[6:]
    copies = Copies(sems)
    places = (
        (0, -8), (0, -4), (0, 16), (0, 20),
        (1, -2), (1, 14), (2, 0), (2, 12), (3, 2), (3, 10), (4, 4), (4, 8),
    )
    waits = [[] for _ in range(STEPS + 1)]
    for source, (level, row) in zip(sources, places):
        waits[level].append(copies.start(source, levels.at[level, place(row)]))
    waits[0] += load_coef(copies, own_coef, gathered, coef)
    edge_steps(6, blocks, copies, waits, levels, coef, params, lambda *_: None)
    for copy in waits[STEPS]:
        copy.wait()

    def out_copy(block):
        return pltpu.make_async_copy(staged.at[block], out.at[:, block_at(block)], out_sems.at[block])

    @pl.loop(0, blocks)
    def _(block):
        for row in range(ROWS):
            staged[block, pl.ds(row, SUBLANES, stride=ROWS), :] = levels[
                STEPS, HALO + row, :, block_at(block)
            ]
        out_copy(block).start()

    lane = lax.broadcasted_iota(jnp.int32, (SUBLANES, LANES), 1)

    @pl.loop(0, predicted.shape[1] // LANES)
    def _(block):
        base = block * LANES
        found = jnp.zeros((SUBLANES, LANES), jnp.float32)
        for i in range(LANES):
            at = pl.ds(pl.multiple_of(offset_of[base + i], LANES), LANES)
            value = levels[STEPS, row_of[base + i], :, at]
            found = jnp.where(lane == i, pltpu.roll(value, shift_of[base + i], 1), found)
        predicted[:, block_at(block)] = found

    @pl.loop(0, blocks)
    def _(block):
        out_copy(block).wait()


def scratch(columns, sems):
    return [
        pltpu.VMEM((STEPS + 1, ROWS + 2 * HALO, SUBLANES, columns), jnp.float32),
        pltpu.VMEM((4, ROWS + 2 * HALO, 1, columns), jnp.float32),
    ], pltpu.SemaphoreType.DMA((sems,))


def kernel_call(body, name, outs, specs, out_specs, scratches, units, operands):
    return pl.pallas_call(
        body,
        out_shape=tuple(jax.ShapeDtypeStruct(shape, jnp.float32) for shape in outs),
        in_specs=specs,
        out_specs=out_specs,
        scratch_shapes=scratches,
        compiler_params=pltpu.CompilerParams(vmem_limit_bytes=VMEM_LIMIT),
        cost_estimate=pl.CostEstimate(
            flops=units * 40 * 32768, bytes_accessed=8 << 20, transcendentals=0
        ),
        name=name,
    )(*operands)


def transport(tracer, own_coef, halo_coef, params, obs_index, halos):
    members, rows, columns = tracer.shape
    if members != SUBLANES or rows != ROWS:
        raise ValueError("block shape")
    blocks = columns // LANES
    group = (GROUP, members, columns)
    flat = (members * rows, columns)
    own = kernel_call(
        functools.partial(to_rows_kernel, blocks), "to_rows",
        [group] * 4, [ANYWHERE], (IN_VMEM,) * 4,
        [pltpu.VMEM((blocks, members * rows, LANES), jnp.float32), pltpu.SemaphoreType.DMA((blocks,))],
        4, [tracer.reshape(flat)],
    )
    low0, high0, low1, high1 = halos(own)
    buffers, sems = scratch(columns, 10)
    inner = kernel_call(
        functools.partial(interior_kernel, blocks), "interior",
        [group] * 5, [ANYWHERE] * 5 + [IN_VMEM], (ANYWHERE,) * 5,
        buffers + [sems], 24, [*own, own_coef, params],
    )
    buffers, sems = scratch(columns, 20)
    first = kernel_call(
        functools.partial(middle_kernel, blocks), "edge_first",
        [group] * 8, [ANYWHERE] * 11 + [IN_VMEM], (ANYWHERE,) * 8,
        buffers + [sems], 32,
        [low0, own[0], own[3], high0, *inner, own_coef, halo_coef, params],
    )
    row_of = obs_index // columns + HALO
    lane_of = obs_index % LANES
    offset_of = obs_index % columns - lane_of
    shift_of = (jnp.arange(obs_index.shape[0], dtype=jnp.int32) - lane_of) % LANES
    buffers, sems = scratch(columns, 15)
    field, predicted = kernel_call(
        functools.partial(last_kernel, blocks), "edge_last",
        [flat, (members, obs_index.shape[0])],
        [ANYWHERE] * 14 + [IN_VMEM] + [IN_SMEM] * 3, (ANYWHERE, IN_VMEM),
        buffers + [pltpu.VMEM((blocks, members * rows, LANES), jnp.float32), sems, pltpu.SemaphoreType.DMA((blocks,))],
        40,
        [low1, low0, high0, high1, *first, own_coef, halo_coef, params, row_of, offset_of, shift_of],
    )
    return field.reshape(tracer.shape), predicted


def products_kernel(total_obs, per_group, spread, everyone, own, values, variance, same, out):
    weight = 1.0 / (variance[...] * total_obs)
    innovation = (values[...] - own[...]) * weight
    predicted = everyone[...]
    anomalies = (predicted - hdot(same[...], predicted) / per_group) * spread
    right = jnp.concatenate([anomalies * weight, innovation], axis=0)
    out[...] = lax.dot_general(
        anomalies,
        right,
        (((1,), (1,)), ((), ())),
        precision=lax.Precision.HIGHEST,
        preferred_element_type=jnp.float32,
    )


def update_kernel(per_group, summands, same, own_same, rank_row, rank_col, anomalies, own, out):
    members = same.shape[0]
    total = summands[0]
    for index in range(1, summands.shape[0]):
        total = total + summands[index]
    together = same[...]
    row = lax.broadcasted_iota(jnp.int32, (members, members), 0)
    col = lax.broadcasted_iota(jnp.int32, (members, members), 1)
    system = jnp.where(row == col, 1.0, 0.0) + together * total[:, 0:members]
    right = own_same[...] * total[:, members:]
    for pivot in range(per_group):
        pick = jnp.where(rank_row[...] == pivot, together, 0.0)
        pivot_system = hdot(pick, system)
        pivot_right = hdot(pick, right)
        pivot_value = jnp.sum(pick * pivot_system, axis=1, keepdims=True)
        factor = jnp.sum(pick * system, axis=1, keepdims=True)
        is_pivot = rank_col[...] == pivot
        scale = 1.0 / pivot_value
        scaled_system, scaled_right = pivot_system * scale, pivot_right * scale
        system = jnp.where(is_pivot, scaled_system, system - factor * scaled_system)
        right = jnp.where(is_pivot, scaled_right, right - factor * scaled_right)
    change = lax.dot_general(
        right,
        anomalies[...],
        (((0,), (0,)), ((), ())),
        precision=lax.Precision.HIGHEST,
        preferred_element_type=jnp.float32,
    )
    out[...] = own[...] + change


def local(tracer, coefficients, parameters, obs_index, obs_values, obs_variance, member_group):
    local_members, rows, columns = tracer.shape
    ens_pos = lax.axis_index("ens")
    ens_count = lax.axis_size("ens")
    slab_count = lax.axis_size("slab")
    if ens_count != coefficients.shape[0] or slab_count & (slab_count - 1):
        raise ValueError("mesh shape")
    forward = [(i, i + 1) for i in range(slab_count - 1)]
    backward = [(target, source) for source, target in forward]

    halving = jnp.array([0.5, 0.5, 1.0, 1.0], jnp.float32)[:, None, None]
    own_array = lax.dynamic_slice_in_dim(coefficients, ens_pos, 1, 0)[0]
    coef_low = lax.ppermute(own_array[rows - HALO :], "slab", forward)
    coef_high = lax.ppermute(own_array[:HALO], "slab", backward)
    shared = jnp.concatenate([coef_low, coef_high, parameters], axis=0)
    gathered = lax.all_gather(shared, "ens", axis=0, tiled=False)
    own_coef = (coefficients * halving)[:, :, None, :]
    halo_coef = (gathered[:, : 2 * HALO] * halving)[:, :, None, :]

    def halos(own):
        low0 = lax.ppermute(own[3], "slab", forward)
        high0 = lax.ppermute(own[0], "slab", backward)
        low1 = lax.ppermute(own[2], "slab", forward)
        high1 = lax.ppermute(own[1], "slab", backward)
        return low0, high0, low1, high1

    members = member_group.shape[0]
    per_group = members // GROUPS
    spread = 1.0 / math.sqrt(per_group - 1)
    same_bool = member_group[:, None] == member_group[None, :]
    same = same_bool.astype(jnp.float32)
    earlier = jnp.arange(members)[None, :] < jnp.arange(members)[:, None]
    rank = jnp.sum((same_bool & earlier).astype(jnp.int32), axis=1)
    own_same = lax.dynamic_slice_in_dim(same, ens_pos * local_members, local_members, 1)
    all_params = gathered[:, 2 * HALO :, :].reshape(members, columns)
    param_anomalies = (all_params - hdot(same, all_params) / per_group) * spread

    field, predicted = transport(tracer, own_coef, halo_coef, parameters, obs_index, halos)
    everyone = lax.all_gather(predicted, "ens", axis=0, tiled=True)
    total_obs = obs_variance.shape[0] * slab_count
    products = pl.pallas_call(
        functools.partial(products_kernel, float(total_obs), per_group, spread),
        out_shape=jax.ShapeDtypeStruct((members, members + local_members), jnp.float32),
        compiler_params=pltpu.CompilerParams(vmem_limit_bytes=VMEM_LIMIT),
        name="products",
    )(everyone, predicted, obs_values, obs_variance[None, :], same)
    distance = 1
    while distance < slab_count:
        pairs = [(i, i ^ distance) for i in range(slab_count)]
        products = products + lax.ppermute(products, "slab", pairs)
        distance *= 2
    updated = pl.pallas_call(
        functools.partial(update_kernel, per_group),
        out_shape=jax.ShapeDtypeStruct(parameters.shape, jnp.float32),
        compiler_params=pltpu.CompilerParams(vmem_limit_bytes=VMEM_LIMIT),
        name="update",
    )(products[None], same, own_same, rank[None, :], rank[:, None], param_anomalies, parameters)
    return (field, updated)


def solution(mesh):
    in_specs = (
        P("ens", "slab", None),
        P(None, "slab", None),
        P("ens", None),
        P("slab"),
        P("ens", "slab"),
        P("slab"),
        P(),
    )
    out_specs = (P("ens", "slab", None), P("ens", None))
    return jax.shard_map(local, mesh=mesh, in_specs=in_specs, out_specs=out_specs, check_vma=False)
```

```python
import functools
import math

import jax
import jax.numpy as jnp
from jax import lax
from jax.experimental import pallas as pl
from jax.experimental.pallas import tpu as pltpu
from jax.sharding import PartitionSpec as P

STEPS = 4
GROUPS = 8
HALO = 2 * STEPS
LANES = 128
SUBLANES = 8
ROWS = 16
GROUP = 4
LAG = 3
WIDE = 8
TOGETHER = 2
VMEM_LIMIT = 30 * 1024 * 1024
TALL_LIMIT = 60 * 1024 * 1024
ANYWHERE = pl.BlockSpec(memory_space=pl.ANY)
IN_VMEM = pl.BlockSpec(memory_space=pltpu.VMEM)
IN_SMEM = pl.BlockSpec(memory_space=pltpu.SMEM)


def hdot(left, right):
    return jnp.dot(left, right, precision=lax.Precision.HIGHEST, preferred_element_type=jnp.float32)


def limited(left, right):
    return jnp.minimum(jnp.maximum(left, jnp.minimum(right, 0.0)), jnp.maximum(right, 0.0))


def block_at(block):
    return pl.ds(pl.multiple_of(block * LANES, LANES), LANES)


def wide(row):
    return jnp.broadcast_to(row, (SUBLANES, LANES))


def columns_pass(source, first_row, count, target, target_row, coef, params, blocks):
    lane = lax.broadcasted_iota(jnp.int32, (SUBLANES, LANES), 1)
    first, last = lane == 0, lane == LANES - 1
    c, c_rolled, d, d_rolled, slope, twice, left, right, laplace = ({} for _ in range(9))
    for tick in range(blocks + 2 * LAG + 4):
        for i in range(count):
            row = first_row + i
            b = tick - 1
            if b <= blocks:
                c[i, b] = source[row, :, block_at(b % blocks)]
                c_rolled[i, b] = pltpu.roll(c[i, b], LANES - 1, 1)
            b = tick - 2
            if -1 <= b <= blocks:
                c_next = c_rolled[i, b]
                if b < blocks:
                    c_next = jnp.where(last, c_rolled[i, b + 1], c_next)
                d[i, b] = c_next - c[i, b]
                d_rolled[i, b] = pltpu.roll(d[i, b], 1, 1)
            b = tick - 2 - LAG
            if -1 <= b <= blocks:
                d_back = d_rolled[i, b]
                if b >= 0:
                    d_back = jnp.where(first, d_rolled[i, b - 1], d_back)
                slope[i, b] = limited(d_back, d[i, b])
                twice[i, b] = d[i, b] + d[i, b]
                laplace[i, b] = d[i, b] - d_back
                left[i, b] = pltpu.roll(twice[i, b] - slope[i, b], 1, 1)
                right[i, b] = pltpu.roll(slope[i, b], LANES - 1, 1)
            b = tick - 3 - 2 * LAG
            if 0 <= b < blocks:
                at = block_at(b)
                speed = wide(coef[1, row, :, at])
                forward = jnp.where(first, left[i, b - 1], left[i, b])
                backward = twice[i, b] - jnp.where(last, right[i, b + 1], right[i, b])
                change = jnp.where(speed > 0.0, forward, backward) + slope[i, b]
                value = c[i, b] - (0.5 * speed) * change
                value = value + wide(coef[2, row, :, at]) * laplace[i, b]
                value = value + params[:, at] * wide(coef[3, row, :, at])
                target[target_row + i, :, at] = value


def rows_pass(source, row, partial, target, coef, at):
    c = [source[row - 2 + i, :, at] for i in range(GROUP + 4)]
    d = [c[i + 1] - c[i] for i in range(GROUP + 3)]
    slope = [None] + [limited(d[i - 1], d[i]) for i in range(1, GROUP + 3)]
    twice = [None] + [d[i] + d[i] for i in range(1, GROUP + 2)]
    for i in range(2, GROUP + 2):
        here = row - 2 + i
        speed = wide(coef[0, here, :, at])
        forward = twice[i - 1] - slope[i - 1]
        backward = twice[i] - slope[i + 1]
        change = wide(coef[2, here, :, at]) * (d[i] - d[i - 1])
        change = change - (0.5 * speed) * (jnp.where(speed > 0.0, forward, backward) + slope[i])
        target[here, :, at] = partial[i - 2, :, at] + change


def advance_group(source, target, row, partial, coef, params, blocks):
    @pl.loop(0, GROUP // TOGETHER)
    def _(i):
        columns_pass(
            source, row + i * TOGETHER, TOGETHER, partial, i * TOGETHER, coef, params, blocks
        )

    @pl.loop(0, blocks // WIDE)
    def _(wide_block):
        for i in range(WIDE):
            rows_pass(source, row, partial, target, coef, block_at(wide_block * WIDE + i))


class Copies:
    def __init__(self, sems):
        self.sems, self.used = sems, 0

    def start(self, source, target):
        copy = pltpu.make_async_copy(source, target, self.sems.at[self.used])
        self.used += 1
        copy.start()
        return copy


def place(row):
    return pl.ds(row + HALO, GROUP)


def to_rows_kernel(blocks, tracer, *rest):
    outs, (staged, sems) = rest[: ROWS // GROUP], rest[ROWS // GROUP :]

    def copy(block):
        return pltpu.make_async_copy(tracer.at[:, block_at(block)], staged.at[block], sems.at[block])

    @pl.loop(0, blocks)
    def _(block):
        copy(block).start()

    @pl.loop(0, blocks)
    def _(block):
        copy(block).wait()
        for row in range(ROWS):
            outs[row // GROUP][row % GROUP, :, block_at(block)] = staged[
                block, pl.ds(row, SUBLANES, stride=ROWS), :
            ]


def interior_kernel(blocks, own0, own1, own2, own3, own_coef, params, *rest):
    outs, (*levels, partial, coef, sems) = rest[:5], rest[5:]
    copies = Copies(sems)
    waits = [
        copies.start(own, levels[0].at[place(GROUP * i)])
        for i, own in enumerate((own0, own1, own2, own3))
    ]
    waits.append(copies.start(own_coef, coef.at[:, HALO : HALO + ROWS, 0]))
    for copy in waits:
        copy.wait()
    for level, start, count in ((0, 2, 3), (1, 4, 2), (2, 6, 1)):
        @pl.loop(0, count)
        def _(i):
            row = start + HALO + GROUP * i
            advance_group(levels[level], levels[level + 1], row, partial, coef, params, blocks)

    waits = [
        copies.start(levels[level].at[place(row)], out)
        for out, (level, row) in zip(outs, ((1, 2), (1, 10), (2, 4), (2, 8), (3, 6)))
    ]
    for copy in waits:
        copy.wait()


def edge_steps(outer, blocks, waits, levels, partial, coef, params, ready):
    for level in range(STEPS):
        for copy in waits[level]:
            copy.wait()
        low, high = 2 * level - outer, ROWS + outer - GROUP - 2 * level

        @pl.loop(0, 2)
        def _(side):
            row = low + HALO + side * (high - low)
            advance_group(levels[level], levels[level + 1], row, partial, coef, params, blocks)

        ready(level, low, high)


def load_coef(copies, own_coef, gathered, coef):
    return [
        copies.start(own_coef, coef.at[:, HALO : HALO + ROWS, 0]),
        copies.start(gathered.at[:, 0:HALO], coef.at[:, 0:HALO, 0]),
        copies.start(gathered.at[:, HALO : 2 * HALO], coef.at[:, HALO + ROWS :, 0]),
    ]


def middle_kernel(blocks, *refs):
    sources, refs = refs[:9], refs[9:]
    own_coef, gathered, params = refs[:3]
    outs, (*levels, partial, coef, sems) = refs[3:11], refs[11:]
    copies = Copies(sems)
    places = ((0, -4), (0, 0), (0, 12), (0, 16), (1, 2), (1, 10), (2, 4), (2, 8), (3, 6))
    waits = [[] for _ in range(STEPS)]
    for source, (level, row) in zip(sources, places):
        waits[level].append(copies.start(source, levels[level].at[place(row)]))
    waits[0] += load_coef(copies, own_coef, gathered, coef)
    sends = []

    def ready(level, low, high):
        for row, out in ((low, outs[2 * level]), (high, outs[2 * level + 1])):
            sends.append(copies.start(levels[level + 1].at[place(row)], out))

    edge_steps(2, blocks, waits, levels, partial, coef, params, ready)
    for copy in sends:
        copy.wait()


def last_kernel(blocks, *refs):
    sources, refs = refs[:12], refs[12:]
    own_coef, gathered, params, row_of, offset_of, shift_of = refs[:6]
    out, predicted, *levels, partial, coef, staged, sems, out_sems = refs[6:]
    copies = Copies(sems)
    places = (
        (0, -8), (0, -4), (0, 16), (0, 20),
        (1, -2), (1, 14), (2, 0), (2, 12), (3, 2), (3, 10), (4, 4), (4, 8),
    )
    waits = [[] for _ in range(STEPS + 1)]
    for source, (level, row) in zip(sources, places):
        waits[level].append(copies.start(source, levels[level].at[place(row)]))
    waits[0] += load_coef(copies, own_coef, gathered, coef)
    edge_steps(6, blocks, waits, levels, partial, coef, params, lambda *_: None)
    for copy in waits[STEPS]:
        copy.wait()

    def out_copy(block):
        return pltpu.make_async_copy(staged.at[block], out.at[:, block_at(block)], out_sems.at[block])

    @pl.loop(0, blocks)
    def _(block):
        for row in range(ROWS):
            staged[block, pl.ds(row, SUBLANES, stride=ROWS), :] = levels[STEPS][
                HALO + row, :, block_at(block)
            ]
        out_copy(block).start()

    lane = lax.broadcasted_iota(jnp.int32, (SUBLANES, LANES), 1)

    @pl.loop(0, predicted.shape[1] // LANES)
    def _(block):
        base = block * LANES
        found = jnp.zeros((SUBLANES, LANES), jnp.float32)
        for i in range(LANES):
            at = pl.ds(pl.multiple_of(offset_of[base + i], LANES), LANES)
            value = levels[STEPS][row_of[base + i], :, at]
            found = jnp.where(lane == i, pltpu.roll(value, shift_of[base + i], 1), found)
        predicted[:, block_at(block)] = found

    @pl.loop(0, blocks)
    def _(block):
        out_copy(block).wait()


def scratch(columns, *more):
    return (
        [pltpu.VMEM((ROWS + 2 * HALO, SUBLANES, columns), jnp.float32)] * (STEPS + 1)
        + [
            pltpu.VMEM((GROUP, SUBLANES, columns), jnp.float32),
            pltpu.VMEM((4, ROWS + 2 * HALO, 1, columns), jnp.float32),
        ]
        + list(more)
    )


def kernel_call(body, name, outs, specs, out_specs, scratches, cost, operands, limit=VMEM_LIMIT):
    return pl.pallas_call(
        body,
        out_shape=tuple(jax.ShapeDtypeStruct(shape, jnp.float32) for shape in outs),
        in_specs=specs,
        out_specs=out_specs,
        scratch_shapes=scratches,
        compiler_params=pltpu.CompilerParams(vmem_limit_bytes=limit),
        cost_estimate=pl.CostEstimate(flops=0, bytes_accessed=cost * 3600000, transcendentals=0),
        name=name,
    )(*operands)


def row_groups(tracer):
    members, rows, columns = tracer.shape
    if members != SUBLANES or rows != ROWS:
        raise ValueError("block shape")
    blocks = columns // LANES
    return kernel_call(
        functools.partial(to_rows_kernel, blocks), "to_rows",
        [(GROUP, members, columns)] * 4, [ANYWHERE], (IN_VMEM,) * 4,
        [
            pltpu.VMEM((blocks, members * rows, LANES), jnp.float32),
            pltpu.SemaphoreType.DMA((blocks,)),
        ],
        3, [tracer.reshape(members * rows, columns)], TALL_LIMIT,
    )


def transport(shape, own, own_coef, halo_coef, params, obs_index, halos):
    members, rows, columns = shape
    blocks = columns // LANES
    group = (GROUP, members, columns)
    flat = (members * rows, columns)
    dma = pltpu.SemaphoreType.DMA
    staged = pltpu.VMEM((blocks, members * rows, LANES), jnp.float32)
    low0, high0 = halos(own[3], own[0])
    inner = kernel_call(
        functools.partial(interior_kernel, blocks), "interior",
        [group] * 5, [ANYWHERE] * 5 + [IN_VMEM], (ANYWHERE,) * 5,
        scratch(columns, dma((10,))), 8, [*own, own_coef, params],
    )
    upper, lower, low0, high0, *_ = lax.optimization_barrier(
        (own[2], own[1], low0, high0, inner[0])
    )
    low1, high1 = halos(upper, lower)
    first = kernel_call(
        functools.partial(middle_kernel, blocks), "edge_first",
        [group] * 8, [ANYWHERE] * 11 + [IN_VMEM], (ANYWHERE,) * 8,
        scratch(columns, dma((20,))), 10,
        [low0, own[0], own[3], high0, *inner, own_coef, halo_coef, params],
    )
    row_of = obs_index // columns + HALO
    lane_of = obs_index % LANES
    offset_of = obs_index % columns - lane_of
    shift_of = (jnp.arange(obs_index.shape[0], dtype=jnp.int32) - lane_of) % LANES
    field, predicted = kernel_call(
        functools.partial(last_kernel, blocks), "edge_last",
        [flat, (members, obs_index.shape[0])],
        [ANYWHERE] * 14 + [IN_VMEM] + [IN_SMEM] * 3, (ANYWHERE, IN_VMEM),
        scratch(columns, staged, dma((15,)), dma((blocks,))), 15,
        [low1, low0, high0, high1, *first, own_coef, halo_coef, params, row_of, offset_of, shift_of],
    )
    return field.reshape(shape), predicted


def products_kernel(total_obs, per_group, spread, everyone, own, values, variance, same, out):
    weight = 1.0 / (variance[...] * total_obs)
    innovation = (values[...] - own[...]) * weight
    predicted = everyone[...]
    anomalies = (predicted - hdot(same[...], predicted) / per_group) * spread
    right = jnp.concatenate([anomalies * weight, innovation], axis=0)
    out[...] = lax.dot_general(
        anomalies,
        right,
        (((1,), (1,)), ((), ())),
        precision=lax.Precision.HIGHEST,
        preferred_element_type=jnp.float32,
    )


def update_kernel(per_group, summands, same, own_same, rank_row, rank_col, anomalies, own, out):
    members = same.shape[0]
    total = summands[0]
    for index in range(1, summands.shape[0]):
        total = total + summands[index]
    together = same[...]
    row = lax.broadcasted_iota(jnp.int32, (members, members), 0)
    col = lax.broadcasted_iota(jnp.int32, (members, members), 1)
    system = jnp.where(row == col, 1.0, 0.0) + together * total[:, 0:members]
    right = own_same[...] * total[:, members:]
    for pivot in range(per_group):
        pick = jnp.where(rank_row[...] == pivot, together, 0.0)
        pivot_system = hdot(pick, system)
        pivot_right = hdot(pick, right)
        pivot_value = jnp.sum(pick * pivot_system, axis=1, keepdims=True)
        factor = jnp.sum(pick * system, axis=1, keepdims=True)
        is_pivot = rank_col[...] == pivot
        scale = 1.0 / pivot_value
        scaled_system, scaled_right = pivot_system * scale, pivot_right * scale
        system = jnp.where(is_pivot, scaled_system, system - factor * scaled_system)
        right = jnp.where(is_pivot, scaled_right, right - factor * scaled_right)
    change = lax.dot_general(
        right,
        anomalies[...],
        (((0,), (0,)), ((), ())),
        precision=lax.Precision.HIGHEST,
        preferred_element_type=jnp.float32,
    )
    out[...] = own[...] + change


def local(tracer, coefficients, parameters, obs_index, obs_values, obs_variance, member_group):
    local_members, rows, columns = tracer.shape
    ens_pos = lax.axis_index("ens")
    ens_count = lax.axis_size("ens")
    slab_count = lax.axis_size("slab")
    if ens_count != coefficients.shape[0] or slab_count & (slab_count - 1):
        raise ValueError("mesh shape")
    forward = [(i, i + 1) for i in range(slab_count - 1)]
    backward = [(target, source) for source, target in forward]

    own_array = lax.dynamic_slice_in_dim(coefficients, ens_pos, 1, 0)[0]
    coef_low = lax.ppermute(own_array[rows - HALO :], "slab", forward)
    coef_high = lax.ppermute(own_array[:HALO], "slab", backward)
    own = row_groups(tracer)
    coef_low, coef_high, _ = lax.optimization_barrier((coef_low, coef_high, own[0]))
    shared = jnp.concatenate([coef_low, coef_high, parameters], axis=0)
    gathered = lax.all_gather(shared, "ens", axis=0, tiled=False)

    def halos(upper, lower):
        return lax.ppermute(upper, "slab", forward), lax.ppermute(lower, "slab", backward)

    members = member_group.shape[0]
    per_group = members // GROUPS
    spread = 1.0 / math.sqrt(per_group - 1)
    same_bool = member_group[:, None] == member_group[None, :]
    same = same_bool.astype(jnp.float32)
    earlier = jnp.arange(members)[None, :] < jnp.arange(members)[:, None]
    rank = jnp.sum((same_bool & earlier).astype(jnp.int32), axis=1)
    own_same = lax.dynamic_slice_in_dim(same, ens_pos * local_members, local_members, 1)
    all_params = gathered[:, 2 * HALO :, :].reshape(members, columns)
    param_anomalies = (all_params - hdot(same, all_params) / per_group) * spread

    field, predicted = transport(
        tracer.shape, own, coefficients, gathered, parameters, obs_index, halos
    )
    everyone = lax.all_gather(predicted, "ens", axis=0, tiled=True)
    total_obs = obs_variance.shape[0] * slab_count
    products = pl.pallas_call(
        functools.partial(products_kernel, float(total_obs), per_group, spread),
        out_shape=jax.ShapeDtypeStruct((members, members + local_members), jnp.float32),
        compiler_params=pltpu.CompilerParams(vmem_limit_bytes=VMEM_LIMIT),
        name="products",
    )(everyone, predicted, obs_values, obs_variance[None, :], same)
    distance = 1
    while distance < slab_count:
        pairs = [(i, i ^ distance) for i in range(slab_count)]
        products = products + lax.ppermute(products, "slab", pairs)
        distance *= 2
    updated = pl.pallas_call(
        functools.partial(update_kernel, per_group),
        out_shape=jax.ShapeDtypeStruct(parameters.shape, jnp.float32),
        compiler_params=pltpu.CompilerParams(vmem_limit_bytes=VMEM_LIMIT),
        name="update",
    )(products[None], same, own_same, rank[None, :], rank[:, None], param_anomalies, parameters)
    return (field, updated)


def solution(mesh):
    in_specs = (
        P("ens", "slab", None),
        P(None, "slab", None),
        P("ens", None),
        P("slab"),
        P("ens", "slab"),
        P("slab"),
        P(),
    )
    out_specs = (P("ens", "slab", None), P("ens", None))
    return jax.shard_map(local, mesh=mesh, in_specs=in_specs, out_specs=out_specs, check_vma=False)
```

```python
import functools
import math

import jax
import jax.numpy as jnp
from jax import lax
from jax.experimental import pallas as pl
from jax.experimental.pallas import tpu as pltpu
from jax.sharding import PartitionSpec as P

STEPS = 4
GROUPS = 8
HALO = 2 * STEPS
LANES = 128
SUBLANES = 8
ROWS = 16
GROUP = 4
LAG = 3
WIDE = 8
TOGETHER = 2
VMEM_LIMIT = 30 * 1024 * 1024
TALL_LIMIT = 60 * 1024 * 1024
COST_BYTES = 200000
ANYWHERE = pl.BlockSpec(memory_space=pltpu.HBM)
IN_VMEM = pl.BlockSpec(memory_space=pltpu.VMEM)
IN_SMEM = pl.BlockSpec(memory_space=pltpu.SMEM)


def hdot(left, right):
    return jnp.dot(left, right, precision=lax.Precision.HIGHEST, preferred_element_type=jnp.float32)


def limited(left, right):
    return jnp.minimum(jnp.maximum(left, jnp.minimum(right, 0.0)), jnp.maximum(right, 0.0))


def block_at(block):
    return pl.ds(pl.multiple_of(block * LANES, LANES), LANES)


def wide(row):
    return jnp.broadcast_to(row, (SUBLANES, LANES))


def columns_pass(source, first_row, count, target, target_row, coef, params, blocks):
    lane = lax.broadcasted_iota(jnp.int32, (SUBLANES, LANES), 1)
    first, last = lane == 0, lane == LANES - 1
    places = [[coef_row(array, first_row + i) for array in range(4)] for i in range(count)]
    c, c_rolled, d, d_rolled, slope, twice, left, right, laplace = ({} for _ in range(9))
    for tick in range(blocks + 2 * LAG + 4):
        for i in range(count):
            row = first_row + i
            b = tick - 1
            if b <= blocks:
                c[i, b] = source[row, :, block_at(b % blocks)]
                c_rolled[i, b] = pltpu.roll(c[i, b], LANES - 1, 1)
            b = tick - 2
            if -1 <= b <= blocks:
                c_next = c_rolled[i, b]
                if b < blocks:
                    c_next = jnp.where(last, c_rolled[i, b + 1], c_next)
                d[i, b] = c_next - c[i, b]
                d_rolled[i, b] = pltpu.roll(d[i, b], 1, 1)
            b = tick - 2 - LAG
            if -1 <= b <= blocks:
                d_back = d_rolled[i, b]
                if b >= 0:
                    d_back = jnp.where(first, d_rolled[i, b - 1], d_back)
                slope[i, b] = limited(d_back, d[i, b])
                twice[i, b] = d[i, b] + d[i, b]
                laplace[i, b] = d[i, b] - d_back
                left[i, b] = pltpu.roll(twice[i, b] - slope[i, b], 1, 1)
                right[i, b] = pltpu.roll(slope[i, b], LANES - 1, 1)
            b = tick - 3 - 2 * LAG
            if 0 <= b < blocks:
                at = block_at(b)
                speed = wide(coef[places[i][1], :, at])
                forward = jnp.where(first, left[i, b - 1], left[i, b])
                backward = twice[i, b] - jnp.where(last, right[i, b + 1], right[i, b])
                change = jnp.where(speed > 0.0, forward, backward) + slope[i, b]
                value = c[i, b] - (0.5 * speed) * change
                value = value + wide(coef[places[i][2], :, at]) * laplace[i, b]
                value = value + params[:, at] * wide(coef[places[i][3], :, at])
                target[target_row + i, :, at] = value


def rows_pass(source, row, places, partial, target, coef, block, blocks):
    at = block_at(block)
    c = [source[row - 2 + i, :, at] for i in range(GROUP + 4)]
    d = [c[i + 1] - c[i] for i in range(GROUP + 3)]
    slope = [None] + [limited(d[i - 1], d[i]) for i in range(1, GROUP + 3)]
    twice = [None] + [d[i] + d[i] for i in range(1, GROUP + 2)]
    for i in range(2, GROUP + 2):
        here = row - 2 + i
        speed = wide(coef[places[i - 2][0], :, at])
        forward = twice[i - 1] - slope[i - 1]
        backward = twice[i] - slope[i + 1]
        change = wide(coef[places[i - 2][1], :, at]) * (d[i] - d[i - 1])
        change = change - (0.5 * speed) * (jnp.where(speed > 0.0, forward, backward) + slope[i])
        value = partial[i - 2, :, at] + change
        if target.shape[1:] == value.shape:
            target[here * blocks + block] = value
        else:
            target[here, :, at] = value


def advance_group(source, target, row, partial, coef, params, blocks):
    @pl.loop(0, GROUP // TOGETHER)
    def _(i):
        columns_pass(
            source, row + i * TOGETHER, TOGETHER, partial, i * TOGETHER, coef, params, blocks
        )

    places = [[coef_row(array, row + i) for array in (0, 2)] for i in range(GROUP)]

    @pl.loop(0, blocks // WIDE)
    def _(wide_block):
        for i in range(WIDE):
            rows_pass(source, row, places, partial, target, coef, wide_block * WIDE + i, blocks)


class Copies:
    def __init__(self, sems):
        self.sems, self.used = sems, 0

    def start(self, source, target):
        copy = pltpu.make_async_copy(source, target, self.sems.at[self.used])
        self.used += 1
        assert self.used <= self.sems.shape[0]
        copy.start()
        return copy


def place(row):
    return pl.ds(row + HALO, GROUP)


def region(levels, level, row, blocks):
    if level == STEPS:
        return levels[level].at[pl.ds((row + HALO) * blocks, GROUP * blocks)]
    return levels[level].at[place(row)]


def fill_rows(blocks, first_rows, tracer, outs, staged, sems):
    def copy(block):
        return pltpu.make_async_copy(tracer.at[:, block_at(block)], staged.at[block], sems.at[block])

    @pl.loop(0, blocks)
    def _(block):
        copy(block).start()

    @pl.loop(0, blocks)
    def _(block):
        copy(block).wait()
        for out, first_row in zip(outs, first_rows):
            for row in range(GROUP):
                out[row, :, block_at(block)] = staged[
                    block, pl.ds(first_row + row, SUBLANES, stride=ROWS), :
                ]


def outer_rows_kernel(blocks, tracer, own_coef, place_of, up, down, staged, sems, coef_sems):
    copies = Copies(coef_sems)
    upper = lax.rem(place_of[0], 2) * 2
    waits = []
    for array in range(4):
        at = pl.ds(2 * array, 2)
        waits.append(copies.start(own_coef.at[array, pl.ds(ROWS - 2, 2)], up.at[GROUP, at]))
        waits.append(copies.start(own_coef.at[array, pl.ds(0, 2)], down.at[GROUP, at]))
    for array in range(2):
        at = pl.ds(4 * array, 4)
        source = own_coef.at[upper + array]
        waits.append(copies.start(source.at[pl.ds(ROWS - 6, 4)], up.at[GROUP + 1, at]))
        waits.append(copies.start(source.at[pl.ds(2, 4)], down.at[GROUP + 1, at]))
    fill_rows(blocks, (0, ROWS - GROUP), tracer, (down, up), staged, sems)
    for copy in waits:
        copy.wait()


def inner_rows_kernel(blocks, tracer, outer, low, high, staged, sems):
    fill_rows(blocks, (GROUP, ROWS - 2 * GROUP), tracer, (low, high), staged, sems)


def interior_kernel(blocks, own0, own1, own2, own3, own_coef, params, *rest):
    outs, (*levels, partial, coef, sems) = rest[:5], rest[5:]
    copies = Copies(sems)
    waits = [
        copies.start(own.at[0:GROUP], levels[0].at[place(GROUP * i)])
        for i, own in enumerate((own0, own1, own2, own3))
    ]
    waits += [
        copies.start(own_coef.at[array], coef.at[pl.ds(array * ROWS, ROWS), 0]) for array in range(4)
    ]
    for copy in waits:
        copy.wait()
    for level, start, count in ((0, 2, 3), (1, 4, 2), (2, 6, 1)):
        @pl.loop(0, count)
        def _(i):
            row = start + HALO + GROUP * i
            advance_group(levels[level], levels[level + 1], row, partial, coef, params, blocks)

    waits = [
        copies.start(levels[level].at[place(row)], out)
        for out, (level, row) in zip(outs, ((1, 2), (1, 10), (2, 4), (2, 8), (3, 6)))
    ]
    for copy in waits:
        copy.wait()


def edge_steps(outer, blocks, waits, levels, partial, coef, params, ready):
    for level in range(STEPS):
        for copy in waits[level]:
            copy.wait()
        low, high = 2 * level - outer, ROWS + outer - GROUP - 2 * level

        @pl.loop(0, 2)
        def _(side):
            row = low + HALO + side * (high - low)
            advance_group(levels[level], levels[level + 1], row, partial, coef, params, blocks)

        ready(level, low, high)


def coef_row(array, row):
    own = array * ROWS + row - HALO
    near_low = 4 * ROWS + 2 * array + row - (HALO - 2)
    near_high = 4 * ROWS + 8 + 2 * array + row - (HALO + ROWS)
    far_low = 4 * ROWS + 16 + 4 * array + row - (HALO - 6)
    far_high = 4 * ROWS + 32 + 4 * array + row - (HALO + ROWS + 2)
    low = jnp.where(row < HALO - 2, far_low, near_low)
    high = jnp.where(row < HALO + ROWS + 2, near_high, far_high)
    return jnp.where(row < HALO, low, jnp.where(row < HALO + ROWS, own, high))


def load_coef(copies, own_coef, low, high, coef):
    waits = [
        copies.start(own_coef.at[array], coef.at[pl.ds(array * ROWS, ROWS), 0]) for array in range(4)
    ]
    for side, source in enumerate((low, high)):
        waits.append(copies.start(source.at[GROUP], coef.at[pl.ds(4 * ROWS + 8 * side, 8), 0]))
    return waits


def load_outer_coef(copies, mine, theirs, place_of, coef):
    waits = []
    own_half = lax.rem(place_of[0], 2)
    for source, half in ((mine, own_half), (theirs, 1 - own_half)):
        for side in range(2):
            first = 4 * ROWS + 16 + 16 * side + 8 * half
            waits.append(copies.start(source.at[side], coef.at[pl.ds(first, 8), 0]))
    return waits


def middle_kernel(blocks, *refs):
    sources, refs = refs[:9], refs[9:]
    own_coef, params = refs[:2]
    outs, (*levels, partial, coef, sems) = refs[2:10], refs[10:]
    copies = Copies(sems)
    places = ((0, -4), (0, 0), (0, 12), (0, 16), (1, 2), (1, 10), (2, 4), (2, 8), (3, 6))
    waits = [[] for _ in range(STEPS)]
    for source, (level, row) in zip(sources, places):
        count = GROUP * blocks if level == STEPS else GROUP
        waits[level].append(
            copies.start(source.at[0:count], region(levels, level, row, blocks))
        )
    waits[0] += load_coef(copies, own_coef, sources[0], sources[3], coef)
    sends = []

    def ready(level, low, high):
        for row, out in ((low, outs[2 * level]), (high, outs[2 * level + 1])):
            sends.append(copies.start(region(levels, level + 1, row, blocks), out))

    edge_steps(2, blocks, waits, levels, partial, coef, params, ready)
    for copy in sends:
        copy.wait()


def last_kernel(blocks, *refs):
    sources, refs = refs[:12], refs[12:]
    own_coef, mine, theirs, params, place_of, cell_of, shift_of = refs[:7]
    out, predicted, *levels, partial, coef, staged, sems, out_sems = refs[7:]
    copies = Copies(sems)
    places = (
        (0, -8), (0, -4), (0, 16), (0, 20),
        (1, -2), (1, 14), (2, 0), (2, 12), (3, 2), (3, 10), (4, 4), (4, 8),
    )
    waits = [[] for _ in range(STEPS + 1)]
    for source, (level, row) in zip(sources, places):
        count = GROUP * blocks if level == STEPS else GROUP
        waits[level].append(
            copies.start(source.at[0:count], region(levels, level, row, blocks))
        )
    waits[0] += load_coef(copies, own_coef, sources[1], sources[2], coef)
    waits[0] += load_outer_coef(copies, mine, theirs, place_of, coef)
    edge_steps(6, blocks, waits, levels, partial, coef, params, lambda *_: None)
    for copy in waits[STEPS]:
        copy.wait()

    def out_copy(block):
        return pltpu.make_async_copy(staged.at[block], out.at[:, block_at(block)], out_sems.at[block])

    @pl.loop(0, blocks)
    def _(block):
        for row in range(ROWS):
            staged[block, pl.ds(row, SUBLANES, stride=ROWS), :] = levels[STEPS][
                (HALO + row) * blocks + block
            ]
        out_copy(block).start()

    lane = lax.broadcasted_iota(jnp.int32, (SUBLANES, LANES), 1)

    @pl.loop(0, predicted.shape[1] // LANES)
    def _(block):
        base = block * LANES
        found = jnp.zeros((SUBLANES, LANES), jnp.float32)
        for i in range(LANES):
            value = levels[STEPS][cell_of[base + i]]
            found = jnp.where(lane == i, pltpu.roll(value, shift_of[base + i], 1), found)
        predicted[:, block_at(block)] = found

    @pl.loop(0, blocks)
    def _(block):
        out_copy(block).wait()


def scratch(columns, *more):
    return (
        [pltpu.VMEM((ROWS + 2 * HALO, SUBLANES, columns), jnp.float32)] * STEPS
        + [
            pltpu.VMEM(
                ((ROWS + 2 * HALO) * columns // LANES, SUBLANES, LANES), jnp.float32
            ),
            pltpu.VMEM((GROUP, SUBLANES, columns), jnp.float32),
            pltpu.VMEM((4 * ROWS + 48, 1, columns), jnp.float32),
        ]
        + list(more)
    )


def kernel_call(body, name, outs, specs, out_specs, scratches, cost, operands, limit=VMEM_LIMIT):
    return pl.pallas_call(
        body,
        out_shape=tuple(jax.ShapeDtypeStruct(shape, jnp.float32) for shape in outs),
        in_specs=specs,
        out_specs=out_specs,
        scratch_shapes=scratches,
        compiler_params=pltpu.CompilerParams(vmem_limit_bytes=limit),
        cost_estimate=pl.CostEstimate(flops=0, bytes_accessed=cost * COST_BYTES, transcendentals=0),
        name=name,
    )(*operands)


def row_groups(tracer, coefficients, place_of):
    members, rows, columns = tracer.shape
    if members != SUBLANES or rows != ROWS:
        raise ValueError("block shape")
    blocks = columns // LANES
    flat = tracer.reshape(members * rows, columns)
    dma = pltpu.SemaphoreType.DMA
    scratches = [pltpu.VMEM((blocks, members * rows, LANES), jnp.float32), dma((blocks,))]
    up, down = kernel_call(
        functools.partial(outer_rows_kernel, blocks), "outer_rows",
        [(GROUP + 2, members, columns)] * 2, [ANYWHERE, ANYWHERE, IN_SMEM], (IN_VMEM,) * 2,
        scratches + [dma((12,))], 3, [flat, coefficients, place_of], TALL_LIMIT,
    )
    low, high = kernel_call(
        functools.partial(inner_rows_kernel, blocks), "inner_rows",
        [(GROUP, members, columns)] * 2, [ANYWHERE, ANYWHERE], (IN_VMEM,) * 2,
        scratches, 3, [flat, up], TALL_LIMIT,
    )
    return down, low, high, up


def transport(shape, own, low0, high0, own_coef, params, place_of, obs_index, halos, other_core):
    members, rows, columns = shape
    blocks = columns // LANES
    group = (GROUP, members, columns)
    flat = (members * rows, columns)
    cells = (GROUP * blocks, members, LANES)
    dma = pltpu.SemaphoreType.DMA
    staged = pltpu.VMEM((blocks, members * rows, LANES), jnp.float32)
    inner = kernel_call(
        functools.partial(interior_kernel, blocks), "interior",
        [group] * 5, [ANYWHERE] * 5 + [IN_VMEM], (ANYWHERE,) * 5,
        scratch(columns, dma((16,))), 8, [*own, own_coef, params],
    )
    upper, lower, low0, high0, *_ = lax.optimization_barrier(
        (own[2], own[1], low0, high0, inner[0])
    )
    low1, high1 = halos(upper, lower)
    first = kernel_call(
        functools.partial(middle_kernel, blocks), "edge_first",
        [group] * 6 + [cells] * 2, [ANYWHERE] * 10 + [IN_VMEM], (ANYWHERE,) * 8,
        scratch(columns, dma((26,))), 10,
        [low0, own[0], own[3], high0, *inner, own_coef, params],
    )
    mine, _ = lax.optimization_barrier((jnp.stack([low0[GROUP + 1], high0[GROUP + 1]]), first[0]))
    theirs = other_core(mine)
    cell_of = obs_index // LANES + HALO * blocks
    lane_of = obs_index % LANES
    shift_of = (jnp.arange(obs_index.shape[0], dtype=jnp.int32) - lane_of) % LANES
    field, predicted = kernel_call(
        functools.partial(last_kernel, blocks), "edge_last",
        [flat, (members, obs_index.shape[0])],
        [ANYWHERE] * 15 + [IN_VMEM] + [IN_SMEM] * 3, (ANYWHERE, IN_VMEM),
        scratch(columns, staged, dma((29,)), dma((blocks,))), 15,
        [low1, low0, high0, high1, *first, own_coef, mine, theirs, params, place_of, cell_of, shift_of],
    )
    return field.reshape(shape), predicted


def products_kernel(total_obs, per_group, spread, everyone, own, values, variance, same, out):
    weight = 1.0 / (variance[...] * total_obs)
    innovation = (values[...] - own[...]) * weight
    predicted = everyone[...]
    anomalies = (predicted - hdot(same[...], predicted) / per_group) * spread
    right = jnp.concatenate([anomalies * weight, innovation], axis=0)
    out[...] = lax.dot_general(
        anomalies,
        right,
        (((1,), (1,)), ((), ())),
        precision=lax.Precision.HIGHEST,
        preferred_element_type=jnp.float32,
    )


def update_kernel(per_group, summands, same, own_same, rank_row, rank_col, anomalies, own, out):
    members = same.shape[0]
    total = summands[0]
    for index in range(1, summands.shape[0]):
        total = total + summands[index]
    together = same[...]
    row = lax.broadcasted_iota(jnp.int32, (members, members), 0)
    col = lax.broadcasted_iota(jnp.int32, (members, members), 1)
    system = jnp.where(row == col, 1.0, 0.0) + together * total[:, 0:members]
    right = own_same[...] * total[:, members:]
    for pivot in range(per_group):
        pick = jnp.where(rank_row[...] == pivot, together, 0.0)
        pivot_system = hdot(pick, system)
        pivot_right = hdot(pick, right)
        pivot_value = jnp.sum(pick * pivot_system, axis=1, keepdims=True)
        factor = jnp.sum(pick * system, axis=1, keepdims=True)
        is_pivot = rank_col[...] == pivot
        scale = 1.0 / pivot_value
        scaled_system, scaled_right = pivot_system * scale, pivot_right * scale
        system = jnp.where(is_pivot, scaled_system, system - factor * scaled_system)
        right = jnp.where(is_pivot, scaled_right, right - factor * scaled_right)
    change = lax.dot_general(
        right,
        anomalies[...],
        (((0,), (0,)), ((), ())),
        precision=lax.Precision.HIGHEST,
        preferred_element_type=jnp.float32,
    )
    out[...] = own[...] + change


def local(tracer, coefficients, parameters, obs_index, obs_values, obs_variance, member_group):
    local_members, rows, columns = tracer.shape
    ens_pos = lax.axis_index("ens")
    ens_count = lax.axis_size("ens")
    slab_count = lax.axis_size("slab")
    if ens_count != 4 or coefficients.shape[0] != 4 or slab_count & (slab_count - 1):
        raise ValueError("mesh shape")
    forward = [(i, i + 1) for i in range(slab_count - 1)]
    backward = [(target, source) for source, target in forward]

    def halos(upper, lower):
        return lax.ppermute(upper, "slab", forward), lax.ppermute(lower, "slab", backward)

    place_of = jnp.reshape(ens_pos, (1,))
    own = row_groups(tracer, coefficients, place_of)
    low0, high0 = halos(own[3], own[0])

    later, _ = lax.optimization_barrier((parameters, own[1]))
    pair = jnp.stack([later, lax.ppermute(later, "ens", [(i, i ^ 1) for i in range(ens_count)])])
    other = lax.ppermute(pair, "ens", [(i, i ^ 2) for i in range(ens_count)])
    shared = jnp.concatenate([pair, other], axis=0)

    def other_core(mine):
        return lax.ppermute(mine, "ens", [(i, i ^ 1) for i in range(ens_count)])

    members = member_group.shape[0]
    per_group = members // GROUPS
    spread = 1.0 / math.sqrt(per_group - 1)
    same_bool = member_group[:, None] == member_group[None, :]
    same = same_bool.astype(jnp.float32)
    earlier = jnp.arange(members)[None, :] < jnp.arange(members)[:, None]
    rank = jnp.sum((same_bool & earlier).astype(jnp.int32), axis=1)
    own_same = lax.dynamic_slice_in_dim(same, ens_pos * local_members, local_members, 1)
    field, predicted = transport(
        tracer.shape, own, low0, high0,
        coefficients, parameters, place_of, obs_index, halos, other_core,
    )
    all_params = jnp.concatenate(
        [lax.dynamic_index_in_dim(shared, ens_pos ^ i, 0, False) for i in range(ens_count)], axis=0
    )
    param_anomalies = (all_params - hdot(same, all_params) / per_group) * spread

    everyone = lax.all_gather(predicted, "ens", axis=0, tiled=True)
    total_obs = obs_variance.shape[0] * slab_count
    products = pl.pallas_call(
        functools.partial(products_kernel, float(total_obs), per_group, spread),
        out_shape=jax.ShapeDtypeStruct((members, members + local_members), jnp.float32),
        compiler_params=pltpu.CompilerParams(vmem_limit_bytes=VMEM_LIMIT),
        name="products",
    )(everyone, predicted, obs_values, obs_variance[None, :], same)
    distance = 1
    while distance < slab_count:
        pairs = [(i, i ^ distance) for i in range(slab_count)]
        products = products + lax.ppermute(products, "slab", pairs)
        distance *= 2
    updated = pl.pallas_call(
        functools.partial(update_kernel, per_group),
        out_shape=jax.ShapeDtypeStruct(parameters.shape, jnp.float32),
        compiler_params=pltpu.CompilerParams(vmem_limit_bytes=VMEM_LIMIT),
        name="update",
    )(products[None], same, own_same, rank[None, :], rank[:, None], param_anomalies, parameters)
    return (field, updated)


def solution(mesh):
    in_specs = (
        P("ens", "slab", None),
        P(None, "slab", None),
        P("ens", None),
        P("slab"),
        P("ens", "slab"),
        P("slab"),
        P(),
    )
    out_specs = (P("ens", "slab", None), P("ens", None))
    return jax.shard_map(local, mesh=mesh, in_specs=in_specs, out_specs=out_specs, check_vma=False)
```

```python
import functools
import math

import jax
import jax.numpy as jnp
from jax import lax
from jax.experimental import pallas as pl
from jax.experimental.pallas import tpu as pltpu
from jax.sharding import PartitionSpec as P

STEPS = 4
GROUPS = 8
HALO = 2 * STEPS
LANES = 128
SUBLANES = 8
ROWS = 16
GROUP = 4
LAG = 3
WIDE = 8
TOGETHER = 2
VMEM_LIMIT = 16 * 1024 * 1024
TALL_LIMIT = 58 * 1024 * 1024
COST_BYTES = 200000
ANYWHERE = pl.BlockSpec(memory_space=pltpu.HBM)
IN_VMEM = pl.BlockSpec(memory_space=pltpu.VMEM)
IN_SMEM = pl.BlockSpec(memory_space=pltpu.SMEM)


def hdot(left, right):
    return jnp.dot(left, right, precision=lax.Precision.HIGHEST, preferred_element_type=jnp.float32)


def limited(left, right):
    return jnp.minimum(jnp.maximum(left, jnp.minimum(right, 0.0)), jnp.maximum(right, 0.0))


def block_at(block):
    return pl.ds(pl.multiple_of(block * LANES, LANES), LANES)


def wide(row):
    return jnp.broadcast_to(row, (SUBLANES, LANES))


def columns_pass(source, first_row, count, target, target_row, coef, params, blocks):
    lane = lax.broadcasted_iota(jnp.int32, (SUBLANES, LANES), 1)
    first, last = lane == 0, lane == LANES - 1
    places = [[coef_row(array, first_row + i) for array in range(4)] for i in range(count)]
    c, c_rolled, d, d_rolled, slope, twice, left, right, laplace = ({} for _ in range(9))
    for tick in range(blocks + 2 * LAG + 4):
        for i in range(count):
            row = first_row + i
            b = tick - 1
            if b <= blocks:
                c[i, b] = source[row, :, block_at(b % blocks)]
                c_rolled[i, b] = pltpu.roll(c[i, b], LANES - 1, 1)
            b = tick - 2
            if -1 <= b <= blocks:
                c_next = c_rolled[i, b]
                if b < blocks:
                    c_next = jnp.where(last, c_rolled[i, b + 1], c_next)
                d[i, b] = c_next - c[i, b]
                d_rolled[i, b] = pltpu.roll(d[i, b], 1, 1)
            b = tick - 2 - LAG
            if -1 <= b <= blocks:
                d_back = d_rolled[i, b]
                if b >= 0:
                    d_back = jnp.where(first, d_rolled[i, b - 1], d_back)
                slope[i, b] = limited(d_back, d[i, b])
                twice[i, b] = d[i, b] + d[i, b]
                laplace[i, b] = d[i, b] - d_back
                left[i, b] = pltpu.roll(twice[i, b] - slope[i, b], 1, 1)
                right[i, b] = pltpu.roll(slope[i, b], LANES - 1, 1)
            b = tick - 3 - 2 * LAG
            if 0 <= b < blocks:
                at = block_at(b)
                speed = wide(coef[places[i][1], :, at])
                forward = jnp.where(first, left[i, b - 1], left[i, b])
                backward = twice[i, b] - jnp.where(last, right[i, b + 1], right[i, b])
                change = jnp.where(speed > 0.0, forward, backward) + slope[i, b]
                value = c[i, b] - (0.5 * speed) * change
                value = value + wide(coef[places[i][2], :, at]) * laplace[i, b]
                value = value + params[:, at] * wide(coef[places[i][3], :, at])
                target[target_row + i, :, at] = value


def rows_pass(source, row, places, partial, target, coef, block, blocks):
    at = block_at(block)
    c = [source[row - 2 + i, :, at] for i in range(GROUP + 4)]
    d = [c[i + 1] - c[i] for i in range(GROUP + 3)]
    slope = [None] + [limited(d[i - 1], d[i]) for i in range(1, GROUP + 3)]
    twice = [None] + [d[i] + d[i] for i in range(1, GROUP + 2)]
    for i in range(2, GROUP + 2):
        here = row - 2 + i
        speed = wide(coef[places[i - 2][0], :, at])
        forward = twice[i - 1] - slope[i - 1]
        backward = twice[i] - slope[i + 1]
        change = wide(coef[places[i - 2][1], :, at]) * (d[i] - d[i - 1])
        change = change - (0.5 * speed) * (jnp.where(speed > 0.0, forward, backward) + slope[i])
        value = partial[i - 2, :, at] + change
        if target.shape[1:] == value.shape:
            target[here * blocks + block] = value
        else:
            target[here, :, at] = value


def advance_group(source, target, row, partial, coef, params, blocks):
    @pl.loop(0, GROUP // TOGETHER)
    def _(i):
        columns_pass(
            source, row + i * TOGETHER, TOGETHER, partial, i * TOGETHER, coef, params, blocks
        )

    places = [[coef_row(array, row + i) for array in (0, 2)] for i in range(GROUP)]

    @pl.loop(0, blocks // WIDE)
    def _(wide_block):
        for i in range(WIDE):
            rows_pass(source, row, places, partial, target, coef, wide_block * WIDE + i, blocks)


class Copies:
    def __init__(self, sems):
        self.sems, self.used = sems, 0

    def start(self, source, target):
        copy = pltpu.make_async_copy(source, target, self.sems.at[self.used])
        self.used += 1
        assert self.used <= self.sems.shape[0]
        copy.start()
        return copy


def place(row):
    return pl.ds(row + HALO, GROUP)


def region(levels, level, row, blocks):
    if level == STEPS:
        return levels[level].at[pl.ds((row + HALO) * blocks, GROUP * blocks)]
    return levels[level].at[place(row)]


def fill_rows(blocks, first_rows, tracer, outs, staged, sems):
    def copy(block):
        return pltpu.make_async_copy(tracer.at[:, block_at(block)], staged.at[block], sems.at[block])

    @pl.loop(0, blocks)
    def _(block):
        copy(block).start()

    @pl.loop(0, blocks)
    def _(block):
        copy(block).wait()
        for out, first_row in zip(outs, first_rows):
            for row in range(GROUP):
                out[row, :, block_at(block)] = staged[
                    block, pl.ds(first_row + row, SUBLANES, stride=ROWS), :
                ]


def outer_rows_kernel(
    blocks, tracer, own_coef, place_of, up, down, up_coef, down_coef, staged, sems, coef_sems
):
    copies = Copies(coef_sems)
    source = own_coef.at[place_of[0]]
    waits = [
        copies.start(source.at[pl.ds(ROWS - HALO, HALO)], up_coef),
        copies.start(source.at[pl.ds(0, HALO)], down_coef),
    ]
    fill_rows(blocks, (0, ROWS - GROUP), tracer, (down, up), staged, sems)
    for copy in waits:
        copy.wait()


def inner_rows_kernel(blocks, tracer, outer, low, high, staged, sems):
    fill_rows(blocks, (GROUP, ROWS - 2 * GROUP), tracer, (low, high), staged, sems)


def interior_kernel(blocks, own0, own1, own2, own3, own_coef, params, *rest):
    outs, (*levels, partial, coef, sems) = rest[:5], rest[5:]
    copies = Copies(sems)
    waits = [
        copies.start(own.at[0:GROUP], levels[0].at[place(GROUP * i)])
        for i, own in enumerate((own0, own1, own2, own3))
    ]
    waits += [
        copies.start(own_coef.at[array], coef.at[pl.ds(array * ROWS, ROWS), 0]) for array in range(4)
    ]
    for copy in waits:
        copy.wait()
    for level, start, count in ((0, 2, 3), (1, 4, 2), (2, 6, 1)):
        @pl.loop(0, count)
        def _(i):
            row = start + HALO + GROUP * i
            advance_group(levels[level], levels[level + 1], row, partial, coef, params, blocks)

    waits = [
        copies.start(levels[level].at[place(row)], out)
        for out, (level, row) in zip(outs, ((1, 2), (1, 10), (2, 4), (2, 8), (3, 6)))
    ]
    for copy in waits:
        copy.wait()


def edge_steps(outer, blocks, waits, levels, partial, coef, params, ready):
    for level in range(STEPS):
        for copy in waits[level]:
            copy.wait()
        low, high = 2 * level - outer, ROWS + outer - GROUP - 2 * level

        @pl.loop(0, 2)
        def _(side):
            row = low + HALO + side * (high - low)
            advance_group(levels[level], levels[level + 1], row, partial, coef, params, blocks)

        ready(level, low, high)


def coef_row(array, row):
    own = array * ROWS + row - HALO
    low = 4 * ROWS + 2 * HALO * array + row
    high = 4 * ROWS + 2 * HALO * array + row - ROWS
    return jnp.where(row < HALO, low, jnp.where(row < HALO + ROWS, own, high))


def load_coef(copies, own_coef, pair, other, place_of, coef):
    waits = [
        copies.start(own_coef.at[array], coef.at[pl.ds(array * ROWS, ROWS), 0]) for array in range(4)
    ]
    for number, source in enumerate((pair.at[0], pair.at[1], other.at[0], other.at[1])):
        array = jnp.bitwise_xor(place_of[0], number)
        for side in range(2):
            first = 4 * ROWS + 2 * HALO * array + HALO * side
            waits.append(copies.start(source.at[side], coef.at[pl.ds(first, HALO), 0]))
    return waits


def middle_kernel(blocks, *refs):
    sources, refs = refs[:9], refs[9:]
    own_coef, pair, other, params, place_of = refs[:5]
    outs, (*levels, partial, coef, sems) = refs[5:13], refs[13:]
    copies = Copies(sems)
    places = ((0, -4), (0, 0), (0, 12), (0, 16), (1, 2), (1, 10), (2, 4), (2, 8), (3, 6))
    waits = [[] for _ in range(STEPS)]
    for source, (level, row) in zip(sources, places):
        count = GROUP * blocks if level == STEPS else GROUP
        waits[level].append(
            copies.start(source.at[0:count], region(levels, level, row, blocks))
        )
    waits[0] += load_coef(copies, own_coef, pair, other, place_of, coef)
    sends = []

    def ready(level, low, high):
        for row, out in ((low, outs[2 * level]), (high, outs[2 * level + 1])):
            sends.append(copies.start(region(levels, level + 1, row, blocks), out))

    edge_steps(2, blocks, waits, levels, partial, coef, params, ready)
    for copy in sends:
        copy.wait()


def last_kernel(blocks, *refs):
    sources, refs = refs[:12], refs[12:]
    own_coef, pair, other, params, place_of, cell_of, shift_of = refs[:7]
    out, predicted, *levels, partial, coef, staged, sems, out_sems = refs[7:]
    copies = Copies(sems)
    places = (
        (0, -8), (0, -4), (0, 16), (0, 20),
        (1, -2), (1, 14), (2, 0), (2, 12), (3, 2), (3, 10), (4, 4), (4, 8),
    )
    waits = [[] for _ in range(STEPS + 1)]
    for source, (level, row) in zip(sources, places):
        count = GROUP * blocks if level == STEPS else GROUP
        waits[level].append(
            copies.start(source.at[0:count], region(levels, level, row, blocks))
        )
    waits[0] += load_coef(copies, own_coef, pair, other, place_of, coef)
    edge_steps(6, blocks, waits, levels, partial, coef, params, lambda *_: None)
    for copy in waits[STEPS]:
        copy.wait()

    def out_copy(block):
        return pltpu.make_async_copy(staged.at[block], out.at[:, block_at(block)], out_sems.at[block])

    @pl.loop(0, blocks)
    def _(block):
        for row in range(ROWS):
            staged[block, pl.ds(row, SUBLANES, stride=ROWS), :] = levels[STEPS][
                (HALO + row) * blocks + block
            ]
        out_copy(block).start()

    lane = lax.broadcasted_iota(jnp.int32, (SUBLANES, LANES), 1)

    @pl.loop(0, predicted.shape[1] // LANES)
    def _(block):
        base = block * LANES
        found = jnp.zeros((SUBLANES, LANES), jnp.float32)
        for i in range(LANES):
            value = levels[STEPS][cell_of[base + i]]
            found = jnp.where(lane == i, pltpu.roll(value, shift_of[base + i], 1), found)
        predicted[:, block_at(block)] = found

    @pl.loop(0, blocks)
    def _(block):
        out_copy(block).wait()


def scratch(columns, *more):
    return (
        [pltpu.VMEM((ROWS + 2 * HALO, SUBLANES, columns), jnp.float32)] * STEPS
        + [
            pltpu.VMEM(
                ((ROWS + 2 * HALO) * columns // LANES, SUBLANES, LANES), jnp.float32
            ),
            pltpu.VMEM((GROUP, SUBLANES, columns), jnp.float32),
            pltpu.VMEM((4 * (ROWS + 2 * HALO), 1, columns), jnp.float32),
        ]
        + list(more)
    )


def kernel_call(body, name, outs, specs, out_specs, scratches, cost, operands):
    return pl.pallas_call(
        body,
        out_shape=tuple(jax.ShapeDtypeStruct(shape, jnp.float32) for shape in outs),
        in_specs=specs,
        out_specs=out_specs,
        scratch_shapes=scratches,
        compiler_params=pltpu.CompilerParams(vmem_limit_bytes=TALL_LIMIT),
        cost_estimate=pl.CostEstimate(flops=0, bytes_accessed=cost * COST_BYTES, transcendentals=0),
        name=name,
    )(*operands)


def row_groups(tracer, coefficients, place_of):
    members, rows, columns = tracer.shape
    if members != SUBLANES or rows != ROWS:
        raise ValueError("block shape")
    blocks = columns // LANES
    flat = tracer.reshape(members * rows, columns)
    dma = pltpu.SemaphoreType.DMA
    scratches = [pltpu.VMEM((blocks, members * rows, LANES), jnp.float32), dma((blocks,))]
    group, edge = (GROUP, members, columns), (HALO, columns)
    up, down, up_coef, down_coef = kernel_call(
        functools.partial(outer_rows_kernel, blocks), "outer_rows",
        [group, group, edge, edge], [ANYWHERE, ANYWHERE, IN_SMEM],
        (IN_VMEM, IN_VMEM, ANYWHERE, ANYWHERE),
        scratches + [dma((2,))], 3, [flat, coefficients, place_of],
    )
    low, high = kernel_call(
        functools.partial(inner_rows_kernel, blocks), "inner_rows",
        [group] * 2, [ANYWHERE, ANYWHERE], (IN_VMEM,) * 2,
        scratches, 3, [flat, up],
    )
    return (down, low, high, up), (up_coef, down_coef)


def transport(shape, own, low0, high0, own_coef, pair, other, params, place_of, obs_index, halos):
    members, rows, columns = shape
    blocks = columns // LANES
    group = (GROUP, members, columns)
    flat = (members * rows, columns)
    cells = (GROUP * blocks, members, LANES)
    dma = pltpu.SemaphoreType.DMA
    staged = pltpu.VMEM((blocks, members * rows, LANES), jnp.float32)
    inner = kernel_call(
        functools.partial(interior_kernel, blocks), "interior",
        [group] * 5, [ANYWHERE] * 5 + [IN_VMEM], (ANYWHERE,) * 5,
        scratch(columns, dma((16,))), 8, [*own, own_coef, params],
    )
    upper, lower, low0, high0, *_ = lax.optimization_barrier(
        (own[2], own[1], low0, high0, inner[0])
    )
    low1, high1 = halos(upper, lower)
    first = kernel_call(
        functools.partial(middle_kernel, blocks), "edge_first",
        [group] * 6 + [cells] * 2, [ANYWHERE] * 12 + [IN_VMEM, IN_SMEM], (ANYWHERE,) * 8,
        scratch(columns, dma((29,))), 10,
        [low0, own[0], own[3], high0, *inner, own_coef, pair, other, params, place_of],
    )
    cell_of = obs_index // LANES + HALO * blocks
    lane_of = obs_index % LANES
    shift_of = (jnp.arange(obs_index.shape[0], dtype=jnp.int32) - lane_of) % LANES
    field, predicted = kernel_call(
        functools.partial(last_kernel, blocks), "edge_last",
        [flat, (members, obs_index.shape[0])],
        [ANYWHERE] * 15 + [IN_VMEM] + [IN_SMEM] * 3, (ANYWHERE, IN_VMEM),
        scratch(columns, staged, dma((29,)), dma((blocks,))), 15,
        [low1, low0, high0, high1, *first, own_coef, pair, other, params, place_of, cell_of, shift_of],
    )
    return field.reshape(shape), predicted, inner[0]


def products_kernel(total_obs, per_group, spread, everyone, own, values, variance, same, out):
    weight = 1.0 / (variance[...] * total_obs)
    innovation = (values[...] - own[...]) * weight
    predicted = everyone[...]
    anomalies = (predicted - hdot(same[...], predicted) / per_group) * spread
    right = jnp.concatenate([anomalies * weight, innovation], axis=0)
    out[...] = lax.dot_general(
        anomalies,
        right,
        (((1,), (1,)), ((), ())),
        precision=lax.Precision.HIGHEST,
        preferred_element_type=jnp.float32,
    )


def update_kernel(per_group, summands, same, own_same, rank_row, rank_col, anomalies, own, out):
    members = same.shape[0]
    total = summands[0]
    for index in range(1, summands.shape[0]):
        total = total + summands[index]
    together = same[...]
    row = lax.broadcasted_iota(jnp.int32, (members, members), 0)
    col = lax.broadcasted_iota(jnp.int32, (members, members), 1)
    system = jnp.where(row == col, 1.0, 0.0) + together * total[:, 0:members]
    right = own_same[...] * total[:, members:]
    for pivot in range(per_group):
        pick = jnp.where(rank_row[...] == pivot, together, 0.0)
        pivot_system = hdot(pick, system)
        pivot_right = hdot(pick, right)
        pivot_value = jnp.sum(pick * pivot_system, axis=1, keepdims=True)
        factor = jnp.sum(pick * system, axis=1, keepdims=True)
        is_pivot = rank_col[...] == pivot
        scale = 1.0 / pivot_value
        scaled_system, scaled_right = pivot_system * scale, pivot_right * scale
        system = jnp.where(is_pivot, scaled_system, system - factor * scaled_system)
        right = jnp.where(is_pivot, scaled_right, right - factor * scaled_right)
    change = lax.dot_general(
        right,
        anomalies[...],
        (((0,), (0,)), ((), ())),
        precision=lax.Precision.HIGHEST,
        preferred_element_type=jnp.float32,
    )
    out[...] = own[...] + change


def local(tracer, coefficients, parameters, obs_index, obs_values, obs_variance, member_group):
    local_members, rows, columns = tracer.shape
    ens_pos = lax.axis_index("ens")
    ens_count = lax.axis_size("ens")
    slab_count = lax.axis_size("slab")
    if ens_count != 4 or coefficients.shape[0] != 4 or slab_count & (slab_count - 1):
        raise ValueError("mesh shape")
    forward = [(i, i + 1) for i in range(slab_count - 1)]
    backward = [(target, source) for source, target in forward]

    def over_ens(mine):
        pair = jnp.stack([mine, lax.ppermute(mine, "ens", [(i, i ^ 1) for i in range(ens_count)])])
        return pair, lax.ppermute(pair, "ens", [(i, i ^ 2) for i in range(ens_count)])

    def halos(upper, lower):
        return lax.ppermute(upper, "slab", forward), lax.ppermute(lower, "slab", backward)

    place_of = jnp.reshape(ens_pos, (1,))
    own, coef_edges = row_groups(tracer, coefficients, place_of)
    low0, high0 = halos(own[3], own[0])

    edge_low, edge_high = halos(*coef_edges)
    pair, other = over_ens(jnp.stack([edge_low, edge_high]))

    members = member_group.shape[0]
    per_group = members // GROUPS
    spread = 1.0 / math.sqrt(per_group - 1)
    same_bool = member_group[:, None] == member_group[None, :]
    same = same_bool.astype(jnp.float32)
    earlier = jnp.arange(members)[None, :] < jnp.arange(members)[:, None]
    rank = jnp.sum((same_bool & earlier).astype(jnp.int32), axis=1)
    own_same = lax.dynamic_slice_in_dim(same, ens_pos * local_members, local_members, 1)
    field, predicted, first_done = transport(
        tracer.shape, own, low0, high0,
        coefficients, pair, other, parameters, place_of, obs_index, halos,
    )

    later, _ = lax.optimization_barrier((parameters, first_done))
    shared = jnp.concatenate(over_ens(later), axis=0)
    all_params = jnp.concatenate(
        [lax.dynamic_index_in_dim(shared, ens_pos ^ i, 0, False) for i in range(ens_count)], axis=0
    )
    param_anomalies = (all_params - hdot(same, all_params) / per_group) * spread
    everyone = lax.all_gather(predicted, "ens", axis=0, tiled=True)
    total_obs = obs_variance.shape[0] * slab_count
    products = pl.pallas_call(
        functools.partial(products_kernel, float(total_obs), per_group, spread),
        out_shape=jax.ShapeDtypeStruct((members, members + local_members), jnp.float32),
        compiler_params=pltpu.CompilerParams(vmem_limit_bytes=VMEM_LIMIT),
        name="products",
    )(everyone, predicted, obs_values, obs_variance[None, :], same)
    distance = 1
    while distance < slab_count:
        pairs = [(i, i ^ distance) for i in range(slab_count)]
        products = products + lax.ppermute(products, "slab", pairs)
        distance *= 2
    updated = pl.pallas_call(
        functools.partial(update_kernel, per_group),
        out_shape=jax.ShapeDtypeStruct(parameters.shape, jnp.float32),
        compiler_params=pltpu.CompilerParams(vmem_limit_bytes=VMEM_LIMIT),
        name="update",
    )(products[None], same, own_same, rank[None, :], rank[:, None], param_anomalies, parameters)
    return (field, updated)


def solution(mesh):
    in_specs = (
        P("ens", "slab", None),
        P(None, "slab", None),
        P("ens", None),
        P("slab"),
        P("ens", "slab"),
        P("slab"),
        P(),
    )
    out_specs = (P("ens", "slab", None), P("ens", None))
    return jax.shard_map(local, mesh=mesh, in_specs=in_specs, out_specs=out_specs, check_vma=False)
```

```python
import functools
import math

import jax
import jax.numpy as jnp
from jax import lax
from jax.experimental import pallas as pl
from jax.experimental.pallas import tpu as pltpu
from jax.sharding import PartitionSpec as P

STEPS = 4
GROUPS = 8
HALO = 2 * STEPS
LANES = 128
SUBLANES = 8
ROWS = 16
GROUP = 4
LAG = 3
VMEM_LIMIT = 16 * 1024 * 1024
TALL_LIMIT = 58 * 1024 * 1024
COST_BYTES = 200000
ANYWHERE = pl.BlockSpec(memory_space=pltpu.HBM)
IN_VMEM = pl.BlockSpec(memory_space=pltpu.VMEM)
IN_SMEM = pl.BlockSpec(memory_space=pltpu.SMEM)


def hdot(left, right):
    return jnp.dot(left, right, precision=lax.Precision.HIGHEST, preferred_element_type=jnp.float32)


def limited(left, right):
    return jnp.minimum(jnp.maximum(left, jnp.minimum(right, 0.0)), jnp.maximum(right, 0.0))


def block_at(block):
    return pl.ds(pl.multiple_of(block * LANES, LANES), LANES)


def wide(row):
    return jnp.broadcast_to(row, (SUBLANES, LANES))


def columns_pass(source, row, target, target_row, coef, params, blocks):
    lane = lax.broadcasted_iota(jnp.int32, (SUBLANES, LANES), 1)
    first, last = lane == 0, lane == LANES - 1
    places = [coef_row(array, row) for array in range(4)]
    c, c_rolled, d, d_rolled, slope, twice, left, right, laplace = ({} for _ in range(9))
    for tick in range(blocks + 2 * LAG + 4):
        b = tick - 1
        if b <= blocks:
            c[b] = source[row, :, block_at(b % blocks)]
            c_rolled[b] = pltpu.roll(c[b], LANES - 1, 1)
        b = tick - 2
        if -1 <= b <= blocks:
            c_next = c_rolled[b]
            if b < blocks:
                c_next = jnp.where(last, c_rolled[b + 1], c_next)
            d[b] = c_next - c[b]
            d_rolled[b] = pltpu.roll(d[b], 1, 1)
        b = tick - 2 - LAG
        if -1 <= b <= blocks:
            d_back = d_rolled[b]
            if b >= 0:
                d_back = jnp.where(first, d_rolled[b - 1], d_back)
            slope[b] = limited(d_back, d[b])
            twice[b] = d[b] + d[b]
            laplace[b] = d[b] - d_back
            left[b] = pltpu.roll(twice[b] - slope[b], 1, 1)
            right[b] = pltpu.roll(slope[b], LANES - 1, 1)
        b = tick - 3 - 2 * LAG
        if 0 <= b < blocks:
            at = block_at(b)
            speed = wide(coef[places[1], :, at])
            forward = jnp.where(first, left[b - 1], left[b])
            backward = twice[b] - jnp.where(last, right[b + 1], right[b])
            change = jnp.where(speed > 0.0, forward, backward) + slope[b]
            value = c[b] - (0.5 * speed) * change
            value = value + wide(coef[places[2], :, at]) * laplace[b]
            value = value + params[:, at] * wide(coef[places[3], :, at])
            target[target_row, :, at] = value


def rows_pass(source, row, places, partial, target, coef, block, blocks):
    at = block_at(block)
    c = [source[row - 2 + i, :, at] for i in range(GROUP + 4)]
    d = [c[i + 1] - c[i] for i in range(GROUP + 3)]
    slope = [None] + [limited(d[i - 1], d[i]) for i in range(1, GROUP + 3)]
    twice = [None] + [d[i] + d[i] for i in range(1, GROUP + 2)]
    for i in range(2, GROUP + 2):
        here = row - 2 + i
        speed = wide(coef[places[i - 2][0], :, at])
        forward = twice[i - 1] - slope[i - 1]
        backward = twice[i] - slope[i + 1]
        change = wide(coef[places[i - 2][1], :, at]) * (d[i] - d[i - 1])
        change = change - (0.5 * speed) * (jnp.where(speed > 0.0, forward, backward) + slope[i])
        value = partial[i - 2, :, at] + change
        if target.shape[1:] == value.shape:
            target[here * blocks + block] = value
        else:
            target[here, :, at] = value


def advance_group(source, target, row, partial, coef, params, blocks):
    for i in range(GROUP):
        columns_pass(source, row + i, partial, i, coef, params, blocks)
    places = [[coef_row(array, row + i) for array in (0, 2)] for i in range(GROUP)]
    for block in range(blocks):
        rows_pass(source, row, places, partial, target, coef, block, blocks)


class Copies:
    def __init__(self, sems):
        self.sems, self.used = sems, 0

    def start(self, source, target):
        copy = pltpu.make_async_copy(source, target, self.sems.at[self.used])
        self.used += 1
        assert self.used <= self.sems.shape[0]
        copy.start()
        return copy


def place(row):
    return pl.ds(row + HALO, GROUP)


def region(levels, level, row, blocks):
    if level == STEPS:
        return levels[level].at[pl.ds((row + HALO) * blocks, GROUP * blocks)]
    return levels[level].at[place(row)]


def fill_rows(blocks, first_rows, tracer, outs, staged, sems):
    def copy(block):
        return pltpu.make_async_copy(tracer.at[:, block_at(block)], staged.at[block], sems.at[block])

    @pl.loop(0, blocks)
    def _(block):
        copy(block).start()

    @pl.loop(0, blocks)
    def _(block):
        copy(block).wait()
        for out, first_row in zip(outs, first_rows):
            for row in range(GROUP):
                out[row, :, block_at(block)] = staged[
                    block, pl.ds(first_row + row, SUBLANES, stride=ROWS), :
                ]


def outer_rows_kernel(
    blocks, tracer, own_coef, place_of, up, down, up_coef, down_coef, staged, sems, coef_sems
):
    copies = Copies(coef_sems)
    source = own_coef.at[place_of[0]]
    waits = [
        copies.start(source.at[pl.ds(ROWS - HALO, HALO)], up_coef),
        copies.start(source.at[pl.ds(0, HALO)], down_coef),
    ]
    fill_rows(blocks, (0, ROWS - GROUP), tracer, (down, up), staged, sems)
    for copy in waits:
        copy.wait()


def inner_rows_kernel(blocks, tracer, outer, low, high, staged, sems):
    fill_rows(blocks, (GROUP, ROWS - 2 * GROUP), tracer, (low, high), staged, sems)


def interior_kernel(blocks, own0, own1, own2, own3, own_coef, params, *rest):
    outs, (*levels, partial, coef, sems) = rest[:5], rest[5:]
    copies = Copies(sems)
    waits = [
        copies.start(own.at[0:GROUP], levels[0].at[place(GROUP * i)])
        for i, own in enumerate((own0, own1, own2, own3))
    ]
    waits += [
        copies.start(own_coef.at[array], coef.at[pl.ds(array * ROWS, ROWS), 0]) for array in range(4)
    ]
    for copy in waits:
        copy.wait()
    for level, start, count in ((0, 2, 3), (1, 4, 2), (2, 6, 1)):
        @pl.loop(0, count)
        def _(i):
            row = start + HALO + GROUP * i
            advance_group(levels[level], levels[level + 1], row, partial, coef, params, blocks)

    waits = [
        copies.start(levels[level].at[place(row)], out)
        for out, (level, row) in zip(outs, ((1, 2), (1, 10), (2, 4), (2, 8), (3, 6)))
    ]
    for copy in waits:
        copy.wait()


def edge_steps(outer, blocks, waits, levels, partial, coef, params, ready):
    for level in range(STEPS):
        for copy in waits[level]:
            copy.wait()
        low, high = 2 * level - outer, ROWS + outer - GROUP - 2 * level

        @pl.loop(0, 2)
        def _(side):
            row = low + HALO + side * (high - low)
            advance_group(levels[level], levels[level + 1], row, partial, coef, params, blocks)

        ready(level, low, high)


def coef_row(array, row):
    own = array * ROWS + row - HALO
    low = 4 * ROWS + 2 * HALO * array + row
    high = 4 * ROWS + 2 * HALO * array + row - ROWS
    return jnp.where(row < HALO, low, jnp.where(row < HALO + ROWS, own, high))


def load_coef(copies, own_coef, pair, other, place_of, coef):
    waits = [
        copies.start(own_coef.at[array], coef.at[pl.ds(array * ROWS, ROWS), 0]) for array in range(4)
    ]
    for number, source in enumerate((pair.at[0], pair.at[1], other.at[0], other.at[1])):
        array = jnp.bitwise_xor(place_of[0], number)
        for side in range(2):
            first = 4 * ROWS + 2 * HALO * array + HALO * side
            waits.append(copies.start(source.at[side], coef.at[pl.ds(first, HALO), 0]))
    return waits


def middle_kernel(blocks, *refs):
    sources, refs = refs[:9], refs[9:]
    own_coef, pair, other, params, place_of = refs[:5]
    outs, (*levels, partial, coef, sems) = refs[5:13], refs[13:]
    copies = Copies(sems)
    places = ((0, -4), (0, 0), (0, 12), (0, 16), (1, 2), (1, 10), (2, 4), (2, 8), (3, 6))
    waits = [[] for _ in range(STEPS)]
    for source, (level, row) in zip(sources, places):
        count = GROUP * blocks if level == STEPS else GROUP
        waits[level].append(
            copies.start(source.at[0:count], region(levels, level, row, blocks))
        )
    waits[0] += load_coef(copies, own_coef, pair, other, place_of, coef)
    sends = []

    def ready(level, low, high):
        for row, out in ((low, outs[2 * level]), (high, outs[2 * level + 1])):
            sends.append(copies.start(region(levels, level + 1, row, blocks), out))

    edge_steps(2, blocks, waits, levels, partial, coef, params, ready)
    for copy in sends:
        copy.wait()


def last_kernel(blocks, *refs):
    sources, refs = refs[:12], refs[12:]
    own_coef, pair, other, params, place_of, cell_of, shift_of = refs[:7]
    low_out, high_out, predicted, *levels, partial, coef, sems = refs[7:]
    copies = Copies(sems)
    places = (
        (0, -8), (0, -4), (0, 16), (0, 20),
        (1, -2), (1, 14), (2, 0), (2, 12), (3, 2), (3, 10), (4, 4), (4, 8),
    )
    waits = [[] for _ in range(STEPS + 1)]
    for source, (level, row) in zip(sources, places):
        count = GROUP * blocks if level == STEPS else GROUP
        waits[level].append(
            copies.start(source.at[0:count], region(levels, level, row, blocks))
        )
    waits[0] += load_coef(copies, own_coef, pair, other, place_of, coef)
    edge_steps(6, blocks, waits, levels, partial, coef, params, lambda *_: None)
    for copy in waits[STEPS]:
        copy.wait()

    sends = [
        copies.start(region(levels, STEPS, row, blocks), out)
        for row, out in ((0, low_out), (ROWS - GROUP, high_out))
    ]
    lane = lax.broadcasted_iota(jnp.int32, (SUBLANES, LANES), 1)

    @pl.loop(0, predicted.shape[1] // LANES)
    def _(block):
        base = block * LANES
        found = jnp.zeros((SUBLANES, LANES), jnp.float32)
        for i in range(LANES):
            value = levels[STEPS][cell_of[base + i]]
            found = jnp.where(lane == i, pltpu.roll(value, shift_of[base + i], 1), found)
        predicted[:, block_at(block)] = found

    for copy in sends:
        copy.wait()


def field_kernel(blocks, *refs):
    parts, (out, cells, staged, sems, out_sems) = refs[: ROWS // GROUP], refs[ROWS // GROUP :]
    copies = Copies(sems)
    size = GROUP * blocks
    waits = [
        copies.start(part, cells.at[pl.ds(i * size, size)]) for i, part in enumerate(parts)
    ]
    for copy in waits:
        copy.wait()

    def out_copy(block):
        return pltpu.make_async_copy(staged.at[block], out.at[:, block_at(block)], out_sems.at[block])

    @pl.loop(0, blocks)
    def _(block):
        for row in range(ROWS):
            staged[block, pl.ds(row, SUBLANES, stride=ROWS), :] = cells[row * blocks + block]
        out_copy(block).start()

    @pl.loop(0, blocks)
    def _(block):
        out_copy(block).wait()


def scratch(columns, *more):
    return (
        [pltpu.VMEM((ROWS + 2 * HALO, SUBLANES, columns), jnp.float32)] * STEPS
        + [
            pltpu.VMEM(
                ((ROWS + 2 * HALO) * columns // LANES, SUBLANES, LANES), jnp.float32
            ),
            pltpu.VMEM((GROUP, SUBLANES, columns), jnp.float32),
            pltpu.VMEM((4 * (ROWS + 2 * HALO), 1, columns), jnp.float32),
        ]
        + list(more)
    )


def kernel_call(body, name, outs, specs, out_specs, scratches, cost, operands):
    return pl.pallas_call(
        body,
        out_shape=tuple(jax.ShapeDtypeStruct(shape, jnp.float32) for shape in outs),
        in_specs=specs,
        out_specs=out_specs,
        scratch_shapes=scratches,
        compiler_params=pltpu.CompilerParams(vmem_limit_bytes=TALL_LIMIT),
        cost_estimate=pl.CostEstimate(flops=0, bytes_accessed=cost * COST_BYTES, transcendentals=0),
        name=name,
    )(*operands)


def row_groups(tracer, coefficients, place_of):
    members, rows, columns = tracer.shape
    if members != SUBLANES or rows != ROWS:
        raise ValueError("block shape")
    blocks = columns // LANES
    flat = tracer.reshape(members * rows, columns)
    dma = pltpu.SemaphoreType.DMA
    scratches = [pltpu.VMEM((blocks, members * rows, LANES), jnp.float32), dma((blocks,))]
    group, edge = (GROUP, members, columns), (HALO, columns)
    up, down, up_coef, down_coef = kernel_call(
        functools.partial(outer_rows_kernel, blocks), "outer_rows",
        [group, group, edge, edge], [ANYWHERE, ANYWHERE, IN_SMEM],
        (IN_VMEM,) * 4,
        scratches + [dma((2,))], 3, [flat, coefficients, place_of],
    )
    low, high = kernel_call(
        functools.partial(inner_rows_kernel, blocks), "inner_rows",
        [group] * 2, [ANYWHERE, ANYWHERE], (IN_VMEM,) * 2,
        scratches, 3, [flat, up],
    )
    return (down, low, high, up), (up_coef, down_coef)


def transport(shape, own, low0, high0, own_coef, pair, other, params, place_of, obs_index, halos):
    members, rows, columns = shape
    blocks = columns // LANES
    group = (GROUP, members, columns)
    flat = (members * rows, columns)
    cells = (GROUP * blocks, members, LANES)
    dma = pltpu.SemaphoreType.DMA
    staged = pltpu.VMEM((blocks, members * rows, LANES), jnp.float32)
    gated, pair = lax.optimization_barrier((params, pair))
    inner = kernel_call(
        functools.partial(interior_kernel, blocks), "interior",
        [group] * 5, [ANYWHERE] * 5 + [IN_VMEM], (ANYWHERE,) * 5,
        scratch(columns, dma((16,))), 8, [*own, own_coef, gated],
    )
    upper, lower, low0, high0, *_ = lax.optimization_barrier(
        (own[2], own[1], low0, high0, inner[0])
    )
    low1, high1 = halos(upper, lower)
    first = kernel_call(
        functools.partial(middle_kernel, blocks), "edge_first",
        [group] * 6 + [cells] * 2, [ANYWHERE] * 12 + [IN_VMEM, IN_SMEM], (ANYWHERE,) * 8,
        scratch(columns, dma((29,))), 10,
        [low0, own[0], own[3], high0, *inner, own_coef, pair, other, params, place_of],
    )
    cell_of = obs_index // LANES + HALO * blocks
    lane_of = obs_index % LANES
    shift_of = (jnp.arange(obs_index.shape[0], dtype=jnp.int32) - lane_of) % LANES
    low4, high4, predicted = kernel_call(
        functools.partial(last_kernel, blocks), "edge_last",
        [cells, cells, (members, obs_index.shape[0])],
        [ANYWHERE] * 15 + [IN_VMEM] + [IN_SMEM] * 3, (ANYWHERE, ANYWHERE, IN_VMEM),
        scratch(columns, dma((31,))), 15,
        [low1, low0, high0, high1, *first, own_coef, pair, other, params, place_of, cell_of, shift_of],
    )
    (field,) = kernel_call(
        functools.partial(field_kernel, blocks), "field",
        [flat], [ANYWHERE] * 4, (ANYWHERE,),
        [pltpu.VMEM((rows * blocks, members, LANES), jnp.float32), staged, dma((4,)), dma((blocks,))],
        4, [low4, first[6], first[7], high4],
    )
    return field.reshape(shape), predicted, inner[0]


def products_kernel(total_obs, per_group, spread, everyone, own, values, variance, same, out):
    weight = 1.0 / (variance[...] * total_obs)
    innovation = (values[...] - own[...]) * weight
    predicted = everyone[...]
    anomalies = (predicted - hdot(same[...], predicted) / per_group) * spread
    right = jnp.concatenate([anomalies * weight, innovation], axis=0)
    out[...] = lax.dot_general(
        anomalies,
        right,
        (((1,), (1,)), ((), ())),
        precision=lax.Precision.HIGHEST,
        preferred_element_type=jnp.float32,
    )


def update_kernel(per_group, summands, same, own_same, rank_row, rank_col, anomalies, own, out):
    members = same.shape[0]
    total = summands[0]
    for index in range(1, summands.shape[0]):
        total = total + summands[index]
    together = same[...]
    row = lax.broadcasted_iota(jnp.int32, (members, members), 0)
    col = lax.broadcasted_iota(jnp.int32, (members, members), 1)
    system = jnp.where(row == col, 1.0, 0.0) + together * total[:, 0:members]
    right = own_same[...] * total[:, members:]
    for pivot in range(per_group):
        pick = jnp.where(rank_row[...] == pivot, together, 0.0)
        pivot_system = hdot(pick, system)
        pivot_right = hdot(pick, right)
        pivot_value = jnp.sum(pick * pivot_system, axis=1, keepdims=True)
        factor = jnp.sum(pick * system, axis=1, keepdims=True)
        is_pivot = rank_col[...] == pivot
        scale = 1.0 / pivot_value
        scaled_system, scaled_right = pivot_system * scale, pivot_right * scale
        system = jnp.where(is_pivot, scaled_system, system - factor * scaled_system)
        right = jnp.where(is_pivot, scaled_right, right - factor * scaled_right)
    change = lax.dot_general(
        right,
        anomalies[...],
        (((0,), (0,)), ((), ())),
        precision=lax.Precision.HIGHEST,
        preferred_element_type=jnp.float32,
    )
    out[...] = own[...] + change


def local(tracer, coefficients, parameters, obs_index, obs_values, obs_variance, member_group):
    local_members, rows, columns = tracer.shape
    ens_pos = lax.axis_index("ens")
    ens_count = lax.axis_size("ens")
    slab_count = lax.axis_size("slab")
    if ens_count != 4 or coefficients.shape[0] != 4 or slab_count & (slab_count - 1):
        raise ValueError("mesh shape")
    forward = [(i, i + 1) for i in range(slab_count - 1)]
    backward = [(target, source) for source, target in forward]

    def over_ens(mine):
        pair = jnp.stack([mine, lax.ppermute(mine, "ens", [(i, i ^ 1) for i in range(ens_count)])])
        return pair, lax.ppermute(pair, "ens", [(i, i ^ 2) for i in range(ens_count)])

    def halos(upper, lower):
        return lax.ppermute(upper, "slab", forward), lax.ppermute(lower, "slab", backward)

    place_of = jnp.reshape(ens_pos, (1,))
    own, coef_edges = row_groups(tracer, coefficients, place_of)
    low0, high0 = halos(own[3], own[0])

    edge_low, edge_high = halos(*coef_edges)
    pair, other = over_ens(jnp.stack([edge_low, edge_high]))

    members = member_group.shape[0]
    per_group = members // GROUPS
    spread = 1.0 / math.sqrt(per_group - 1)
    same_bool = member_group[:, None] == member_group[None, :]
    same = same_bool.astype(jnp.float32)
    earlier = jnp.arange(members)[None, :] < jnp.arange(members)[:, None]
    rank = jnp.sum((same_bool & earlier).astype(jnp.int32), axis=1)
    own_same = lax.dynamic_slice_in_dim(same, ens_pos * local_members, local_members, 1)
    field, predicted, first_done = transport(
        tracer.shape, own, low0, high0,
        coefficients, pair, other, parameters, place_of, obs_index, halos,
    )

    later, _ = lax.optimization_barrier((parameters, first_done))
    shared = jnp.concatenate(over_ens(later), axis=0)
    all_params = jnp.concatenate(
        [lax.dynamic_index_in_dim(shared, ens_pos ^ i, 0, False) for i in range(ens_count)], axis=0
    )
    param_anomalies = (all_params - hdot(same, all_params) / per_group) * spread
    everyone = lax.all_gather(predicted, "ens", axis=0, tiled=True)
    total_obs = obs_variance.shape[0] * slab_count
    products = pl.pallas_call(
        functools.partial(products_kernel, float(total_obs), per_group, spread),
        out_shape=jax.ShapeDtypeStruct((members, members + local_members), jnp.float32),
        compiler_params=pltpu.CompilerParams(vmem_limit_bytes=VMEM_LIMIT),
        name="products",
    )(everyone, predicted, obs_values, obs_variance[None, :], same)
    distance = 1
    while distance < slab_count:
        pairs = [(i, i ^ distance) for i in range(slab_count)]
        products = products + lax.ppermute(products, "slab", pairs)
        distance *= 2
    updated = pl.pallas_call(
        functools.partial(update_kernel, per_group),
        out_shape=jax.ShapeDtypeStruct(parameters.shape, jnp.float32),
        compiler_params=pltpu.CompilerParams(vmem_limit_bytes=VMEM_LIMIT),
        name="update",
    )(products[None], same, own_same, rank[None, :], rank[:, None], param_anomalies, parameters)
    return (field, updated)


def solution(mesh):
    in_specs = (
        P("ens", "slab", None),
        P(None, "slab", None),
        P("ens", None),
        P("slab"),
        P("ens", "slab"),
        P("slab"),
        P(),
    )
    out_specs = (P("ens", "slab", None), P("ens", None))
    return jax.shard_map(local, mesh=mesh, in_specs=in_specs, out_specs=out_specs, check_vma=False)
```

```python
import functools
import math

import jax
import jax.numpy as jnp
from jax import lax
from jax.experimental import pallas as pl
from jax.experimental.pallas import tpu as pltpu
from jax.sharding import PartitionSpec as P

STEPS = 4
GROUPS = 8
HALO = 2 * STEPS
LANES = 128
SUBLANES = 8
ROWS = 16
GROUP = 4
LAG = 3
TOGETHER = 2
WIDE = 8
MOVED = 16
PICKED = 32
ALL_ROWS = ROWS + 2 * HALO
VMEM_LIMIT = 16 * 1024 * 1024
TALL_LIMIT = 58 * 1024 * 1024
COST_BYTES = 200000
ANYWHERE = pl.BlockSpec(memory_space=pltpu.HBM)
IN_VMEM = pl.BlockSpec(memory_space=pltpu.VMEM)
IN_SMEM = pl.BlockSpec(memory_space=pltpu.SMEM)


def hdot(left, right):
    return jnp.dot(left, right, precision=lax.Precision.HIGHEST, preferred_element_type=jnp.float32)


def limited(left, right):
    return jnp.minimum(jnp.maximum(left, jnp.minimum(right, 0.0)), jnp.maximum(right, 0.0))


def block_at(block):
    return pl.ds(pl.multiple_of(block * LANES, LANES), LANES)


def wide(row):
    return jnp.broadcast_to(row, (SUBLANES, LANES))


def columns_pass(levels, cell, row, count, partial, first_cell, coef, params, blocks):
    lane = lax.broadcasted_iota(jnp.int32, (SUBLANES, LANES), 1)
    first, last = lane == 0, lane == LANES - 1
    places = [[coef_row(array, row + i) for array in range(4)] for i in range(count)]
    c, c_rolled, d, d_rolled, slope, twice, left, right, laplace = ({} for _ in range(9))
    for tick in range(blocks + 2 * LAG + 4):
        for i in range(count):
            b = tick - 1
            if b <= blocks:
                c[i, b] = levels[cell + i * blocks + b % blocks]
                c_rolled[i, b] = pltpu.roll(c[i, b], LANES - 1, 1)
            b = tick - 2
            if -1 <= b <= blocks:
                c_next = c_rolled[i, b]
                if b < blocks:
                    c_next = jnp.where(last, c_rolled[i, b + 1], c_next)
                d[i, b] = c_next - c[i, b]
                d_rolled[i, b] = pltpu.roll(d[i, b], 1, 1)
            b = tick - 2 - LAG
            if -1 <= b <= blocks:
                d_back = d_rolled[i, b]
                if b >= 0:
                    d_back = jnp.where(first, d_rolled[i, b - 1], d_back)
                slope[i, b] = limited(d_back, d[i, b])
                twice[i, b] = d[i, b] + d[i, b]
                laplace[i, b] = d[i, b] - d_back
                left[i, b] = pltpu.roll(twice[i, b] - slope[i, b], 1, 1)
                right[i, b] = pltpu.roll(slope[i, b], LANES - 1, 1)
            b = tick - 3 - 2 * LAG
            if 0 <= b < blocks:
                at = block_at(b)
                speed = wide(coef[places[i][1], :, at])
                forward = jnp.where(first, left[i, b - 1], left[i, b])
                backward = twice[i, b] - jnp.where(last, right[i, b + 1], right[i, b])
                change = jnp.where(speed > 0.0, forward, backward) + slope[i, b]
                value = c[i, b] - (0.5 * speed) * change
                value = value + wide(coef[places[i][2], :, at]) * laplace[i, b]
                value = value + params[:, at] * wide(coef[places[i][3], :, at])
                partial[first_cell + i * blocks + b] = value


def rows_pass(levels, cell, places, partial, result, coef, block, blocks):
    at = block_at(block)
    c = [levels[cell + (i - 2) * blocks + block] for i in range(GROUP + 4)]
    d = [c[i + 1] - c[i] for i in range(GROUP + 3)]
    slope = [None] + [limited(d[i - 1], d[i]) for i in range(1, GROUP + 3)]
    twice = [None] + [d[i] + d[i] for i in range(1, GROUP + 2)]
    for i in range(2, GROUP + 2):
        speed = wide(coef[places[i - 2][0], :, at])
        forward = twice[i - 1] - slope[i - 1]
        backward = twice[i] - slope[i + 1]
        change = wide(coef[places[i - 2][1], :, at]) * (d[i] - d[i - 1])
        change = change - (0.5 * speed) * (jnp.where(speed > 0.0, forward, backward) + slope[i])
        here = (i - 2) * blocks + block
        result[here] = partial[here] + change


def advance_group(level, row, levels, partial, result, coef, params, blocks):
    cell = (level * ALL_ROWS + row) * blocks

    @pl.loop(0, GROUP // TOGETHER)
    def _(i):
        done = i * (TOGETHER * blocks)
        columns_pass(
            levels, cell + done, row + i * TOGETHER, TOGETHER, partial, done, coef, params, blocks
        )

    places = [[coef_row(array, row + i) for array in (0, 2)] for i in range(GROUP)]

    @pl.loop(0, blocks // WIDE)
    def _(wide_block):
        for i in range(WIDE):
            rows_pass(levels, cell, places, partial, result, coef, wide_block * WIDE + i, blocks)

    @pl.loop(0, GROUP * blocks // MOVED)
    def _(i):
        first = i * MOVED
        moved = [result[first + k] for k in range(MOVED)]
        for k in range(MOVED):
            levels[cell + ALL_ROWS * blocks + first + k] = moved[k]


class Copies:
    def __init__(self, sems):
        self.sems, self.used = sems, 0

    def make(self, source, target):
        copy = pltpu.make_async_copy(source, target, self.sems.at[self.used])
        self.used += 1
        assert self.used <= self.sems.shape[0]
        return copy

    def start(self, source, target):
        copy = self.make(source, target)
        copy.start()
        return copy


def region(levels, level, row, blocks):
    return levels.at[pl.ds((level * ALL_ROWS + HALO + row) * blocks, GROUP * blocks)]


def fill_rows(blocks, first_rows, tracer, outs, staged, sems):
    def copy(block):
        return pltpu.make_async_copy(tracer.at[:, block_at(block)], staged.at[block], sems.at[block])

    @pl.loop(0, blocks)
    def _(block):
        copy(block).start()

    @pl.loop(0, blocks)
    def _(block):
        copy(block).wait()
        for out, first_row in zip(outs, first_rows):
            for row in range(GROUP):
                out[row * blocks + block] = staged[
                    block, pl.ds(first_row + row, SUBLANES, stride=ROWS), :
                ]


def outer_rows_kernel(
    blocks, tracer, own_coef, place_of, up, down, up_coef, down_coef, staged, sems, coef_sems
):
    copies = Copies(coef_sems)
    source = own_coef.at[place_of[0]]
    waits = [
        copies.start(source.at[pl.ds(ROWS - HALO, HALO)], up_coef),
        copies.start(source.at[pl.ds(0, HALO)], down_coef),
    ]
    fill_rows(blocks, (0, ROWS - GROUP), tracer, (down, up), staged, sems)
    for copy in waits:
        copy.wait()


def inner_rows_kernel(blocks, tracer, outer, low, high, staged, sems):
    fill_rows(blocks, (GROUP, ROWS - 2 * GROUP), tracer, (low, high), staged, sems)


def interior_kernel(blocks, own0, own1, own2, own3, own_coef, params, *rest):
    outs, (levels, partial, result, coef, sems) = rest[:5], rest[5:]
    copies = Copies(sems)
    waits = [
        copies.start(own, region(levels, 0, GROUP * i, blocks))
        for i, own in enumerate((own0, own1, own2, own3))
    ]
    waits += [
        copies.start(own_coef.at[array], coef.at[pl.ds(array * ROWS, ROWS), 0]) for array in range(4)
    ]
    for copy in waits:
        copy.wait()

    @pl.loop(0, 6)
    def _(i):
        level = jnp.where(i < 3, 0, jnp.where(i < 5, 1, 2))
        row = jnp.where(i < 3, 2 + 4 * i, jnp.where(i < 5, 4 * i - 8, 6))
        advance_group(level, row + HALO, levels, partial, result, coef, params, blocks)

    waits = [
        copies.start(region(levels, level, row, blocks), out)
        for out, (level, row) in zip(outs, ((1, 2), (1, 10), (2, 4), (2, 8), (3, 6)))
    ]
    for copy in waits:
        copy.wait()


def edge_steps(outer, blocks, waits, sends, levels, partial, result, coef, params):
    @pl.loop(0, 2 * STEPS)
    def _(step):
        level, side = lax.div(step, 2), lax.rem(step, 2)
        for k in range(STEPS):
            @pl.when(step == 2 * k)
            def _():
                for copy in waits[k]:
                    copy.wait()

        low = 2 * level - outer
        high = ROWS + outer - GROUP - 2 * level
        row = jnp.where(side == 0, low, high) + HALO
        advance_group(level, row, levels, partial, result, coef, params, blocks)
        for k, copy in enumerate(sends):
            pl.when(step == k)(copy.start)


def coef_row(array, row):
    own = array * ROWS + row - HALO
    low = 4 * ROWS + 2 * HALO * array + row
    high = 4 * ROWS + 2 * HALO * array + row - ROWS
    return jnp.where(row < HALO, low, jnp.where(row < HALO + ROWS, own, high))


def load_coef(copies, own_coef, pair, other, place_of, coef):
    waits = [
        copies.start(own_coef.at[array], coef.at[pl.ds(array * ROWS, ROWS), 0]) for array in range(4)
    ]
    for number, source in enumerate((pair.at[0], pair.at[1], other.at[0], other.at[1])):
        array = jnp.bitwise_xor(place_of[0], number)
        for side in range(2):
            first = 4 * ROWS + 2 * HALO * array + HALO * side
            waits.append(copies.start(source.at[side], coef.at[pl.ds(first, HALO), 0]))
    return waits


def middle_kernel(blocks, *refs):
    sources, refs = refs[:9], refs[9:]
    own_coef, pair, other, params, place_of = refs[:5]
    outs, (levels, partial, result, coef, sems) = refs[5:13], refs[13:]
    copies = Copies(sems)
    places = ((0, -4), (0, 0), (0, 12), (0, 16), (1, 2), (1, 10), (2, 4), (2, 8), (3, 6))
    waits = [[] for _ in range(STEPS)]
    for source, (level, row) in zip(sources, places):
        waits[level].append(copies.start(source, region(levels, level, row, blocks)))
    waits[0] += load_coef(copies, own_coef, pair, other, place_of, coef)
    places = [(k + 1, row) for k in range(STEPS) for row in (2 * k - 2, ROWS + 2 - GROUP - 2 * k)]
    sends = [
        copies.make(region(levels, level, row, blocks), out)
        for out, (level, row) in zip(outs, places)
    ]
    edge_steps(2, blocks, waits, sends, levels, partial, result, coef, params)
    for copy in sends:
        copy.wait()


def last_kernel(blocks, *refs):
    sources, refs = refs[:12], refs[12:]
    own_coef, pair, other, params, place_of, cell_of, shift_of = refs[:7]
    low_out, high_out, predicted, levels, partial, result, coef, sems = refs[7:]
    copies = Copies(sems)
    places = (
        (0, -8), (0, -4), (0, 16), (0, 20),
        (1, -2), (1, 14), (2, 0), (2, 12), (3, 2), (3, 10), (4, 4), (4, 8),
    )
    waits = [[] for _ in range(STEPS + 1)]
    for source, (level, row) in zip(sources, places):
        waits[level].append(copies.start(source, region(levels, level, row, blocks)))
    waits[0] += load_coef(copies, own_coef, pair, other, place_of, coef)
    edge_steps(6, blocks, waits, (), levels, partial, result, coef, params)
    for copy in waits[STEPS]:
        copy.wait()
    sends = [
        copies.start(region(levels, STEPS, row, blocks), out)
        for row, out in ((0, low_out), (ROWS - GROUP, high_out))
    ]
    lane = lax.broadcasted_iota(jnp.int32, (SUBLANES, LANES), 1)

    @pl.loop(0, predicted.shape[1] // LANES)
    def _(block):
        base = block * LANES

        def some(part, found):
            for i in range(PICKED):
                o = part * PICKED + i
                value = pltpu.roll(levels[cell_of[base + o]], shift_of[base + o], 1)
                found = jnp.where(lane == o, value, found)
            return found

        empty = jnp.zeros((SUBLANES, LANES), jnp.float32)
        predicted[:, block_at(block)] = lax.fori_loop(0, LANES // PICKED, some, empty)

    for copy in sends:
        copy.wait()


def field_kernel(blocks, *refs):
    parts, (out, cells, staged, sems, out_sems) = refs[: ROWS // GROUP], refs[ROWS // GROUP :]
    copies = Copies(sems)
    size = GROUP * blocks
    waits = [
        copies.start(part, cells.at[pl.ds(i * size, size)]) for i, part in enumerate(parts)
    ]
    for copy in waits:
        copy.wait()

    def out_copy(block):
        return pltpu.make_async_copy(staged.at[block], out.at[:, block_at(block)], out_sems.at[block])

    @pl.loop(0, blocks)
    def _(block):
        for row in range(ROWS):
            staged[block, pl.ds(row, SUBLANES, stride=ROWS), :] = cells[row * blocks + block]
        out_copy(block).start()

    @pl.loop(0, blocks)
    def _(block):
        out_copy(block).wait()


def scratch(columns, *more):
    blocks = columns // LANES
    group = pltpu.VMEM((GROUP * blocks, SUBLANES, LANES), jnp.float32)
    return [
        pltpu.VMEM(((STEPS + 1) * ALL_ROWS * blocks, SUBLANES, LANES), jnp.float32),
        group,
        group,
        pltpu.VMEM((4 * ALL_ROWS, 1, columns), jnp.float32),
        *more,
    ]


def kernel_call(body, name, outs, specs, out_specs, scratches, cost, operands):
    return pl.pallas_call(
        body,
        out_shape=tuple(jax.ShapeDtypeStruct(shape, jnp.float32) for shape in outs),
        in_specs=specs,
        out_specs=out_specs,
        scratch_shapes=scratches,
        compiler_params=pltpu.CompilerParams(vmem_limit_bytes=TALL_LIMIT),
        cost_estimate=pl.CostEstimate(flops=0, bytes_accessed=cost * COST_BYTES, transcendentals=0),
        name=name,
    )(*operands)


def row_groups(tracer, coefficients, place_of):
    members, rows, columns = tracer.shape
    if members != SUBLANES or rows != ROWS:
        raise ValueError("block shape")
    blocks = columns // LANES
    flat = tracer.reshape(members * rows, columns)
    dma = pltpu.SemaphoreType.DMA
    scratches = [pltpu.VMEM((blocks, members * rows, LANES), jnp.float32), dma((blocks,))]
    group, edge = (GROUP * blocks, members, LANES), (HALO, columns)
    up, down, up_coef, down_coef = kernel_call(
        functools.partial(outer_rows_kernel, blocks), "outer_rows",
        [group, group, edge, edge], [ANYWHERE, ANYWHERE, IN_SMEM],
        (IN_VMEM,) * 4,
        scratches + [dma((2,))], 3, [flat, coefficients, place_of],
    )
    low, high = kernel_call(
        functools.partial(inner_rows_kernel, blocks), "inner_rows",
        [group] * 2, [ANYWHERE, ANYWHERE], (IN_VMEM,) * 2,
        scratches, 3, [flat, up],
    )
    return (down, low, high, up), (up_coef, down_coef)


def transport(shape, own, low0, high0, own_coef, pair, other, params, place_of, obs_index, halos):
    members, rows, columns = shape
    blocks = columns // LANES
    group = (GROUP * blocks, members, LANES)
    flat = (members * rows, columns)
    dma = pltpu.SemaphoreType.DMA
    staged = pltpu.VMEM((blocks, members * rows, LANES), jnp.float32)
    gated, pair = lax.optimization_barrier((params, pair))
    inner = kernel_call(
        functools.partial(interior_kernel, blocks), "interior",
        [group] * 5, [ANYWHERE] * 5 + [IN_VMEM], (ANYWHERE,) * 5,
        scratch(columns, dma((16,))), 8, [*own, own_coef, gated],
    )
    upper, lower, low0, high0, *_ = lax.optimization_barrier(
        (own[2], own[1], low0, high0, inner[0])
    )
    low1, high1 = halos(upper, lower)
    first = kernel_call(
        functools.partial(middle_kernel, blocks), "edge_first",
        [group] * 8, [ANYWHERE] * 12 + [IN_VMEM, IN_SMEM], (ANYWHERE,) * 8,
        scratch(columns, dma((29,))), 10,
        [low0, own[0], own[3], high0, *inner, own_coef, pair, other, params, place_of],
    )
    cell_of = obs_index // LANES + (STEPS * ALL_ROWS + HALO) * blocks
    lane_of = obs_index % LANES
    shift_of = (jnp.arange(obs_index.shape[0], dtype=jnp.int32) - lane_of) % LANES
    low4, high4, predicted = kernel_call(
        functools.partial(last_kernel, blocks), "edge_last",
        [group, group, (members, obs_index.shape[0])],
        [ANYWHERE] * 15 + [IN_VMEM] + [IN_SMEM] * 3, (ANYWHERE, ANYWHERE, IN_VMEM),
        scratch(columns, dma((31,))), 15,
        [low1, low0, high0, high1, *first, own_coef, pair, other, params, place_of, cell_of, shift_of],
    )
    (field,) = kernel_call(
        functools.partial(field_kernel, blocks), "field",
        [flat], [ANYWHERE] * 4, (ANYWHERE,),
        [pltpu.VMEM((rows * blocks, members, LANES), jnp.float32), staged, dma((4,)), dma((blocks,))],
        4, [low4, first[6], first[7], high4],
    )
    return field.reshape(shape), predicted, inner[0]


def products_kernel(total_obs, per_group, spread, everyone, own, values, variance, same, out):
    weight = 1.0 / (variance[...] * total_obs)
    innovation = (values[...] - own[...]) * weight
    predicted = everyone[...]
    anomalies = (predicted - hdot(same[...], predicted) / per_group) * spread
    right = jnp.concatenate([anomalies * weight, innovation], axis=0)
    out[...] = lax.dot_general(
        anomalies,
        right,
        (((1,), (1,)), ((), ())),
        precision=lax.Precision.HIGHEST,
        preferred_element_type=jnp.float32,
    )


def update_kernel(per_group, summands, same, own_same, rank_row, rank_col, anomalies, own, out):
    members = same.shape[0]
    total = summands[0]
    for index in range(1, summands.shape[0]):
        total = total + summands[index]
    together = same[...]
    row = lax.broadcasted_iota(jnp.int32, (members, members), 0)
    col = lax.broadcasted_iota(jnp.int32, (members, members), 1)
    system = jnp.where(row == col, 1.0, 0.0) + together * total[:, 0:members]
    right = own_same[...] * total[:, members:]
    for pivot in range(per_group):
        pick = jnp.where(rank_row[...] == pivot, together, 0.0)
        pivot_system = hdot(pick, system)
        pivot_right = hdot(pick, right)
        pivot_value = jnp.sum(pick * pivot_system, axis=1, keepdims=True)
        factor = jnp.sum(pick * system, axis=1, keepdims=True)
        is_pivot = rank_col[...] == pivot
        scale = 1.0 / pivot_value
        scaled_system, scaled_right = pivot_system * scale, pivot_right * scale
        system = jnp.where(is_pivot, scaled_system, system - factor * scaled_system)
        right = jnp.where(is_pivot, scaled_right, right - factor * scaled_right)
    change = lax.dot_general(
        right,
        anomalies[...],
        (((0,), (0,)), ((), ())),
        precision=lax.Precision.HIGHEST,
        preferred_element_type=jnp.float32,
    )
    out[...] = own[...] + change


def local(tracer, coefficients, parameters, obs_index, obs_values, obs_variance, member_group):
    local_members, rows, columns = tracer.shape
    ens_pos = lax.axis_index("ens")
    ens_count = lax.axis_size("ens")
    slab_count = lax.axis_size("slab")
    if ens_count != 4 or coefficients.shape[0] != 4 or slab_count & (slab_count - 1):
        raise ValueError("mesh shape")
    forward = [(i, i + 1) for i in range(slab_count - 1)]
    backward = [(target, source) for source, target in forward]

    def over_ens(mine):
        pair = jnp.stack([mine, lax.ppermute(mine, "ens", [(i, i ^ 1) for i in range(ens_count)])])
        return pair, lax.ppermute(pair, "ens", [(i, i ^ 2) for i in range(ens_count)])

    def halos(upper, lower):
        return lax.ppermute(upper, "slab", forward), lax.ppermute(lower, "slab", backward)

    place_of = jnp.reshape(ens_pos, (1,))
    own, coef_edges = row_groups(tracer, coefficients, place_of)
    low0, high0 = halos(own[3], own[0])

    edge_low, edge_high = halos(*coef_edges)
    pair, other = over_ens(jnp.stack([edge_low, edge_high]))

    members = member_group.shape[0]
    per_group = members // GROUPS
    spread = 1.0 / math.sqrt(per_group - 1)
    same_bool = member_group[:, None] == member_group[None, :]
    same = same_bool.astype(jnp.float32)
    earlier = jnp.arange(members)[None, :] < jnp.arange(members)[:, None]
    rank = jnp.sum((same_bool & earlier).astype(jnp.int32), axis=1)
    own_same = lax.dynamic_slice_in_dim(same, ens_pos * local_members, local_members, 1)
    field, predicted, first_done = transport(
        tracer.shape, own, low0, high0,
        coefficients, pair, other, parameters, place_of, obs_index, halos,
    )

    later, _ = lax.optimization_barrier((parameters, first_done))
    shared = jnp.concatenate(over_ens(later), axis=0)
    all_params = jnp.concatenate(
        [lax.dynamic_index_in_dim(shared, ens_pos ^ i, 0, False) for i in range(ens_count)], axis=0
    )
    param_anomalies = (all_params - hdot(same, all_params) / per_group) * spread
    everyone = lax.all_gather(predicted, "ens", axis=0, tiled=True)
    total_obs = obs_variance.shape[0] * slab_count
    products = pl.pallas_call(
        functools.partial(products_kernel, float(total_obs), per_group, spread),
        out_shape=jax.ShapeDtypeStruct((members, members + local_members), jnp.float32),
        compiler_params=pltpu.CompilerParams(vmem_limit_bytes=VMEM_LIMIT),
        name="products",
    )(everyone, predicted, obs_values, obs_variance[None, :], same)
    distance = 1
    while distance < slab_count:
        pairs = [(i, i ^ distance) for i in range(slab_count)]
        products = products + lax.ppermute(products, "slab", pairs)
        distance *= 2
    updated = pl.pallas_call(
        functools.partial(update_kernel, per_group),
        out_shape=jax.ShapeDtypeStruct(parameters.shape, jnp.float32),
        compiler_params=pltpu.CompilerParams(vmem_limit_bytes=VMEM_LIMIT),
        name="update",
    )(products[None], same, own_same, rank[None, :], rank[:, None], param_anomalies, parameters)
    return (field, updated)


def solution(mesh):
    in_specs = (
        P("ens", "slab", None),
        P(None, "slab", None),
        P("ens", None),
        P("slab"),
        P("ens", "slab"),
        P("slab"),
        P(),
    )
    out_specs = (P("ens", "slab", None), P("ens", None))
    return jax.shard_map(local, mesh=mesh, in_specs=in_specs, out_specs=out_specs, check_vma=False)
```

```python
import functools
import math

import jax
import jax.numpy as jnp
from jax import lax
from jax.experimental import pallas as pl
from jax.experimental.pallas import tpu as pltpu
from jax.sharding import PartitionSpec as P

STEPS = 4
GROUPS = 8
HALO = 2 * STEPS
LANES = 128
SUBLANES = 8
ROWS = 16
GROUP = 4
WIDE = 4
TOGETHER = 2
MOVED = 16
PICKED = 128
ALL_ROWS = ROWS + 2 * HALO
VMEM_LIMIT = 16 * 1024 * 1024
TALL_LIMIT = 58 * 1024 * 1024
COST_BYTES = 200000
ANYWHERE = pl.BlockSpec(memory_space=pltpu.HBM)
IN_VMEM = pl.BlockSpec(memory_space=pltpu.VMEM)
IN_SMEM = pl.BlockSpec(memory_space=pltpu.SMEM)


def hdot(left, right):
    return jnp.dot(left, right, precision=lax.Precision.HIGHEST, preferred_element_type=jnp.float32)


def limited(left, right):
    return jnp.minimum(jnp.maximum(left, jnp.minimum(right, 0.0)), jnp.maximum(right, 0.0))


def block_at(block):
    return pl.ds(pl.multiple_of(block * LANES, LANES), LANES)


def wide(row):
    return jnp.broadcast_to(row, (SUBLANES, LANES))


def edge_lanes():
    lane = lax.broadcasted_iota(jnp.int32, (SUBLANES, LANES), 1)
    return lane == 0, lane == LANES - 1


def to_left(value):
    return pltpu.roll(value, LANES - 1, 1)


def to_right(value):
    return pltpu.roll(value, 1, 1)


def difference_pass(levels, cell, first_cell, diff, blocks):
    _, last = edge_lanes()
    centre = levels[cell]
    rolled = to_left(centre)
    for b in range(blocks):
        following = levels[cell + (b + 1) % blocks]
        rolled_following = to_left(following)
        diff[first_cell + b] = jnp.where(last, rolled_following, rolled) - centre
        centre, rolled = following, rolled_following


def slope_pass(levels, cell, places, first_cell, diff, slopes, linear, coef, params, blocks):
    first, _ = edge_lanes()
    rolled = to_right(diff[first_cell + blocks - 1])
    for b in range(blocks):
        at = block_at(b)
        d = diff[first_cell + b]
        here = to_right(d)
        d_back = jnp.where(first, rolled, here)
        rolled = here
        slopes[first_cell + b] = limited(d_back, d)
        value = levels[cell + b] + wide(coef[places[2], :, at]) * (d - d_back)
        linear[first_cell + b] = value + params[:, at] * wide(coef[places[3], :, at])


def flux_pass(places, first_cell, diff, slopes, linear, partial, coef, blocks):
    first, last = edge_lanes()

    def parts(b):
        d, slope = diff[first_cell + b], slopes[first_cell + b]
        twice = d + d
        return slope, twice, to_right(twice - slope), to_left(slope)

    before = parts(blocks - 1)
    here = parts(0)
    for b in range(blocks):
        after = parts((b + 1) % blocks)
        speed = wide(coef[places[1], :, block_at(b)])
        forward = jnp.where(first, before[2], here[2])
        backward = here[1] - jnp.where(last, after[3], here[3])
        change = jnp.where(speed > 0.0, forward, backward) + here[0]
        partial[first_cell + b] = linear[first_cell + b] - (0.5 * speed) * change
        before, here = here, after


def rows_pass(levels, cell, places, partial, result, coef, block, blocks):
    at = block_at(block)
    c = [levels[cell + (i - 2) * blocks + block] for i in range(GROUP + 4)]
    d = [c[i + 1] - c[i] for i in range(GROUP + 3)]
    slope = [None] + [limited(d[i - 1], d[i]) for i in range(1, GROUP + 3)]
    twice = [None] + [d[i] + d[i] for i in range(1, GROUP + 2)]
    for i in range(2, GROUP + 2):
        speed = wide(coef[places[i - 2][0], :, at])
        forward = twice[i - 1] - slope[i - 1]
        backward = twice[i] - slope[i + 1]
        change = wide(coef[places[i - 2][2], :, at]) * (d[i] - d[i - 1])
        change = change - (0.5 * speed) * (jnp.where(speed > 0.0, forward, backward) + slope[i])
        here = (i - 2) * blocks + block
        result[here] = partial[here] + change


def advance_group(level, row, levels, work, result, coef, params, blocks):
    diff, slopes, linear, partial = work
    cell = (level * ALL_ROWS + row) * blocks
    places = [[coef_row(array, row + i) for array in range(4)] for i in range(GROUP)]

    def over_rows(one_row):
        @pl.loop(0, GROUP // TOGETHER)
        def _(pair):
            for k in range(TOGETHER):
                i = pair * TOGETHER + k
                one_row([coef_row(array, row + i) for array in range(4)], i * blocks)

    over_rows(lambda _, at: difference_pass(levels, cell + at, at, diff, blocks))
    over_rows(
        lambda where, at: slope_pass(
            levels, cell + at, where, at, diff, slopes, linear, coef, params, blocks
        )
    )
    over_rows(
        lambda where, at: flux_pass(where, at, diff, slopes, linear, partial, coef, blocks)
    )

    @pl.loop(0, blocks // WIDE)
    def _(wide_block):
        for i in range(WIDE):
            rows_pass(levels, cell, places, partial, result, coef, wide_block * WIDE + i, blocks)

    @pl.loop(0, GROUP * blocks // MOVED)
    def _(i):
        first = i * MOVED
        moved = [result[first + k] for k in range(MOVED)]
        for k in range(MOVED):
            levels[cell + ALL_ROWS * blocks + first + k] = moved[k]


class Copies:
    def __init__(self, sems):
        self.sems, self.used = sems, 0

    def make(self, source, target):
        copy = pltpu.make_async_copy(source, target, self.sems.at[self.used])
        self.used += 1
        assert self.used <= self.sems.shape[0]
        return copy

    def start(self, source, target):
        copy = self.make(source, target)
        copy.start()
        return copy


def region(levels, level, row, blocks):
    return levels.at[pl.ds((level * ALL_ROWS + HALO + row) * blocks, GROUP * blocks)]


def fill_rows(blocks, first_rows, tracer, outs, staged, sems):
    def copy(block):
        return pltpu.make_async_copy(tracer.at[:, block_at(block)], staged.at[block], sems.at[block])

    @pl.loop(0, blocks)
    def _(block):
        copy(block).start()

    @pl.loop(0, blocks)
    def _(block):
        copy(block).wait()
        for out, first_row in zip(outs, first_rows):
            for row in range(GROUP):
                out[row * blocks + block] = staged[
                    block, pl.ds(first_row + row, SUBLANES, stride=ROWS), :
                ]


def outer_rows_kernel(
    blocks, tracer, own_coef, place_of, up, down, up_coef, down_coef, staged, sems, coef_sems
):
    copies = Copies(coef_sems)
    source = own_coef.at[place_of[0]]
    waits = [
        copies.start(source.at[pl.ds(ROWS - HALO, HALO)], up_coef),
        copies.start(source.at[pl.ds(0, HALO)], down_coef),
    ]
    fill_rows(blocks, (0, ROWS - GROUP), tracer, (down, up), staged, sems)
    for copy in waits:
        copy.wait()


def inner_rows_kernel(blocks, tracer, outer, low, high, staged, sems):
    fill_rows(blocks, (GROUP, ROWS - 2 * GROUP), tracer, (low, high), staged, sems)


def interior_kernel(blocks, own0, own1, own2, own3, own_coef, params, *rest):
    outs, (levels, *work, result, coef, sems) = rest[:5], rest[5:]
    copies = Copies(sems)
    waits = [
        copies.start(own, region(levels, 0, GROUP * i, blocks))
        for i, own in enumerate((own0, own1, own2, own3))
    ]
    waits += [
        copies.start(own_coef.at[array], coef.at[pl.ds(array * ROWS, ROWS), 0]) for array in range(4)
    ]
    for copy in waits:
        copy.wait()

    @pl.loop(0, 6)
    def _(i):
        level = jnp.where(i < 3, 0, jnp.where(i < 5, 1, 2))
        row = jnp.where(i < 3, 2 + 4 * i, jnp.where(i < 5, 4 * i - 8, 6))
        advance_group(level, row + HALO, levels, work, result, coef, params, blocks)

    waits = [
        copies.start(region(levels, level, row, blocks), out)
        for out, (level, row) in zip(outs, ((1, 2), (1, 10), (2, 4), (2, 8), (3, 6)))
    ]
    for copy in waits:
        copy.wait()


def edge_steps(outer, blocks, waits, sends, levels, work, result, coef, params):
    @pl.loop(0, 2 * STEPS)
    def _(step):
        level, side = lax.div(step, 2), lax.rem(step, 2)
        for k in range(STEPS):
            @pl.when(step == 2 * k)
            def _():
                for copy in waits[k]:
                    copy.wait()

        low = 2 * level - outer
        high = ROWS + outer - GROUP - 2 * level
        row = jnp.where(side == 0, low, high) + HALO
        advance_group(level, row, levels, work, result, coef, params, blocks)
        for k, copy in enumerate(sends):
            pl.when(step == k)(copy.start)


def coef_row(array, row):
    own = array * ROWS + row - HALO
    low = 4 * ROWS + 2 * HALO * array + row
    high = 4 * ROWS + 2 * HALO * array + row - ROWS
    return jnp.where(row < HALO, low, jnp.where(row < HALO + ROWS, own, high))


def load_coef(copies, own_coef, pair, other, place_of, coef):
    waits = [
        copies.start(own_coef.at[array], coef.at[pl.ds(array * ROWS, ROWS), 0]) for array in range(4)
    ]
    for number, source in enumerate((pair.at[0], pair.at[1], other.at[0], other.at[1])):
        array = jnp.bitwise_xor(place_of[0], number)
        for side in range(2):
            first = 4 * ROWS + 2 * HALO * array + HALO * side
            waits.append(copies.start(source.at[side], coef.at[pl.ds(first, HALO), 0]))
    return waits


def middle_kernel(blocks, *refs):
    sources, refs = refs[:9], refs[9:]
    own_coef, pair, other, params, place_of = refs[:5]
    outs, (levels, *work, result, coef, sems) = refs[5:13], refs[13:]
    copies = Copies(sems)
    places = ((0, -4), (0, 0), (0, 12), (0, 16), (1, 2), (1, 10), (2, 4), (2, 8), (3, 6))
    waits = [[] for _ in range(STEPS)]
    for source, (level, row) in zip(sources, places):
        waits[level].append(copies.start(source, region(levels, level, row, blocks)))
    waits[0] += load_coef(copies, own_coef, pair, other, place_of, coef)
    places = [(k + 1, row) for k in range(STEPS) for row in (2 * k - 2, ROWS + 2 - GROUP - 2 * k)]
    sends = [
        copies.make(region(levels, level, row, blocks), out)
        for out, (level, row) in zip(outs, places)
    ]
    edge_steps(2, blocks, waits, sends, levels, work, result, coef, params)
    for copy in sends:
        copy.wait()


def last_kernel(blocks, *refs):
    sources, refs = refs[:12], refs[12:]
    own_coef, pair, other, params, place_of, cell_of, shift_of = refs[:7]
    low_out, high_out, predicted, levels, *work, result, coef, sems = refs[7:]
    copies = Copies(sems)
    places = (
        (0, -8), (0, -4), (0, 16), (0, 20),
        (1, -2), (1, 14), (2, 0), (2, 12), (3, 2), (3, 10), (4, 4), (4, 8),
    )
    waits = [[] for _ in range(STEPS + 1)]
    for source, (level, row) in zip(sources, places):
        waits[level].append(copies.start(source, region(levels, level, row, blocks)))
    waits[0] += load_coef(copies, own_coef, pair, other, place_of, coef)
    edge_steps(6, blocks, waits, (), levels, work, result, coef, params)
    for copy in waits[STEPS]:
        copy.wait()
    sends = [
        copies.start(region(levels, STEPS, row, blocks), out)
        for row, out in ((0, low_out), (ROWS - GROUP, high_out))
    ]
    lane = lax.broadcasted_iota(jnp.int32, (SUBLANES, LANES), 1)

    @pl.loop(0, predicted.shape[1] // LANES)
    def _(block):
        base = block * LANES

        def some(part, found):
            for i in range(PICKED):
                o = part * PICKED + i
                value = pltpu.roll(levels[cell_of[base + o]], shift_of[base + o], 1)
                found = jnp.where(lane == o, value, found)
            return found

        empty = jnp.zeros((SUBLANES, LANES), jnp.float32)
        predicted[:, block_at(block)] = lax.fori_loop(0, LANES // PICKED, some, empty)

    for copy in sends:
        copy.wait()


def field_kernel(blocks, *refs):
    parts, (out, cells, staged, sems, out_sems) = refs[: ROWS // GROUP], refs[ROWS // GROUP :]
    copies = Copies(sems)
    size = GROUP * blocks
    waits = [
        copies.start(part, cells.at[pl.ds(i * size, size)]) for i, part in enumerate(parts)
    ]
    for copy in waits:
        copy.wait()

    def out_copy(block):
        return pltpu.make_async_copy(staged.at[block], out.at[:, block_at(block)], out_sems.at[block])

    @pl.loop(0, blocks)
    def _(block):
        for row in range(ROWS):
            staged[block, pl.ds(row, SUBLANES, stride=ROWS), :] = cells[row * blocks + block]
        out_copy(block).start()

    @pl.loop(0, blocks)
    def _(block):
        out_copy(block).wait()


def scratch(columns, *more):
    blocks = columns // LANES
    group = pltpu.VMEM((GROUP * blocks, SUBLANES, LANES), jnp.float32)
    return [
        pltpu.VMEM(((STEPS + 1) * ALL_ROWS * blocks, SUBLANES, LANES), jnp.float32),
        *[group] * 5,
        pltpu.VMEM((4 * ALL_ROWS, 1, columns), jnp.float32),
        *more,
    ]


def kernel_call(body, name, outs, specs, out_specs, scratches, cost, operands):
    return pl.pallas_call(
        body,
        out_shape=tuple(jax.ShapeDtypeStruct(shape, jnp.float32) for shape in outs),
        in_specs=specs,
        out_specs=out_specs,
        scratch_shapes=scratches,
        compiler_params=pltpu.CompilerParams(vmem_limit_bytes=TALL_LIMIT),
        cost_estimate=pl.CostEstimate(flops=0, bytes_accessed=cost * COST_BYTES, transcendentals=0),
        name=name,
    )(*operands)


def row_groups(tracer, coefficients, place_of):
    members, rows, columns = tracer.shape
    if members != SUBLANES or rows != ROWS:
        raise ValueError("block shape")
    blocks = columns // LANES
    flat = tracer.reshape(members * rows, columns)
    dma = pltpu.SemaphoreType.DMA
    scratches = [pltpu.VMEM((blocks, members * rows, LANES), jnp.float32), dma((blocks,))]
    group, edge = (GROUP * blocks, members, LANES), (HALO, columns)
    up, down, up_coef, down_coef = kernel_call(
        functools.partial(outer_rows_kernel, blocks), "outer_rows",
        [group, group, edge, edge], [ANYWHERE, ANYWHERE, IN_SMEM],
        (IN_VMEM,) * 4,
        scratches + [dma((2,))], 3, [flat, coefficients, place_of],
    )
    low, high = kernel_call(
        functools.partial(inner_rows_kernel, blocks), "inner_rows",
        [group] * 2, [ANYWHERE, ANYWHERE], (IN_VMEM,) * 2,
        scratches, 3, [flat, up],
    )
    return (down, low, high, up), (up_coef, down_coef)


def transport(shape, own, low0, high0, own_coef, pair, other, params, place_of, obs_index, halos):
    members, rows, columns = shape
    blocks = columns // LANES
    group = (GROUP * blocks, members, LANES)
    flat = (members * rows, columns)
    dma = pltpu.SemaphoreType.DMA
    staged = pltpu.VMEM((blocks, members * rows, LANES), jnp.float32)
    gated, pair = lax.optimization_barrier((params, pair))
    inner = kernel_call(
        functools.partial(interior_kernel, blocks), "interior",
        [group] * 5, [ANYWHERE] * 5 + [IN_VMEM], (ANYWHERE,) * 5,
        scratch(columns, dma((16,))), 8, [*own, own_coef, gated],
    )
    upper, lower, low0, high0, *_ = lax.optimization_barrier(
        (own[2], own[1], low0, high0, inner[0])
    )
    low1, high1 = halos(upper, lower)
    first = kernel_call(
        functools.partial(middle_kernel, blocks), "edge_first",
        [group] * 8, [ANYWHERE] * 12 + [IN_VMEM, IN_SMEM], (ANYWHERE,) * 8,
        scratch(columns, dma((29,))), 10,
        [low0, own[0], own[3], high0, *inner, own_coef, pair, other, params, place_of],
    )
    cell_of = obs_index // LANES + (STEPS * ALL_ROWS + HALO) * blocks
    lane_of = obs_index % LANES
    shift_of = (jnp.arange(obs_index.shape[0], dtype=jnp.int32) - lane_of) % LANES
    low4, high4, predicted = kernel_call(
        functools.partial(last_kernel, blocks), "edge_last",
        [group, group, (members, obs_index.shape[0])],
        [ANYWHERE] * 15 + [IN_VMEM] + [IN_SMEM] * 3, (ANYWHERE, ANYWHERE, IN_VMEM),
        scratch(columns, dma((31,))), 15,
        [low1, low0, high0, high1, *first, own_coef, pair, other, params, place_of, cell_of, shift_of],
    )
    (field,) = kernel_call(
        functools.partial(field_kernel, blocks), "field",
        [flat], [ANYWHERE] * 4, (ANYWHERE,),
        [pltpu.VMEM((rows * blocks, members, LANES), jnp.float32), staged, dma((4,)), dma((blocks,))],
        4, [low4, first[6], first[7], high4],
    )
    return field.reshape(shape), predicted, inner[0]


def products_kernel(total_obs, per_group, spread, everyone, own, values, variance, same, out):
    weight = 1.0 / (variance[...] * total_obs)
    innovation = (values[...] - own[...]) * weight
    predicted = everyone[...]
    anomalies = (predicted - hdot(same[...], predicted) / per_group) * spread
    right = jnp.concatenate([anomalies * weight, innovation], axis=0)
    out[...] = lax.dot_general(
        anomalies,
        right,
        (((1,), (1,)), ((), ())),
        precision=lax.Precision.HIGHEST,
        preferred_element_type=jnp.float32,
    )


def update_kernel(per_group, summands, same, own_same, rank_row, rank_col, anomalies, own, out):
    members = same.shape[0]
    total = summands[0]
    for index in range(1, summands.shape[0]):
        total = total + summands[index]
    together = same[...]
    row = lax.broadcasted_iota(jnp.int32, (members, members), 0)
    col = lax.broadcasted_iota(jnp.int32, (members, members), 1)
    system = jnp.where(row == col, 1.0, 0.0) + together * total[:, 0:members]
    right = own_same[...] * total[:, members:]
    for pivot in range(per_group):
        pick = jnp.where(rank_row[...] == pivot, together, 0.0)
        pivot_system = hdot(pick, system)
        pivot_right = hdot(pick, right)
        pivot_value = jnp.sum(pick * pivot_system, axis=1, keepdims=True)
        factor = jnp.sum(pick * system, axis=1, keepdims=True)
        is_pivot = rank_col[...] == pivot
        scale = 1.0 / pivot_value
        scaled_system, scaled_right = pivot_system * scale, pivot_right * scale
        system = jnp.where(is_pivot, scaled_system, system - factor * scaled_system)
        right = jnp.where(is_pivot, scaled_right, right - factor * scaled_right)
    change = lax.dot_general(
        right,
        anomalies[...],
        (((0,), (0,)), ((), ())),
        precision=lax.Precision.HIGHEST,
        preferred_element_type=jnp.float32,
    )
    out[...] = own[...] + change


def local(tracer, coefficients, parameters, obs_index, obs_values, obs_variance, member_group):
    local_members, rows, columns = tracer.shape
    ens_pos = lax.axis_index("ens")
    ens_count = lax.axis_size("ens")
    slab_count = lax.axis_size("slab")
    if ens_count != 4 or coefficients.shape[0] != 4 or slab_count & (slab_count - 1):
        raise ValueError("mesh shape")
    forward = [(i, i + 1) for i in range(slab_count - 1)]
    backward = [(target, source) for source, target in forward]

    def over_ens(mine):
        pair = jnp.stack([mine, lax.ppermute(mine, "ens", [(i, i ^ 1) for i in range(ens_count)])])
        return pair, lax.ppermute(pair, "ens", [(i, i ^ 2) for i in range(ens_count)])

    def halos(upper, lower):
        return lax.ppermute(upper, "slab", forward), lax.ppermute(lower, "slab", backward)

    place_of = jnp.reshape(ens_pos, (1,))
    own, coef_edges = row_groups(tracer, coefficients, place_of)
    low0, high0 = halos(own[3], own[0])

    edge_low, edge_high = halos(*coef_edges)
    pair, other = over_ens(jnp.stack([edge_low, edge_high]))

    members = member_group.shape[0]
    per_group = members // GROUPS
    spread = 1.0 / math.sqrt(per_group - 1)
    same_bool = member_group[:, None] == member_group[None, :]
    same = same_bool.astype(jnp.float32)
    earlier = jnp.arange(members)[None, :] < jnp.arange(members)[:, None]
    rank = jnp.sum((same_bool & earlier).astype(jnp.int32), axis=1)
    own_same = lax.dynamic_slice_in_dim(same, ens_pos * local_members, local_members, 1)
    field, predicted, first_done = transport(
        tracer.shape, own, low0, high0,
        coefficients, pair, other, parameters, place_of, obs_index, halos,
    )

    later, _ = lax.optimization_barrier((parameters, first_done))
    shared = jnp.concatenate(over_ens(later), axis=0)
    all_params = jnp.concatenate(
        [lax.dynamic_index_in_dim(shared, ens_pos ^ i, 0, False) for i in range(ens_count)], axis=0
    )
    param_anomalies = (all_params - hdot(same, all_params) / per_group) * spread
    everyone = lax.all_gather(predicted, "ens", axis=0, tiled=True)
    total_obs = obs_variance.shape[0] * slab_count
    products = pl.pallas_call(
        functools.partial(products_kernel, float(total_obs), per_group, spread),
        out_shape=jax.ShapeDtypeStruct((members, members + local_members), jnp.float32),
        compiler_params=pltpu.CompilerParams(vmem_limit_bytes=VMEM_LIMIT),
        name="products",
    )(everyone, predicted, obs_values, obs_variance[None, :], same)
    distance = 1
    while distance < slab_count:
        pairs = [(i, i ^ distance) for i in range(slab_count)]
        products = products + lax.ppermute(products, "slab", pairs)
        distance *= 2
    updated = pl.pallas_call(
        functools.partial(update_kernel, per_group),
        out_shape=jax.ShapeDtypeStruct(parameters.shape, jnp.float32),
        compiler_params=pltpu.CompilerParams(vmem_limit_bytes=VMEM_LIMIT),
        name="update",
    )(products[None], same, own_same, rank[None, :], rank[:, None], param_anomalies, parameters)
    return (field, updated)


def solution(mesh):
    in_specs = (
        P("ens", "slab", None),
        P(None, "slab", None),
        P("ens", None),
        P("slab"),
        P("ens", "slab"),
        P("slab"),
        P(),
    )
    out_specs = (P("ens", "slab", None), P("ens", None))
    return jax.shard_map(local, mesh=mesh, in_specs=in_specs, out_specs=out_specs, check_vma=False)
```

```python
import functools
import math

import jax
import jax.numpy as jnp
from jax import lax
from jax.experimental import pallas as pl
from jax.experimental.pallas import tpu as pltpu
from jax.sharding import PartitionSpec as P

STEPS = 4
GROUPS = 8
HALO = 2 * STEPS
LANES = 128
SUBLANES = 8
ROWS = 16
GROUP = 4
WIDE = 4
TOGETHER = 2
MOVED = 16
PICKED = 128
ALL_ROWS = ROWS + 2 * HALO
VMEM_LIMIT = 16 * 1024 * 1024
TALL_LIMIT = 58 * 1024 * 1024
COST_BYTES = 200000
ANYWHERE = pl.BlockSpec(memory_space=pltpu.HBM)
IN_VMEM = pl.BlockSpec(memory_space=pltpu.VMEM)
IN_SMEM = pl.BlockSpec(memory_space=pltpu.SMEM)


def hdot(left, right):
    return jnp.dot(left, right, precision=lax.Precision.HIGHEST, preferred_element_type=jnp.float32)


def limited(left, right):
    return jnp.minimum(jnp.maximum(left, jnp.minimum(right, 0.0)), jnp.maximum(right, 0.0))


def block_at(block):
    return pl.ds(pl.multiple_of(block * LANES, LANES), LANES)


def everywhere(coef, block, place):
    return coef[block, pl.ds(place, SUBLANES, stride=0), :]


def edge_lanes():
    lane = lax.broadcasted_iota(jnp.int32, (SUBLANES, LANES), 1)
    return lane == 0, lane == LANES - 1


def to_left(value):
    return pltpu.roll(value, LANES - 1, 1)


def to_right(value):
    return pltpu.roll(value, 1, 1)


def difference_pass(levels, cell, first_cell, diff, blocks):
    _, last = edge_lanes()
    centre = levels[cell]
    rolled = to_left(centre)
    for b in range(blocks):
        following = levels[cell + (b + 1) % blocks]
        rolled_following = to_left(following)
        diff[first_cell + b] = jnp.where(last, rolled_following, rolled) - centre
        centre, rolled = following, rolled_following


def slope_pass(levels, cell, places, first_cell, diff, slopes, linear, coef, params, blocks):
    first, _ = edge_lanes()
    rolled = to_right(diff[first_cell + blocks - 1])
    for b in range(blocks):
        at = block_at(b)
        d = diff[first_cell + b]
        here = to_right(d)
        d_back = jnp.where(first, rolled, here)
        rolled = here
        slopes[first_cell + b] = limited(d_back, d)
        value = levels[cell + b] + everywhere(coef, b, places[2]) * (d - d_back)
        linear[first_cell + b] = value + params[:, at] * everywhere(coef, b, places[3])


def flux_pass(places, first_cell, diff, slopes, linear, partial, coef, blocks):
    first, last = edge_lanes()

    def parts(b):
        d, slope = diff[first_cell + b], slopes[first_cell + b]
        twice = d + d
        return slope, twice, to_right(twice - slope), to_left(slope)

    before = parts(blocks - 1)
    here = parts(0)
    for b in range(blocks):
        after = parts((b + 1) % blocks)
        speed = everywhere(coef, b, places[1])
        forward = jnp.where(first, before[2], here[2])
        backward = here[1] - jnp.where(last, after[3], here[3])
        change = jnp.where(speed > 0.0, forward, backward) + here[0]
        partial[first_cell + b] = linear[first_cell + b] - (0.5 * speed) * change
        before, here = here, after


def rows_pass(levels, cell, places, partial, result, coef, block, blocks):
    c = [levels[cell + (i - 2) * blocks + block] for i in range(GROUP + 4)]
    d = [c[i + 1] - c[i] for i in range(GROUP + 3)]
    slope = [None] + [limited(d[i - 1], d[i]) for i in range(1, GROUP + 3)]
    twice = [None] + [d[i] + d[i] for i in range(1, GROUP + 2)]
    for i in range(2, GROUP + 2):
        speed = everywhere(coef, block, places[i - 2][0])
        forward = twice[i - 1] - slope[i - 1]
        backward = twice[i] - slope[i + 1]
        change = everywhere(coef, block, places[i - 2][2]) * (d[i] - d[i - 1])
        change = change - (0.5 * speed) * (jnp.where(speed > 0.0, forward, backward) + slope[i])
        here = (i - 2) * blocks + block
        result[here] = partial[here] + change


def advance_group(level, row, levels, work, result, coef, params, blocks):
    diff, slopes, linear, partial = work
    cell = (level * ALL_ROWS + row) * blocks
    places = [[coef_row(array, row + i) for array in range(4)] for i in range(GROUP)]

    def over_rows(one_row):
        @pl.loop(0, GROUP // TOGETHER)
        def _(pair):
            for k in range(TOGETHER):
                i = pair * TOGETHER + k
                one_row([coef_row(array, row + i) for array in range(4)], i * blocks)

    over_rows(lambda _, at: difference_pass(levels, cell + at, at, diff, blocks))
    over_rows(
        lambda where, at: slope_pass(
            levels, cell + at, where, at, diff, slopes, linear, coef, params, blocks
        )
    )
    over_rows(
        lambda where, at: flux_pass(where, at, diff, slopes, linear, partial, coef, blocks)
    )

    @pl.loop(0, blocks // WIDE)
    def _(wide_block):
        for i in range(WIDE):
            rows_pass(levels, cell, places, partial, result, coef, wide_block * WIDE + i, blocks)

    @pl.loop(0, GROUP * blocks // MOVED)
    def _(i):
        first = i * MOVED
        moved = [result[first + k] for k in range(MOVED)]
        for k in range(MOVED):
            levels[cell + ALL_ROWS * blocks + first + k] = moved[k]


class Copies:
    def __init__(self, sems):
        self.sems, self.used = sems, 0

    def make(self, source, target):
        copy = pltpu.make_async_copy(source, target, self.sems.at[self.used])
        self.used += 1
        assert self.used <= self.sems.shape[0]
        return copy

    def start(self, source, target):
        copy = self.make(source, target)
        copy.start()
        return copy


def region(levels, level, row, blocks):
    return levels.at[pl.ds((level * ALL_ROWS + HALO + row) * blocks, GROUP * blocks)]


def fill_rows(blocks, first_rows, tracer, outs, staged, sems):
    def copy(block):
        return pltpu.make_async_copy(tracer.at[:, block_at(block)], staged.at[block], sems.at[block])

    @pl.loop(0, blocks)
    def _(block):
        copy(block).start()

    @pl.loop(0, blocks)
    def _(block):
        copy(block).wait()
        for out, first_row in zip(outs, first_rows):
            for row in range(GROUP):
                out[row * blocks + block] = staged[
                    block, pl.ds(first_row + row, SUBLANES, stride=ROWS), :
                ]


def outer_rows_kernel(
    blocks, tracer, own_coef, place_of, up, down, up_coef, down_coef, edge, edge_sem, staged, sems
):
    copy = pltpu.make_async_copy(own_coef.at[place_of[0]], edge, edge_sem)
    copy.start()
    fill_rows(blocks, (0, ROWS - GROUP), tracer, (down, up), staged, sems)
    copy.wait()
    for block in range(blocks):
        at = block_at(block)
        up_coef[block] = edge[ROWS - HALO :, at]
        down_coef[block] = edge[0:HALO, at]


def inner_rows_kernel(
    blocks, tracer, own_coef, outer, low, high, by_block, whole, coef_sem, staged, sems
):
    copy = pltpu.make_async_copy(own_coef, whole, coef_sem)
    copy.start()
    fill_rows(blocks, (GROUP, ROWS - 2 * GROUP), tracer, (low, high), staged, sems)
    copy.wait()

    @pl.loop(0, blocks)
    def _(block):
        for array in range(4):
            by_block[block, array * ROWS : (array + 1) * ROWS, :] = whole[array, :, block_at(block)]


def interior_kernel(blocks, own0, own1, own2, own3, own_coef, params, *rest):
    outs, (levels, *work, result, coef, sems) = rest[:5], rest[5:]
    copies = Copies(sems)
    waits = [
        copies.start(own, region(levels, 0, GROUP * i, blocks))
        for i, own in enumerate((own0, own1, own2, own3))
    ]
    waits.append(copies.start(own_coef, coef.at[:, 0 : 4 * ROWS]))
    for copy in waits:
        copy.wait()

    @pl.loop(0, 6)
    def _(i):
        level = jnp.where(i < 3, 0, jnp.where(i < 5, 1, 2))
        row = jnp.where(i < 3, 2 + 4 * i, jnp.where(i < 5, 4 * i - 8, 6))
        advance_group(level, row + HALO, levels, work, result, coef, params, blocks)

    waits = [
        copies.start(region(levels, level, row, blocks), out)
        for out, (level, row) in zip(outs, ((1, 2), (1, 10), (2, 4), (2, 8), (3, 6)))
    ]
    for copy in waits:
        copy.wait()


def edge_steps(outer, blocks, waits, sends, levels, work, result, coef, params):
    @pl.loop(0, 2 * STEPS)
    def _(step):
        level, side = lax.div(step, 2), lax.rem(step, 2)
        for k in range(STEPS):
            @pl.when(step == 2 * k)
            def _():
                for copy in waits[k]:
                    copy.wait()

        low = 2 * level - outer
        high = ROWS + outer - GROUP - 2 * level
        row = jnp.where(side == 0, low, high) + HALO
        advance_group(level, row, levels, work, result, coef, params, blocks)
        for k, copy in enumerate(sends):
            pl.when(step == k)(copy.start)


def coef_row(array, row):
    own = array * ROWS + row - HALO
    low = 4 * ROWS + 2 * HALO * array + row
    high = 4 * ROWS + 2 * HALO * array + row - ROWS
    return jnp.where(row < HALO, low, jnp.where(row < HALO + ROWS, own, high))


def load_coef(copies, own_coef, pair, other, place_of, coef):
    waits = [copies.start(own_coef, coef.at[:, 0 : 4 * ROWS])]
    for number, source in enumerate((pair.at[0], pair.at[1], other.at[0], other.at[1])):
        array = jnp.bitwise_xor(place_of[0], number)
        for side in range(2):
            first = 4 * ROWS + 2 * HALO * array + HALO * side
            waits.append(copies.start(source.at[side], coef.at[:, pl.ds(first, HALO)]))
    return waits


def middle_kernel(blocks, *refs):
    sources, refs = refs[:9], refs[9:]
    own_coef, pair, other, params, place_of = refs[:5]
    outs, (levels, *work, result, coef, sems) = refs[5:13], refs[13:]
    copies = Copies(sems)
    places = ((0, -4), (0, 0), (0, 12), (0, 16), (1, 2), (1, 10), (2, 4), (2, 8), (3, 6))
    waits = [[] for _ in range(STEPS)]
    for source, (level, row) in zip(sources, places):
        waits[level].append(copies.start(source, region(levels, level, row, blocks)))
    waits[0] += load_coef(copies, own_coef, pair, other, place_of, coef)
    places = [(k + 1, row) for k in range(STEPS) for row in (2 * k - 2, ROWS + 2 - GROUP - 2 * k)]
    sends = [
        copies.make(region(levels, level, row, blocks), out)
        for out, (level, row) in zip(outs, places)
    ]
    edge_steps(2, blocks, waits, sends, levels, work, result, coef, params)
    for copy in sends:
        copy.wait()


def last_kernel(blocks, *refs):
    sources, refs = refs[:12], refs[12:]
    own_coef, pair, other, params, place_of, cell_of, shift_of = refs[:7]
    low_out, high_out, predicted, levels, *work, result, coef, sems = refs[7:]
    copies = Copies(sems)
    places = (
        (0, -8), (0, -4), (0, 16), (0, 20),
        (1, -2), (1, 14), (2, 0), (2, 12), (3, 2), (3, 10), (4, 4), (4, 8),
    )
    waits = [[] for _ in range(STEPS + 1)]
    for source, (level, row) in zip(sources, places):
        waits[level].append(copies.start(source, region(levels, level, row, blocks)))
    waits[0] += load_coef(copies, own_coef, pair, other, place_of, coef)
    edge_steps(6, blocks, waits, (), levels, work, result, coef, params)
    for copy in waits[STEPS]:
        copy.wait()
    sends = [
        copies.start(region(levels, STEPS, row, blocks), out)
        for row, out in ((0, low_out), (ROWS - GROUP, high_out))
    ]
    lane = lax.broadcasted_iota(jnp.int32, (SUBLANES, LANES), 1)

    @pl.loop(0, predicted.shape[1] // LANES)
    def _(block):
        base = block * LANES

        def some(part, found):
            for i in range(PICKED):
                o = part * PICKED + i
                value = pltpu.roll(levels[cell_of[base + o]], shift_of[base + o], 1)
                found = jnp.where(lane == o, value, found)
            return found

        empty = jnp.zeros((SUBLANES, LANES), jnp.float32)
        predicted[:, block_at(block)] = lax.fori_loop(0, LANES // PICKED, some, empty)

    for copy in sends:
        copy.wait()


def field_kernel(blocks, *refs):
    parts, (out, cells, staged, sems, out_sems) = refs[: ROWS // GROUP], refs[ROWS // GROUP :]
    copies = Copies(sems)
    size = GROUP * blocks
    waits = [
        copies.start(part, cells.at[pl.ds(i * size, size)]) for i, part in enumerate(parts)
    ]
    for copy in waits:
        copy.wait()

    def out_copy(block):
        return pltpu.make_async_copy(staged.at[block], out.at[:, block_at(block)], out_sems.at[block])

    @pl.loop(0, blocks)
    def _(block):
        for row in range(ROWS):
            staged[block, pl.ds(row, SUBLANES, stride=ROWS), :] = cells[row * blocks + block]
        out_copy(block).start()

    @pl.loop(0, blocks)
    def _(block):
        out_copy(block).wait()


def scratch(columns, *more):
    blocks = columns // LANES
    group = pltpu.VMEM((GROUP * blocks, SUBLANES, LANES), jnp.float32)
    return [
        pltpu.VMEM(((STEPS + 1) * ALL_ROWS * blocks, SUBLANES, LANES), jnp.float32),
        *[group] * 5,
        pltpu.VMEM((blocks, 4 * ALL_ROWS, LANES), jnp.float32),
        *more,
    ]


def kernel_call(body, name, outs, specs, out_specs, scratches, cost, operands):
    return pl.pallas_call(
        body,
        out_shape=tuple(jax.ShapeDtypeStruct(shape, jnp.float32) for shape in outs),
        in_specs=specs,
        out_specs=out_specs,
        scratch_shapes=scratches,
        compiler_params=pltpu.CompilerParams(vmem_limit_bytes=TALL_LIMIT),
        cost_estimate=pl.CostEstimate(flops=0, bytes_accessed=cost * COST_BYTES, transcendentals=0),
        name=name,
    )(*operands)


def row_groups(tracer, coefficients, place_of):
    members, rows, columns = tracer.shape
    if members != SUBLANES or rows != ROWS:
        raise ValueError("block shape")
    blocks = columns // LANES
    flat = tracer.reshape(members * rows, columns)
    dma = pltpu.SemaphoreType.DMA
    scratches = [pltpu.VMEM((blocks, members * rows, LANES), jnp.float32), dma((blocks,))]
    group, edge = (GROUP * blocks, members, LANES), (blocks, HALO, LANES)
    up, down, up_coef, down_coef = kernel_call(
        functools.partial(outer_rows_kernel, blocks), "outer_rows",
        [group, group, edge, edge], [ANYWHERE, ANYWHERE, IN_SMEM], (IN_VMEM,) * 4,
        [pltpu.VMEM((rows, columns), jnp.float32), dma] + scratches, 3,
        [flat, coefficients, place_of],
    )
    low, high, by_block = kernel_call(
        functools.partial(inner_rows_kernel, blocks), "inner_rows",
        [group, group, (blocks, 4 * rows, LANES)], [ANYWHERE] * 3, (IN_VMEM,) * 3,
        [pltpu.VMEM((4, rows, columns), jnp.float32), dma] + scratches, 3,
        [flat, coefficients, up],
    )
    return (down, low, high, up), (up_coef, down_coef), by_block


def transport(shape, own, low0, high0, own_coef, pair, other, params, place_of, obs_index, halos):
    members, rows, columns = shape
    blocks = columns // LANES
    group = (GROUP * blocks, members, LANES)
    flat = (members * rows, columns)
    dma = pltpu.SemaphoreType.DMA
    staged = pltpu.VMEM((blocks, members * rows, LANES), jnp.float32)
    gated, pair = lax.optimization_barrier((params, pair))
    inner = kernel_call(
        functools.partial(interior_kernel, blocks), "interior",
        [group] * 5, [ANYWHERE] * 5 + [IN_VMEM], (ANYWHERE,) * 5,
        scratch(columns, dma((16,))), 8, [*own, own_coef, gated],
    )
    upper, lower, low0, high0, *_ = lax.optimization_barrier(
        (own[2], own[1], low0, high0, inner[0])
    )
    low1, high1 = halos(upper, lower)
    first = kernel_call(
        functools.partial(middle_kernel, blocks), "edge_first",
        [group] * 8, [ANYWHERE] * 12 + [IN_VMEM, IN_SMEM], (ANYWHERE,) * 8,
        scratch(columns, dma((29,))), 10,
        [low0, own[0], own[3], high0, *inner, own_coef, pair, other, params, place_of],
    )
    cell_of = obs_index // LANES + (STEPS * ALL_ROWS + HALO) * blocks
    lane_of = obs_index % LANES
    shift_of = (jnp.arange(obs_index.shape[0], dtype=jnp.int32) - lane_of) % LANES
    low4, high4, predicted = kernel_call(
        functools.partial(last_kernel, blocks), "edge_last",
        [group, group, (members, obs_index.shape[0])],
        [ANYWHERE] * 15 + [IN_VMEM] + [IN_SMEM] * 3, (ANYWHERE, ANYWHERE, IN_VMEM),
        scratch(columns, dma((31,))), 15,
        [low1, low0, high0, high1, *first, own_coef, pair, other, params, place_of, cell_of, shift_of],
    )
    (field,) = kernel_call(
        functools.partial(field_kernel, blocks), "field",
        [flat], [ANYWHERE] * 4, (ANYWHERE,),
        [pltpu.VMEM((rows * blocks, members, LANES), jnp.float32), staged, dma((4,)), dma((blocks,))],
        4, [low4, first[6], first[7], high4],
    )
    return field.reshape(shape), predicted, inner[0]


def products_kernel(total_obs, per_group, spread, everyone, own, values, variance, same, out):
    weight = 1.0 / (variance[...] * total_obs)
    innovation = (values[...] - own[...]) * weight
    predicted = everyone[...]
    anomalies = (predicted - hdot(same[...], predicted) / per_group) * spread
    right = jnp.concatenate([anomalies * weight, innovation], axis=0)
    out[...] = lax.dot_general(
        anomalies,
        right,
        (((1,), (1,)), ((), ())),
        precision=lax.Precision.HIGHEST,
        preferred_element_type=jnp.float32,
    )


def update_kernel(per_group, summands, same, own_same, rank_row, rank_col, anomalies, own, out):
    members = same.shape[0]
    total = summands[0]
    for index in range(1, summands.shape[0]):
        total = total + summands[index]
    together = same[...]
    row = lax.broadcasted_iota(jnp.int32, (members, members), 0)
    col = lax.broadcasted_iota(jnp.int32, (members, members), 1)
    system = jnp.where(row == col, 1.0, 0.0) + together * total[:, 0:members]
    right = own_same[...] * total[:, members:]
    for pivot in range(per_group):
        pick = jnp.where(rank_row[...] == pivot, together, 0.0)
        pivot_system = hdot(pick, system)
        pivot_right = hdot(pick, right)
        pivot_value = jnp.sum(pick * pivot_system, axis=1, keepdims=True)
        factor = jnp.sum(pick * system, axis=1, keepdims=True)
        is_pivot = rank_col[...] == pivot
        scale = 1.0 / pivot_value
        scaled_system, scaled_right = pivot_system * scale, pivot_right * scale
        system = jnp.where(is_pivot, scaled_system, system - factor * scaled_system)
        right = jnp.where(is_pivot, scaled_right, right - factor * scaled_right)
    change = lax.dot_general(
        right,
        anomalies[...],
        (((0,), (0,)), ((), ())),
        precision=lax.Precision.HIGHEST,
        preferred_element_type=jnp.float32,
    )
    out[...] = own[...] + change


def local(tracer, coefficients, parameters, obs_index, obs_values, obs_variance, member_group):
    local_members, rows, columns = tracer.shape
    ens_pos = lax.axis_index("ens")
    ens_count = lax.axis_size("ens")
    slab_count = lax.axis_size("slab")
    if ens_count != 4 or coefficients.shape[0] != 4 or slab_count & (slab_count - 1):
        raise ValueError("mesh shape")
    forward = [(i, i + 1) for i in range(slab_count - 1)]
    backward = [(target, source) for source, target in forward]

    def over_ens(mine):
        pair = jnp.stack([mine, lax.ppermute(mine, "ens", [(i, i ^ 1) for i in range(ens_count)])])
        return pair, lax.ppermute(pair, "ens", [(i, i ^ 2) for i in range(ens_count)])

    def halos(upper, lower):
        return lax.ppermute(upper, "slab", forward), lax.ppermute(lower, "slab", backward)

    place_of = jnp.reshape(ens_pos, (1,))
    own, coef_edges, own_coef = row_groups(tracer, coefficients, place_of)
    low0, high0 = halos(own[3], own[0])

    edge_low, edge_high = halos(*coef_edges)
    pair, other = over_ens(jnp.stack([edge_low, edge_high]))

    members = member_group.shape[0]
    per_group = members // GROUPS
    spread = 1.0 / math.sqrt(per_group - 1)
    same_bool = member_group[:, None] == member_group[None, :]
    same = same_bool.astype(jnp.float32)
    earlier = jnp.arange(members)[None, :] < jnp.arange(members)[:, None]
    rank = jnp.sum((same_bool & earlier).astype(jnp.int32), axis=1)
    own_same = lax.dynamic_slice_in_dim(same, ens_pos * local_members, local_members, 1)
    field, predicted, first_done = transport(
        tracer.shape, own, low0, high0,
        own_coef, pair, other, parameters, place_of, obs_index, halos,
    )

    later, _ = lax.optimization_barrier((parameters, first_done))
    shared = jnp.concatenate(over_ens(later), axis=0)
    all_params = jnp.concatenate(
        [lax.dynamic_index_in_dim(shared, ens_pos ^ i, 0, False) for i in range(ens_count)], axis=0
    )
    param_anomalies = (all_params - hdot(same, all_params) / per_group) * spread
    everyone = lax.all_gather(predicted, "ens", axis=0, tiled=True)
    total_obs = obs_variance.shape[0] * slab_count
    products = pl.pallas_call(
        functools.partial(products_kernel, float(total_obs), per_group, spread),
        out_shape=jax.ShapeDtypeStruct((members, members + local_members), jnp.float32),
        compiler_params=pltpu.CompilerParams(vmem_limit_bytes=VMEM_LIMIT),
        name="products",
    )(everyone, predicted, obs_values, obs_variance[None, :], same)
    distance = 1
    while distance < slab_count:
        pairs = [(i, i ^ distance) for i in range(slab_count)]
        products = products + lax.ppermute(products, "slab", pairs)
        distance *= 2
    updated = pl.pallas_call(
        functools.partial(update_kernel, per_group),
        out_shape=jax.ShapeDtypeStruct(parameters.shape, jnp.float32),
        compiler_params=pltpu.CompilerParams(vmem_limit_bytes=VMEM_LIMIT),
        name="update",
    )(products[None], same, own_same, rank[None, :], rank[:, None], param_anomalies, parameters)
    return (field, updated)


def solution(mesh):
    in_specs = (
        P("ens", "slab", None),
        P(None, "slab", None),
        P("ens", None),
        P("slab"),
        P("ens", "slab"),
        P("slab"),
        P(),
    )
    out_specs = (P("ens", "slab", None), P("ens", None))
    return jax.shard_map(local, mesh=mesh, in_specs=in_specs, out_specs=out_specs, check_vma=False)
```

```python
import functools
import math

import jax
import jax.numpy as jnp
from jax import lax
from jax.experimental import pallas as pl
from jax.experimental.pallas import tpu as pltpu
from jax.sharding import PartitionSpec as P

STEPS = 4
GROUPS = 8
HALO = 2 * STEPS
LANES = 128
SUBLANES = 8
ROWS = 16
GROUP = 4
WIDE = 4
TOGETHER = 2
MOVED = 16
FOLD = 4
PICKED = 128
ALL_ROWS = ROWS + 2 * HALO
VMEM_LIMIT = 16 * 1024 * 1024
TALL_LIMIT = 58 * 1024 * 1024
COST_BYTES = 200000
ANYWHERE = pl.BlockSpec(memory_space=pltpu.HBM)
IN_VMEM = pl.BlockSpec(memory_space=pltpu.VMEM)
IN_SMEM = pl.BlockSpec(memory_space=pltpu.SMEM)


def hdot(left, right):
    return jnp.dot(left, right, precision=lax.Precision.HIGHEST, preferred_element_type=jnp.float32)


def limited(left, right):
    return jnp.minimum(jnp.maximum(left, jnp.minimum(right, 0.0)), jnp.maximum(right, 0.0))


def block_at(block):
    return pl.ds(pl.multiple_of(block * LANES, LANES), LANES)


def everywhere(coef, block, place):
    return coef[block, pl.ds(place, SUBLANES, stride=0), :]


def edge_lanes():
    lane = lax.broadcasted_iota(jnp.int32, (SUBLANES, LANES), 1)
    return lane == 0, lane == LANES - 1


def dealt(values, back=False):
    shape = (FOLD * LANES, FOLD * LANES)
    natural = lax.broadcasted_iota(jnp.int32, shape, 1 if back else 0)
    place = lax.broadcasted_iota(jnp.int32, shape, 0 if back else 1)
    moves = natural == FOLD * lax.rem(place, LANES) + lax.div(place, LANES)
    moves = jnp.where(moves, 1.0, 0.0).astype(jnp.bfloat16)
    products = []
    for _ in range(3):
        piece = values.astype(jnp.bfloat16)
        products.append(jnp.dot(piece, moves, preferred_element_type=jnp.float32))
        values = values - piece.astype(jnp.float32)
    return products[0] + (products[1] + products[2])


class Neighbours:
    def __init__(self, get, blocks):
        self.get, self.blocks, self.rolled = get, blocks, {}
        self.first, self.last = edge_lanes()

    def turned(self, b, shift):
        b %= self.blocks
        if (b, shift) not in self.rolled:
            self.rolled[b, shift] = pltpu.roll(self.get(b), shift, 1)
        return self.rolled[b, shift]

    def following(self, b):
        if b % FOLD < FOLD - 1:
            return self.get(b + 1)
        start = b - (FOLD - 1)
        return jnp.where(
            self.last, self.turned(start + FOLD, LANES - 1), self.turned(start, LANES - 1)
        )

    def preceding(self, b):
        if b % FOLD > 0:
            return self.get(b - 1)
        end = b + FOLD - 1
        return jnp.where(self.first, self.turned(end - FOLD, 1), self.turned(end, 1))


def difference_pass(levels, cell, first_cell, diff, blocks):
    centre = Neighbours(lambda b: levels[cell + b], blocks)
    for b in range(blocks):
        diff[first_cell + b] = centre.following(b) - centre.get(b)


def slope_pass(levels, cell, places, first_cell, diff, slopes, linear, coef, params, blocks):
    differences = Neighbours(lambda b: diff[first_cell + b], blocks)
    for b in range(blocks):
        at = block_at(b)
        d, d_back = differences.get(b), differences.preceding(b)
        slopes[first_cell + b] = limited(d_back, d)
        value = levels[cell + b] + everywhere(coef, b, places[2]) * (d - d_back)
        linear[first_cell + b] = value + params[:, at] * everywhere(coef, b, places[3])


def flux_pass(places, first_cell, diff, slopes, linear, partial, coef, blocks):
    def left_part(b):
        d = diff[first_cell + b]
        return d + d - slopes[first_cell + b]

    left = Neighbours(left_part, blocks)
    slope = Neighbours(lambda b: slopes[first_cell + b], blocks)
    for b in range(blocks):
        speed = everywhere(coef, b, places[1])
        d = diff[first_cell + b]
        backward = d + d - slope.following(b)
        change = jnp.where(speed > 0.0, left.preceding(b), backward) + slope.get(b)
        partial[first_cell + b] = linear[first_cell + b] - (0.5 * speed) * change


def rows_pass(levels, cell, places, partial, result, coef, block, blocks):
    c = [levels[cell + (i - 2) * blocks + block] for i in range(GROUP + 4)]
    d = [c[i + 1] - c[i] for i in range(GROUP + 3)]
    slope = [None] + [limited(d[i - 1], d[i]) for i in range(1, GROUP + 3)]
    twice = [None] + [d[i] + d[i] for i in range(1, GROUP + 2)]
    for i in range(2, GROUP + 2):
        speed = everywhere(coef, block, places[i - 2][0])
        forward = twice[i - 1] - slope[i - 1]
        backward = twice[i] - slope[i + 1]
        change = everywhere(coef, block, places[i - 2][2]) * (d[i] - d[i - 1])
        change = change - (0.5 * speed) * (jnp.where(speed > 0.0, forward, backward) + slope[i])
        here = (i - 2) * blocks + block
        result[here] = partial[here] + change


def advance_group(level, row, levels, work, result, coef, params, blocks):
    diff, slopes, linear, partial = work
    cell = (level * ALL_ROWS + row) * blocks
    places = [[coef_row(array, row + i) for array in range(4)] for i in range(GROUP)]

    def over_rows(one_row):
        @pl.loop(0, GROUP // TOGETHER)
        def _(pair):
            for k in range(TOGETHER):
                i = pair * TOGETHER + k
                one_row([coef_row(array, row + i) for array in range(4)], i * blocks)

    over_rows(lambda _, at: difference_pass(levels, cell + at, at, diff, blocks))
    over_rows(
        lambda where, at: slope_pass(
            levels, cell + at, where, at, diff, slopes, linear, coef, params, blocks
        )
    )
    over_rows(
        lambda where, at: flux_pass(where, at, diff, slopes, linear, partial, coef, blocks)
    )

    @pl.loop(0, blocks // WIDE)
    def _(wide_block):
        for i in range(WIDE):
            rows_pass(levels, cell, places, partial, result, coef, wide_block * WIDE + i, blocks)

    @pl.loop(0, GROUP * blocks // MOVED)
    def _(i):
        first = i * MOVED
        moved = [result[first + k] for k in range(MOVED)]
        for k in range(MOVED):
            levels[cell + ALL_ROWS * blocks + first + k] = moved[k]


class Copies:
    def __init__(self, sems):
        self.sems, self.used = sems, 0

    def make(self, source, target):
        copy = pltpu.make_async_copy(source, target, self.sems.at[self.used])
        self.used += 1
        assert self.used <= self.sems.shape[0]
        return copy

    def start(self, source, target):
        copy = self.make(source, target)
        copy.start()
        return copy


def region(levels, level, row, blocks):
    return levels.at[pl.ds((level * ALL_ROWS + HALO + row) * blocks, GROUP * blocks)]


def fill_rows(blocks, first_rows, tracer, mixed, staged, sems):
    def copy(block):
        return pltpu.make_async_copy(tracer.at[:, block_at(block)], staged.at[block], sems.at[block])

    @pl.loop(0, blocks)
    def _(block):
        copy(block).start()

    lines = len(first_rows) * GROUP * SUBLANES

    @pl.loop(0, blocks // FOLD)
    def _(part):
        for q in range(FOLD):
            block = part * FOLD + q
            copy(block).wait()
            for k, first_row in enumerate(first_rows):
                for row in range(GROUP):
                    line = part * lines + (k * GROUP + row) * SUBLANES
                    mixed[pl.ds(pl.multiple_of(line, SUBLANES), SUBLANES), block_at(q)] = staged[
                        block, pl.ds(first_row + row, SUBLANES, stride=ROWS), :
                    ]


def take_rows(blocks, mixed, outs):
    lines = len(outs) * GROUP * SUBLANES

    @pl.loop(0, blocks // FOLD)
    def _(part):
        for k, out in enumerate(outs):
            for row in range(GROUP):
                line = part * lines + (k * GROUP + row) * SUBLANES
                for p in range(FOLD):
                    out[row * blocks + part * FOLD + p] = mixed[
                        pl.ds(pl.multiple_of(line, SUBLANES), SUBLANES), block_at(p)
                    ]


def outer_rows_kernel(
    blocks, tracer, own_coef, place_of, up, down, up_coef, down_coef, edge, edge_sem, mixed, staged, sems
):
    copy = pltpu.make_async_copy(own_coef.at[place_of[0]], edge, edge_sem)
    copy.start()
    fill_rows(blocks, (0, ROWS - GROUP), tracer, mixed, staged, sems)
    copy.wait()
    parts = blocks // FOLD
    field_lines = parts * 2 * GROUP * SUBLANES
    width = FOLD * LANES
    for part in range(parts):
        mixed[field_lines + part * ROWS : field_lines + (part + 1) * ROWS, :] = edge[
            :, part * width : (part + 1) * width
        ]
    mixed[...] = dealt(mixed[...])
    take_rows(blocks, mixed, (down, up))
    for part in range(parts):
        line = field_lines + part * ROWS
        for p in range(FOLD):
            down_coef[part * FOLD + p] = mixed[line : line + HALO, block_at(p)]
            up_coef[part * FOLD + p] = mixed[line + ROWS - HALO : line + ROWS, block_at(p)]


def inner_rows_kernel(
    blocks, tracer, own_coef, params, outer, low, high, by_block, dealt_params, whole, coef_sem, mixed,
    staged, sems,
):
    copy = pltpu.make_async_copy(own_coef, whole, coef_sem)
    copy.start()
    fill_rows(blocks, (GROUP, ROWS - 2 * GROUP), tracer, mixed, staged, sems)
    copy.wait()
    parts = blocks // FOLD
    coef_lines = parts * 2 * GROUP * SUBLANES
    param_lines = coef_lines + parts * 4 * ROWS
    width = FOLD * LANES
    for part in range(parts):
        at = slice(part * width, (part + 1) * width)
        for array in range(4):
            line = coef_lines + (part * 4 + array) * ROWS
            mixed[line : line + ROWS, :] = whole[array, :, at]
        line = param_lines + part * SUBLANES
        mixed[line : line + SUBLANES, :] = params[:, at]
    mixed[...] = dealt(mixed[...])
    take_rows(blocks, mixed, (low, high))
    for part in range(parts):
        line = coef_lines + part * 4 * ROWS
        for p in range(FOLD):
            block = part * FOLD + p
            by_block[block] = mixed[line : line + 4 * ROWS, block_at(p)]
            dealt_params[:, block_at(block)] = mixed[
                param_lines + part * SUBLANES : param_lines + (part + 1) * SUBLANES, block_at(p)
            ]


def interior_kernel(blocks, own0, own1, own2, own3, own_coef, params, *rest):
    outs, (levels, *work, result, coef, sems) = rest[:5], rest[5:]
    copies = Copies(sems)
    waits = [
        copies.start(own, region(levels, 0, GROUP * i, blocks))
        for i, own in enumerate((own0, own1, own2, own3))
    ]
    waits.append(copies.start(own_coef, coef.at[:, 0 : 4 * ROWS]))
    for copy in waits:
        copy.wait()

    @pl.loop(0, 6)
    def _(i):
        level = jnp.where(i < 3, 0, jnp.where(i < 5, 1, 2))
        row = jnp.where(i < 3, 2 + 4 * i, jnp.where(i < 5, 4 * i - 8, 6))
        advance_group(level, row + HALO, levels, work, result, coef, params, blocks)

    waits = [
        copies.start(region(levels, level, row, blocks), out)
        for out, (level, row) in zip(outs, ((1, 2), (1, 10), (2, 4), (2, 8), (3, 6)))
    ]
    for copy in waits:
        copy.wait()


def edge_steps(outer, blocks, waits, sends, levels, work, result, coef, params):
    @pl.loop(0, 2 * STEPS)
    def _(step):
        level, side = lax.div(step, 2), lax.rem(step, 2)
        for k in range(STEPS):
            @pl.when(step == 2 * k)
            def _():
                for copy in waits[k]:
                    copy.wait()

        low = 2 * level - outer
        high = ROWS + outer - GROUP - 2 * level
        row = jnp.where(side == 0, low, high) + HALO
        advance_group(level, row, levels, work, result, coef, params, blocks)
        for k, copy in enumerate(sends):
            pl.when(step == k)(copy.start)


def coef_row(array, row):
    own = array * ROWS + row - HALO
    low = 4 * ROWS + 2 * HALO * array + row
    high = 4 * ROWS + 2 * HALO * array + row - ROWS
    return jnp.where(row < HALO, low, jnp.where(row < HALO + ROWS, own, high))


def load_coef(copies, own_coef, pair, other, place_of, coef):
    waits = [copies.start(own_coef, coef.at[:, 0 : 4 * ROWS])]
    for number, source in enumerate((pair.at[0], pair.at[1], other.at[0], other.at[1])):
        array = jnp.bitwise_xor(place_of[0], number)
        for side in range(2):
            first = 4 * ROWS + 2 * HALO * array + HALO * side
            waits.append(copies.start(source.at[side], coef.at[:, pl.ds(first, HALO)]))
    return waits


def middle_kernel(blocks, *refs):
    sources, refs = refs[:9], refs[9:]
    own_coef, pair, other, params, place_of = refs[:5]
    outs, (levels, *work, result, coef, sems) = refs[5:13], refs[13:]
    copies = Copies(sems)
    places = ((0, -4), (0, 0), (0, 12), (0, 16), (1, 2), (1, 10), (2, 4), (2, 8), (3, 6))
    waits = [[] for _ in range(STEPS)]
    for source, (level, row) in zip(sources, places):
        waits[level].append(copies.start(source, region(levels, level, row, blocks)))
    waits[0] += load_coef(copies, own_coef, pair, other, place_of, coef)
    places = [(k + 1, row) for k in range(STEPS) for row in (2 * k - 2, ROWS + 2 - GROUP - 2 * k)]
    sends = [
        copies.make(region(levels, level, row, blocks), out)
        for out, (level, row) in zip(outs, places)
    ]
    edge_steps(2, blocks, waits, sends, levels, work, result, coef, params)
    for copy in sends:
        copy.wait()


def last_kernel(blocks, *refs):
    sources, refs = refs[:12], refs[12:]
    own_coef, pair, other, params, place_of, cell_of, shift_of = refs[:7]
    low_out, high_out, predicted, levels, *work, result, coef, sems = refs[7:]
    copies = Copies(sems)
    places = (
        (0, -8), (0, -4), (0, 16), (0, 20),
        (1, -2), (1, 14), (2, 0), (2, 12), (3, 2), (3, 10), (4, 4), (4, 8),
    )
    waits = [[] for _ in range(STEPS + 1)]
    for source, (level, row) in zip(sources, places):
        waits[level].append(copies.start(source, region(levels, level, row, blocks)))
    waits[0] += load_coef(copies, own_coef, pair, other, place_of, coef)
    edge_steps(6, blocks, waits, (), levels, work, result, coef, params)
    for copy in waits[STEPS]:
        copy.wait()
    sends = [
        copies.start(region(levels, STEPS, row, blocks), out)
        for row, out in ((0, low_out), (ROWS - GROUP, high_out))
    ]
    lane = lax.broadcasted_iota(jnp.int32, (SUBLANES, LANES), 1)

    @pl.loop(0, predicted.shape[1] // LANES)
    def _(block):
        base = block * LANES

        def some(part, found):
            for i in range(PICKED):
                o = part * PICKED + i
                value = pltpu.roll(levels[cell_of[base + o]], shift_of[base + o], 1)
                found = jnp.where(lane == o, value, found)
            return found

        empty = jnp.zeros((SUBLANES, LANES), jnp.float32)
        predicted[:, block_at(block)] = lax.fori_loop(0, LANES // PICKED, some, empty)

    for copy in sends:
        copy.wait()


def field_kernel(blocks, *refs):
    parts, (out, cells, mixed, staged, sems, out_sems) = refs[: ROWS // GROUP], refs[ROWS // GROUP :]
    copies = Copies(sems)
    size = GROUP * blocks
    waits = [
        copies.start(part, cells.at[pl.ds(i * size, size)]) for i, part in enumerate(parts)
    ]
    for copy in waits:
        copy.wait()
    lines = ROWS * SUBLANES

    def line_at(part, row):
        return pl.ds(pl.multiple_of(part * lines + row * SUBLANES, SUBLANES), SUBLANES)

    @pl.loop(0, blocks // FOLD)
    def _(part):
        for row in range(ROWS):
            for p in range(FOLD):
                mixed[line_at(part, row), block_at(p)] = cells[row * blocks + part * FOLD + p]

    mixed[...] = dealt(mixed[...], back=True)

    def out_copy(block):
        return pltpu.make_async_copy(staged.at[block], out.at[:, block_at(block)], out_sems.at[block])

    @pl.loop(0, blocks // FOLD)
    def _(part):
        for q in range(FOLD):
            block = part * FOLD + q
            for row in range(ROWS):
                staged[block, pl.ds(row, SUBLANES, stride=ROWS), :] = mixed[
                    line_at(part, row), block_at(q)
                ]
            out_copy(block).start()

    @pl.loop(0, blocks)
    def _(block):
        out_copy(block).wait()


def scratch(columns, *more):
    blocks = columns // LANES
    group = pltpu.VMEM((GROUP * blocks, SUBLANES, LANES), jnp.float32)
    return [
        pltpu.VMEM(((STEPS + 1) * ALL_ROWS * blocks, SUBLANES, LANES), jnp.float32),
        *[group] * 5,
        pltpu.VMEM((blocks, 4 * ALL_ROWS, LANES), jnp.float32),
        *more,
    ]


def kernel_call(body, name, outs, specs, out_specs, scratches, cost, operands):
    return pl.pallas_call(
        body,
        out_shape=tuple(jax.ShapeDtypeStruct(shape, jnp.float32) for shape in outs),
        in_specs=specs,
        out_specs=out_specs,
        scratch_shapes=scratches,
        compiler_params=pltpu.CompilerParams(vmem_limit_bytes=TALL_LIMIT),
        cost_estimate=pl.CostEstimate(flops=0, bytes_accessed=cost * COST_BYTES, transcendentals=0),
        name=name,
    )(*operands)


def row_groups(tracer, coefficients, params, place_of):
    members, rows, columns = tracer.shape
    if members != SUBLANES or rows != ROWS or columns % (FOLD * LANES):
        raise ValueError("block shape")
    blocks = columns // LANES
    parts = blocks // FOLD
    flat = tracer.reshape(members * rows, columns)
    dma = pltpu.SemaphoreType.DMA
    staged = [pltpu.VMEM((blocks, members * rows, LANES), jnp.float32), dma((blocks,))]

    def mixed(lines):
        return pltpu.VMEM((parts * lines, FOLD * LANES), jnp.float32)

    group, edge = (GROUP * blocks, members, LANES), (blocks, HALO, LANES)
    up, down, up_coef, down_coef = kernel_call(
        functools.partial(outer_rows_kernel, blocks), "outer_rows",
        [group, group, edge, edge], [ANYWHERE, ANYWHERE, IN_SMEM], (IN_VMEM,) * 4,
        [pltpu.VMEM((rows, columns), jnp.float32), dma, mixed(2 * GROUP * members + rows)] + staged, 3,
        [flat, coefficients, place_of],
    )
    low, high, by_block, dealt_params = kernel_call(
        functools.partial(inner_rows_kernel, blocks), "inner_rows",
        [group, group, (blocks, 4 * rows, LANES), params.shape],
        [ANYWHERE, ANYWHERE, IN_VMEM, ANYWHERE], (IN_VMEM,) * 4,
        [
            pltpu.VMEM((4, rows, columns), jnp.float32), dma,
            mixed(2 * GROUP * members + 4 * rows + members),
        ] + staged, 3,
        [flat, coefficients, params, up],
    )
    return (down, low, high, up), (up_coef, down_coef), by_block, dealt_params


def transport(shape, own, low0, high0, own_coef, pair, other, params, place_of, obs_index, halos):
    members, rows, columns = shape
    blocks = columns // LANES
    group = (GROUP * blocks, members, LANES)
    flat = (members * rows, columns)
    dma = pltpu.SemaphoreType.DMA
    staged = pltpu.VMEM((blocks, members * rows, LANES), jnp.float32)
    gated, pair = lax.optimization_barrier((params, pair))
    inner = kernel_call(
        functools.partial(interior_kernel, blocks), "interior",
        [group] * 5, [ANYWHERE] * 5 + [IN_VMEM], (ANYWHERE,) * 5,
        scratch(columns, dma((16,))), 8, [*own, own_coef, gated],
    )
    upper, lower, low0, high0, *_ = lax.optimization_barrier(
        (own[2], own[1], low0, high0, inner[0])
    )
    low1, high1 = halos(upper, lower)
    first = kernel_call(
        functools.partial(middle_kernel, blocks), "edge_first",
        [group] * 8, [ANYWHERE] * 12 + [IN_VMEM, IN_SMEM], (ANYWHERE,) * 8,
        scratch(columns, dma((29,))), 10,
        [low0, own[0], own[3], high0, *inner, own_coef, pair, other, params, place_of],
    )
    obs_row, obs_col = obs_index // columns, obs_index % columns
    width = FOLD * LANES
    obs_block = obs_col // width * FOLD + obs_col % FOLD
    cell_of = (STEPS * ALL_ROWS + HALO + obs_row) * blocks + obs_block
    lane_of = obs_col % width // FOLD
    shift_of = (jnp.arange(obs_index.shape[0], dtype=jnp.int32) - lane_of) % LANES
    low4, high4, predicted = kernel_call(
        functools.partial(last_kernel, blocks), "edge_last",
        [group, group, (members, obs_index.shape[0])],
        [ANYWHERE] * 15 + [IN_VMEM] + [IN_SMEM] * 3, (ANYWHERE, ANYWHERE, IN_VMEM),
        scratch(columns, dma((31,))), 15,
        [low1, low0, high0, high1, *first, own_coef, pair, other, params, place_of, cell_of, shift_of],
    )
    (field,) = kernel_call(
        functools.partial(field_kernel, blocks), "field",
        [flat], [ANYWHERE] * 4, (ANYWHERE,),
        [
            pltpu.VMEM((rows * blocks, members, LANES), jnp.float32),
            pltpu.VMEM((members * rows * blocks // FOLD, FOLD * LANES), jnp.float32),
            staged, dma((4,)), dma((blocks,)),
        ],
        4, [low4, first[6], first[7], high4],
    )
    return field.reshape(shape), predicted, inner[0]


def products_kernel(total_obs, per_group, spread, everyone, own, values, variance, same, out):
    weight = 1.0 / (variance[...] * total_obs)
    innovation = (values[...] - own[...]) * weight
    predicted = everyone[...]
    anomalies = (predicted - hdot(same[...], predicted) / per_group) * spread
    right = jnp.concatenate([anomalies * weight, innovation], axis=0)
    out[...] = lax.dot_general(
        anomalies,
        right,
        (((1,), (1,)), ((), ())),
        precision=lax.Precision.HIGHEST,
        preferred_element_type=jnp.float32,
    )


def update_kernel(per_group, summands, same, own_same, rank_row, rank_col, anomalies, own, out):
    members = same.shape[0]
    total = summands[0]
    for index in range(1, summands.shape[0]):
        total = total + summands[index]
    together = same[...]
    row = lax.broadcasted_iota(jnp.int32, (members, members), 0)
    col = lax.broadcasted_iota(jnp.int32, (members, members), 1)
    system = jnp.where(row == col, 1.0, 0.0) + together * total[:, 0:members]
    right = own_same[...] * total[:, members:]
    for pivot in range(per_group):
        pick = jnp.where(rank_row[...] == pivot, together, 0.0)
        pivot_system = hdot(pick, system)
        pivot_right = hdot(pick, right)
        pivot_value = jnp.sum(pick * pivot_system, axis=1, keepdims=True)
        factor = jnp.sum(pick * system, axis=1, keepdims=True)
        is_pivot = rank_col[...] == pivot
        scale = 1.0 / pivot_value
        scaled_system, scaled_right = pivot_system * scale, pivot_right * scale
        system = jnp.where(is_pivot, scaled_system, system - factor * scaled_system)
        right = jnp.where(is_pivot, scaled_right, right - factor * scaled_right)
    change = lax.dot_general(
        right,
        anomalies[...],
        (((0,), (0,)), ((), ())),
        precision=lax.Precision.HIGHEST,
        preferred_element_type=jnp.float32,
    )
    out[...] = own[...] + change


def local(tracer, coefficients, parameters, obs_index, obs_values, obs_variance, member_group):
    local_members, rows, columns = tracer.shape
    ens_pos = lax.axis_index("ens")
    ens_count = lax.axis_size("ens")
    slab_count = lax.axis_size("slab")
    if ens_count != 4 or coefficients.shape[0] != 4 or slab_count & (slab_count - 1):
        raise ValueError("mesh shape")
    forward = [(i, i + 1) for i in range(slab_count - 1)]
    backward = [(target, source) for source, target in forward]

    def over_ens(mine):
        pair = jnp.stack([mine, lax.ppermute(mine, "ens", [(i, i ^ 1) for i in range(ens_count)])])
        return pair, lax.ppermute(pair, "ens", [(i, i ^ 2) for i in range(ens_count)])

    def halos(upper, lower):
        return lax.ppermute(upper, "slab", forward), lax.ppermute(lower, "slab", backward)

    place_of = jnp.reshape(ens_pos, (1,))
    own, coef_edges, own_coef, dealt_params = row_groups(
        tracer, coefficients, parameters, place_of
    )
    low0, high0 = halos(own[3], own[0])

    edge_low, edge_high = halos(*coef_edges)
    pair, other = over_ens(jnp.stack([edge_low, edge_high]))

    members = member_group.shape[0]
    per_group = members // GROUPS
    spread = 1.0 / math.sqrt(per_group - 1)
    same_bool = member_group[:, None] == member_group[None, :]
    same = same_bool.astype(jnp.float32)
    earlier = jnp.arange(members)[None, :] < jnp.arange(members)[:, None]
    rank = jnp.sum((same_bool & earlier).astype(jnp.int32), axis=1)
    own_same = lax.dynamic_slice_in_dim(same, ens_pos * local_members, local_members, 1)
    field, predicted, first_done = transport(
        tracer.shape, own, low0, high0,
        own_coef, pair, other, dealt_params, place_of, obs_index, halos,
    )

    later, _ = lax.optimization_barrier((parameters, first_done))
    shared = jnp.concatenate(over_ens(later), axis=0)
    all_params = jnp.concatenate(
        [lax.dynamic_index_in_dim(shared, ens_pos ^ i, 0, False) for i in range(ens_count)], axis=0
    )
    param_anomalies = (all_params - hdot(same, all_params) / per_group) * spread
    everyone = lax.all_gather(predicted, "ens", axis=0, tiled=True)
    total_obs = obs_variance.shape[0] * slab_count
    products = pl.pallas_call(
        functools.partial(products_kernel, float(total_obs), per_group, spread),
        out_shape=jax.ShapeDtypeStruct((members, members + local_members), jnp.float32),
        compiler_params=pltpu.CompilerParams(vmem_limit_bytes=VMEM_LIMIT),
        name="products",
    )(everyone, predicted, obs_values, obs_variance[None, :], same)
    distance = 1
    while distance < slab_count:
        pairs = [(i, i ^ distance) for i in range(slab_count)]
        products = products + lax.ppermute(products, "slab", pairs)
        distance *= 2
    updated = pl.pallas_call(
        functools.partial(update_kernel, per_group),
        out_shape=jax.ShapeDtypeStruct(parameters.shape, jnp.float32),
        compiler_params=pltpu.CompilerParams(vmem_limit_bytes=VMEM_LIMIT),
        name="update",
    )(products[None], same, own_same, rank[None, :], rank[:, None], param_anomalies, parameters)
    return (field, updated)


def solution(mesh):
    in_specs = (
        P("ens", "slab", None),
        P(None, "slab", None),
        P("ens", None),
        P("slab"),
        P("ens", "slab"),
        P("slab"),
        P(),
    )
    out_specs = (P("ens", "slab", None), P("ens", None))
    return jax.shard_map(local, mesh=mesh, in_specs=in_specs, out_specs=out_specs, check_vma=False)
```

```python
import functools
import math

import jax
import jax.numpy as jnp
from jax import lax
from jax.experimental import pallas as pl
from jax.experimental.pallas import tpu as pltpu
from jax.sharding import PartitionSpec as P

STEPS = 4
GROUPS = 8
HALO = 2 * STEPS
LANES = 128
SUBLANES = 8
ROWS = 16
GROUP = 4
FOLD = 4
PICKED = 128
ALL_ROWS = ROWS + 2 * HALO
VMEM_LIMIT = 16 * 1024 * 1024
TALL_LIMIT = 58 * 1024 * 1024
COST_BYTES = 200000
ANYWHERE = pl.BlockSpec(memory_space=pltpu.HBM)
IN_VMEM = pl.BlockSpec(memory_space=pltpu.VMEM)
IN_SMEM = pl.BlockSpec(memory_space=pltpu.SMEM)


def hdot(left, right):
    return jnp.dot(left, right, precision=lax.Precision.HIGHEST, preferred_element_type=jnp.float32)


def limited(left, right):
    return jnp.minimum(jnp.maximum(left, jnp.minimum(right, 0.0)), jnp.maximum(right, 0.0))


def block_at(block):
    return pl.ds(pl.multiple_of(block * LANES, LANES), LANES)


def everywhere(coef, block, place):
    return coef[block, pl.ds(place, SUBLANES, stride=0), :]


def edge_lanes():
    lane = lax.broadcasted_iota(jnp.int32, (SUBLANES, LANES), 1)
    return lane == 0, lane == LANES - 1


def dealt(values, back=False):
    shape = (FOLD * LANES, FOLD * LANES)
    natural = lax.broadcasted_iota(jnp.int32, shape, 1 if back else 0)
    place = lax.broadcasted_iota(jnp.int32, shape, 0 if back else 1)
    moves = natural == FOLD * lax.rem(place, LANES) + lax.div(place, LANES)
    moves = jnp.where(moves, 1.0, 0.0).astype(jnp.bfloat16)
    products = []
    for _ in range(3):
        piece = values.astype(jnp.bfloat16)
        products.append(jnp.dot(piece, moves, preferred_element_type=jnp.float32))
        values = values - piece.astype(jnp.float32)
    return products[0] + (products[1] + products[2])


def stencil(line, speeds):
    d = [line[i + 1] - line[i] for i in range(GROUP + 3)]
    slope = [None] + [limited(d[i - 1], d[i]) for i in range(1, GROUP + 3)]
    twice = [None] + [d[i] + d[i] for i in range(1, GROUP + 2)]
    results = []
    for i in range(2, GROUP + 2):
        speed = speeds[i - 2]
        forward = twice[i - 1] - slope[i - 1]
        backward = twice[i] - slope[i + 1]
        flux = speed * (jnp.where(speed > 0.0, forward, backward) + slope[i])
        results.append((flux, d[i] - d[i - 1]))
    return results


def advance_tile(cell, places, part, parts, levels, coef, params, blocks):
    start = part * FOLD
    before = lax.rem(part + parts - 1, parts) * FOLD
    after = lax.rem(part + 1, parts) * FOLD
    first, last = edge_lanes()
    own = [
        [levels[cell + (i - 2) * blocks + start + p] for p in range(FOLD)] for i in range(GROUP + 4)
    ]
    along_rows = [
        stencil(
            [own[i][p] for i in range(GROUP + 4)],
            [everywhere(coef, start + p, places[i][0]) for i in range(GROUP)],
        )
        for p in range(FOLD)
    ]
    values = []
    for i in range(GROUP):
        row = own[i + 2]
        here = cell + i * blocks
        left = [
            jnp.where(first, pltpu.roll(levels[here + before + p], 1, 1), pltpu.roll(row[p], 1, 1))
            for p in (FOLD - 2, FOLD - 1)
        ]
        right = [
            jnp.where(
                last,
                pltpu.roll(levels[here + after + p], LANES - 1, 1),
                pltpu.roll(row[p], LANES - 1, 1),
            )
            for p in (0, 1)
        ]
        along_columns = stencil(
            [*left, *row, *right], [everywhere(coef, start + p, places[i][1]) for p in range(FOLD)]
        )
        for p in range(FOLD):
            flux_x, lap_x = along_rows[p][i]
            flux_y, lap_y = along_columns[p]
            value = row[p] - 0.5 * (flux_x + flux_y)
            value = value + everywhere(coef, start + p, places[i][2]) * (lap_x + lap_y)
            source = params[:, block_at(start + p)] * everywhere(coef, start + p, places[i][3])
            values.append((here + start + p, value + source))
    for place, value in values:
        levels[place + ALL_ROWS * blocks] = value


def advance_group(level, row, levels, coef, params, blocks):
    cell = (level * ALL_ROWS + row) * blocks
    places = [[coef_row(array, row + i) for array in range(4)] for i in range(GROUP)]
    parts = blocks // FOLD

    @pl.loop(0, parts)
    def _(part):
        advance_tile(cell, places, part, parts, levels, coef, params, blocks)


class Copies:
    def __init__(self, sems):
        self.sems, self.used = sems, 0

    def make(self, source, target):
        copy = pltpu.make_async_copy(source, target, self.sems.at[self.used])
        self.used += 1
        assert self.used <= self.sems.shape[0]
        return copy

    def start(self, source, target):
        copy = self.make(source, target)
        copy.start()
        return copy


def region(levels, level, row, blocks):
    return levels.at[pl.ds((level * ALL_ROWS + HALO + row) * blocks, GROUP * blocks)]


def fill_rows(blocks, first_rows, tracer, mixed, staged, sems):
    def copy(block):
        return pltpu.make_async_copy(tracer.at[:, block_at(block)], staged.at[block], sems.at[block])

    @pl.loop(0, blocks)
    def _(block):
        copy(block).start()

    lines = len(first_rows) * GROUP * SUBLANES

    @pl.loop(0, blocks // FOLD)
    def _(part):
        for q in range(FOLD):
            block = part * FOLD + q
            copy(block).wait()
            for k, first_row in enumerate(first_rows):
                for row in range(GROUP):
                    line = part * lines + (k * GROUP + row) * SUBLANES
                    mixed[pl.ds(pl.multiple_of(line, SUBLANES), SUBLANES), block_at(q)] = staged[
                        block, pl.ds(first_row + row, SUBLANES, stride=ROWS), :
                    ]


def take_rows(blocks, mixed, outs):
    lines = len(outs) * GROUP * SUBLANES

    @pl.loop(0, blocks // FOLD)
    def _(part):
        for k, out in enumerate(outs):
            for row in range(GROUP):
                line = part * lines + (k * GROUP + row) * SUBLANES
                for p in range(FOLD):
                    out[row * blocks + part * FOLD + p] = mixed[
                        pl.ds(pl.multiple_of(line, SUBLANES), SUBLANES), block_at(p)
                    ]


def outer_rows_kernel(
    blocks, tracer, own_coef, place_of, up, down, up_coef, down_coef, edge, edge_sem, mixed, staged, sems
):
    copy = pltpu.make_async_copy(own_coef.at[place_of[0]], edge, edge_sem)
    copy.start()
    fill_rows(blocks, (0, ROWS - GROUP), tracer, mixed, staged, sems)
    copy.wait()
    parts = blocks // FOLD
    field_lines = parts * 2 * GROUP * SUBLANES
    width = FOLD * LANES
    for part in range(parts):
        mixed[field_lines + part * ROWS : field_lines + (part + 1) * ROWS, :] = edge[
            :, part * width : (part + 1) * width
        ]
    mixed[...] = dealt(mixed[...])
    take_rows(blocks, mixed, (down, up))
    for part in range(parts):
        line = field_lines + part * ROWS
        for p in range(FOLD):
            down_coef[part * FOLD + p] = mixed[line : line + HALO, block_at(p)]
            up_coef[part * FOLD + p] = mixed[line + ROWS - HALO : line + ROWS, block_at(p)]


def inner_rows_kernel(
    blocks, tracer, own_coef, params, outer, low, high, by_block, dealt_params, whole, coef_sem, mixed,
    staged, sems,
):
    copy = pltpu.make_async_copy(own_coef, whole, coef_sem)
    copy.start()
    fill_rows(blocks, (GROUP, ROWS - 2 * GROUP), tracer, mixed, staged, sems)
    copy.wait()
    parts = blocks // FOLD
    coef_lines = parts * 2 * GROUP * SUBLANES
    param_lines = coef_lines + parts * 4 * ROWS
    width = FOLD * LANES
    for part in range(parts):
        at = slice(part * width, (part + 1) * width)
        for array in range(4):
            line = coef_lines + (part * 4 + array) * ROWS
            mixed[line : line + ROWS, :] = whole[array, :, at]
        line = param_lines + part * SUBLANES
        mixed[line : line + SUBLANES, :] = params[:, at]
    mixed[...] = dealt(mixed[...])
    take_rows(blocks, mixed, (low, high))
    for part in range(parts):
        line = coef_lines + part * 4 * ROWS
        for p in range(FOLD):
            block = part * FOLD + p
            by_block[block] = mixed[line : line + 4 * ROWS, block_at(p)]
            dealt_params[:, block_at(block)] = mixed[
                param_lines + part * SUBLANES : param_lines + (part + 1) * SUBLANES, block_at(p)
            ]


def interior_kernel(blocks, own0, own1, own2, own3, own_coef, params, *rest):
    outs, (levels, coef, sems) = rest[:5], rest[5:]
    copies = Copies(sems)
    waits = [
        copies.start(own, region(levels, 0, GROUP * i, blocks))
        for i, own in enumerate((own0, own1, own2, own3))
    ]
    waits.append(copies.start(own_coef, coef.at[:, 0 : 4 * ROWS]))
    for copy in waits:
        copy.wait()

    @pl.loop(0, 6)
    def _(i):
        level = jnp.where(i < 3, 0, jnp.where(i < 5, 1, 2))
        row = jnp.where(i < 3, 2 + 4 * i, jnp.where(i < 5, 4 * i - 8, 6))
        advance_group(level, row + HALO, levels, coef, params, blocks)

    waits = [
        copies.start(region(levels, level, row, blocks), out)
        for out, (level, row) in zip(outs, ((1, 2), (1, 10), (2, 4), (2, 8), (3, 6)))
    ]
    for copy in waits:
        copy.wait()


def edge_steps(outer, blocks, waits, sends, levels, coef, params):
    @pl.loop(0, 2 * STEPS)
    def _(step):
        level, side = lax.div(step, 2), lax.rem(step, 2)
        for k in range(STEPS):
            @pl.when(step == 2 * k)
            def _():
                for copy in waits[k]:
                    copy.wait()

        low = 2 * level - outer
        high = ROWS + outer - GROUP - 2 * level
        row = jnp.where(side == 0, low, high) + HALO
        advance_group(level, row, levels, coef, params, blocks)
        for k, copy in enumerate(sends):
            pl.when(step == k)(copy.start)


def coef_row(array, row):
    own = array * ROWS + row - HALO
    low = 4 * ROWS + 2 * HALO * array + row
    high = 4 * ROWS + 2 * HALO * array + row - ROWS
    return jnp.where(row < HALO, low, jnp.where(row < HALO + ROWS, own, high))


def load_coef(copies, own_coef, pair, other, place_of, coef):
    waits = [copies.start(own_coef, coef.at[:, 0 : 4 * ROWS])]
    for number, source in enumerate((pair.at[0], pair.at[1], other.at[0], other.at[1])):
        array = jnp.bitwise_xor(place_of[0], number)
        for side in range(2):
            first = 4 * ROWS + 2 * HALO * array + HALO * side
            waits.append(copies.start(source.at[side], coef.at[:, pl.ds(first, HALO)]))
    return waits


def middle_kernel(blocks, *refs):
    sources, refs = refs[:9], refs[9:]
    own_coef, pair, other, params, place_of = refs[:5]
    outs, (levels, coef, sems) = refs[5:13], refs[13:]
    copies = Copies(sems)
    places = ((0, -4), (0, 0), (0, 12), (0, 16), (1, 2), (1, 10), (2, 4), (2, 8), (3, 6))
    waits = [[] for _ in range(STEPS)]
    for source, (level, row) in zip(sources, places):
        waits[level].append(copies.start(source, region(levels, level, row, blocks)))
    waits[0] += load_coef(copies, own_coef, pair, other, place_of, coef)
    places = [(k + 1, row) for k in range(STEPS) for row in (2 * k - 2, ROWS + 2 - GROUP - 2 * k)]
    sends = [
        copies.make(region(levels, level, row, blocks), out)
        for out, (level, row) in zip(outs, places)
    ]
    edge_steps(2, blocks, waits, sends, levels, coef, params)
    for copy in sends:
        copy.wait()


def last_kernel(blocks, *refs):
    sources, refs = refs[:12], refs[12:]
    own_coef, pair, other, params, place_of, cell_of, shift_of = refs[:7]
    low_out, high_out, predicted, levels, coef, sems = refs[7:]
    copies = Copies(sems)
    places = (
        (0, -8), (0, -4), (0, 16), (0, 20),
        (1, -2), (1, 14), (2, 0), (2, 12), (3, 2), (3, 10), (4, 4), (4, 8),
    )
    waits = [[] for _ in range(STEPS + 1)]
    for source, (level, row) in zip(sources, places):
        waits[level].append(copies.start(source, region(levels, level, row, blocks)))
    waits[0] += load_coef(copies, own_coef, pair, other, place_of, coef)
    edge_steps(6, blocks, waits, (), levels, coef, params)
    for copy in waits[STEPS]:
        copy.wait()
    sends = [
        copies.start(region(levels, STEPS, row, blocks), out)
        for row, out in ((0, low_out), (ROWS - GROUP, high_out))
    ]
    lane = lax.broadcasted_iota(jnp.int32, (SUBLANES, LANES), 1)

    @pl.loop(0, predicted.shape[1] // LANES)
    def _(block):
        base = block * LANES

        def some(part, found):
            for i in range(PICKED):
                o = part * PICKED + i
                value = pltpu.roll(levels[cell_of[base + o]], shift_of[base + o], 1)
                found = jnp.where(lane == o, value, found)
            return found

        empty = jnp.zeros((SUBLANES, LANES), jnp.float32)
        predicted[:, block_at(block)] = lax.fori_loop(0, LANES // PICKED, some, empty)

    for copy in sends:
        copy.wait()


def field_kernel(blocks, *refs):
    parts, (out, cells, mixed, staged, sems, out_sems) = refs[: ROWS // GROUP], refs[ROWS // GROUP :]
    copies = Copies(sems)
    size = GROUP * blocks
    waits = [
        copies.start(part, cells.at[pl.ds(i * size, size)]) for i, part in enumerate(parts)
    ]
    for copy in waits:
        copy.wait()
    lines = ROWS * SUBLANES

    def line_at(part, row):
        return pl.ds(pl.multiple_of(part * lines + row * SUBLANES, SUBLANES), SUBLANES)

    @pl.loop(0, blocks // FOLD)
    def _(part):
        for row in range(ROWS):
            for p in range(FOLD):
                mixed[line_at(part, row), block_at(p)] = cells[row * blocks + part * FOLD + p]

    mixed[...] = dealt(mixed[...], back=True)

    def out_copy(block):
        return pltpu.make_async_copy(staged.at[block], out.at[:, block_at(block)], out_sems.at[block])

    @pl.loop(0, blocks // FOLD)
    def _(part):
        for q in range(FOLD):
            block = part * FOLD + q
            for row in range(ROWS):
                staged[block, pl.ds(row, SUBLANES, stride=ROWS), :] = mixed[
                    line_at(part, row), block_at(q)
                ]
            out_copy(block).start()

    @pl.loop(0, blocks)
    def _(block):
        out_copy(block).wait()


def scratch(columns, *more):
    blocks = columns // LANES
    return [
        pltpu.VMEM(((STEPS + 1) * ALL_ROWS * blocks, SUBLANES, LANES), jnp.float32),
        pltpu.VMEM((blocks, 4 * ALL_ROWS, LANES), jnp.float32),
        *more,
    ]


def kernel_call(body, name, outs, specs, out_specs, scratches, cost, operands):
    return pl.pallas_call(
        body,
        out_shape=tuple(jax.ShapeDtypeStruct(shape, jnp.float32) for shape in outs),
        in_specs=specs,
        out_specs=out_specs,
        scratch_shapes=scratches,
        compiler_params=pltpu.CompilerParams(vmem_limit_bytes=TALL_LIMIT),
        cost_estimate=pl.CostEstimate(flops=0, bytes_accessed=cost * COST_BYTES, transcendentals=0),
        name=name,
    )(*operands)


def row_groups(tracer, coefficients, params, place_of):
    members, rows, columns = tracer.shape
    if members != SUBLANES or rows != ROWS or columns % (FOLD * LANES):
        raise ValueError("block shape")
    blocks = columns // LANES
    parts = blocks // FOLD
    flat = tracer.reshape(members * rows, columns)
    dma = pltpu.SemaphoreType.DMA
    staged = [pltpu.VMEM((blocks, members * rows, LANES), jnp.float32), dma((blocks,))]

    def mixed(lines):
        return pltpu.VMEM((parts * lines, FOLD * LANES), jnp.float32)

    group, edge = (GROUP * blocks, members, LANES), (blocks, HALO, LANES)
    up, down, up_coef, down_coef = kernel_call(
        functools.partial(outer_rows_kernel, blocks), "outer_rows",
        [group, group, edge, edge], [ANYWHERE, ANYWHERE, IN_SMEM], (IN_VMEM,) * 4,
        [pltpu.VMEM((rows, columns), jnp.float32), dma, mixed(2 * GROUP * members + rows)] + staged, 3,
        [flat, coefficients, place_of],
    )
    low, high, by_block, dealt_params = kernel_call(
        functools.partial(inner_rows_kernel, blocks), "inner_rows",
        [group, group, (blocks, 4 * rows, LANES), params.shape],
        [ANYWHERE, ANYWHERE, IN_VMEM, ANYWHERE], (IN_VMEM,) * 4,
        [
            pltpu.VMEM((4, rows, columns), jnp.float32), dma,
            mixed(2 * GROUP * members + 4 * rows + members),
        ] + staged, 3,
        [flat, coefficients, params, up],
    )
    return (down, low, high, up), (up_coef, down_coef), by_block, dealt_params


def transport(shape, own, low0, high0, own_coef, pair, other, params, place_of, obs_index, halos):
    members, rows, columns = shape
    blocks = columns // LANES
    group = (GROUP * blocks, members, LANES)
    flat = (members * rows, columns)
    dma = pltpu.SemaphoreType.DMA
    staged = pltpu.VMEM((blocks, members * rows, LANES), jnp.float32)
    inner = kernel_call(
        functools.partial(interior_kernel, blocks), "interior",
        [group] * 5, [ANYWHERE] * 5 + [IN_VMEM], (ANYWHERE,) * 5,
        scratch(columns, dma((16,))), 8, [*own, own_coef, params],
    )
    upper, lower, low0, high0, *_ = lax.optimization_barrier(
        (own[2], own[1], low0, high0, inner[0])
    )
    low1, high1 = halos(upper, lower)
    first = kernel_call(
        functools.partial(middle_kernel, blocks), "edge_first",
        [group] * 8, [ANYWHERE] * 12 + [IN_VMEM, IN_SMEM], (ANYWHERE,) * 8,
        scratch(columns, dma((29,))), 10,
        [low0, own[0], own[3], high0, *inner, own_coef, pair, other, params, place_of],
    )
    obs_row, obs_col = obs_index // columns, obs_index % columns
    width = FOLD * LANES
    obs_block = obs_col // width * FOLD + obs_col % FOLD
    cell_of = (STEPS * ALL_ROWS + HALO + obs_row) * blocks + obs_block
    lane_of = obs_col % width // FOLD
    shift_of = (jnp.arange(obs_index.shape[0], dtype=jnp.int32) - lane_of) % LANES
    low4, high4, predicted = kernel_call(
        functools.partial(last_kernel, blocks), "edge_last",
        [group, group, (members, obs_index.shape[0])],
        [ANYWHERE] * 15 + [IN_VMEM] + [IN_SMEM] * 3, (ANYWHERE, ANYWHERE, IN_VMEM),
        scratch(columns, dma((31,))), 15,
        [low1, low0, high0, high1, *first, own_coef, pair, other, params, place_of, cell_of, shift_of],
    )
    (field,) = kernel_call(
        functools.partial(field_kernel, blocks), "field",
        [flat], [ANYWHERE] * 4, (ANYWHERE,),
        [
            pltpu.VMEM((rows * blocks, members, LANES), jnp.float32),
            pltpu.VMEM((members * rows * blocks // FOLD, FOLD * LANES), jnp.float32),
            staged, dma((4,)), dma((blocks,)),
        ],
        4, [low4, first[6], first[7], high4],
    )
    return field.reshape(shape), predicted, inner[0]


def products_kernel(total_obs, per_group, spread, everyone, own, values, variance, same, out):
    weight = 1.0 / (variance[...] * total_obs)
    innovation = (values[...] - own[...]) * weight
    predicted = everyone[...]
    anomalies = (predicted - hdot(same[...], predicted) / per_group) * spread
    right = jnp.concatenate([anomalies * weight, innovation], axis=0)
    out[...] = lax.dot_general(
        anomalies,
        right,
        (((1,), (1,)), ((), ())),
        precision=lax.Precision.HIGHEST,
        preferred_element_type=jnp.float32,
    )


def update_kernel(per_group, summands, same, own_same, rank_row, rank_col, anomalies, own, out):
    members = same.shape[0]
    total = summands[0]
    for index in range(1, summands.shape[0]):
        total = total + summands[index]
    together = same[...]
    row = lax.broadcasted_iota(jnp.int32, (members, members), 0)
    col = lax.broadcasted_iota(jnp.int32, (members, members), 1)
    system = jnp.where(row == col, 1.0, 0.0) + together * total[:, 0:members]
    right = own_same[...] * total[:, members:]
    for pivot in range(per_group):
        pick = jnp.where(rank_row[...] == pivot, together, 0.0)
        pivot_system = hdot(pick, system)
        pivot_right = hdot(pick, right)
        pivot_value = jnp.sum(pick * pivot_system, axis=1, keepdims=True)
        factor = jnp.sum(pick * system, axis=1, keepdims=True)
        is_pivot = rank_col[...] == pivot
        scale = 1.0 / pivot_value
        scaled_system, scaled_right = pivot_system * scale, pivot_right * scale
        system = jnp.where(is_pivot, scaled_system, system - factor * scaled_system)
        right = jnp.where(is_pivot, scaled_right, right - factor * scaled_right)
    change = lax.dot_general(
        right,
        anomalies[...],
        (((0,), (0,)), ((), ())),
        precision=lax.Precision.HIGHEST,
        preferred_element_type=jnp.float32,
    )
    out[...] = own[...] + change


def local(tracer, coefficients, parameters, obs_index, obs_values, obs_variance, member_group):
    local_members, rows, columns = tracer.shape
    ens_pos = lax.axis_index("ens")
    ens_count = lax.axis_size("ens")
    slab_count = lax.axis_size("slab")
    if ens_count != 4 or coefficients.shape[0] != 4 or slab_count & (slab_count - 1):
        raise ValueError("mesh shape")
    forward = [(i, i + 1) for i in range(slab_count - 1)]
    backward = [(target, source) for source, target in forward]

    def over_ens(mine):
        pair = jnp.stack([mine, lax.ppermute(mine, "ens", [(i, i ^ 1) for i in range(ens_count)])])
        return pair, lax.ppermute(pair, "ens", [(i, i ^ 2) for i in range(ens_count)])

    def halos(upper, lower):
        return lax.ppermute(upper, "slab", forward), lax.ppermute(lower, "slab", backward)

    place_of = jnp.reshape(ens_pos, (1,))
    own, coef_edges, own_coef, dealt_params = row_groups(
        tracer, coefficients, parameters, place_of
    )
    low0, high0 = halos(own[3], own[0])

    edge_low, edge_high = halos(*coef_edges)
    pair, other = over_ens(jnp.stack([edge_low, edge_high]))

    members = member_group.shape[0]
    per_group = members // GROUPS
    spread = 1.0 / math.sqrt(per_group - 1)
    same_bool = member_group[:, None] == member_group[None, :]
    same = same_bool.astype(jnp.float32)
    earlier = jnp.arange(members)[None, :] < jnp.arange(members)[:, None]
    rank = jnp.sum((same_bool & earlier).astype(jnp.int32), axis=1)
    own_same = lax.dynamic_slice_in_dim(same, ens_pos * local_members, local_members, 1)
    field, predicted, first_done = transport(
        tracer.shape, own, low0, high0,
        own_coef, pair, other, dealt_params, place_of, obs_index, halos,
    )

    later, _ = lax.optimization_barrier((parameters, first_done))
    shared = jnp.concatenate(over_ens(later), axis=0)
    all_params = jnp.concatenate(
        [lax.dynamic_index_in_dim(shared, ens_pos ^ i, 0, False) for i in range(ens_count)], axis=0
    )
    param_anomalies = (all_params - hdot(same, all_params) / per_group) * spread
    everyone = lax.all_gather(predicted, "ens", axis=0, tiled=True)
    total_obs = obs_variance.shape[0] * slab_count
    products = pl.pallas_call(
        functools.partial(products_kernel, float(total_obs), per_group, spread),
        out_shape=jax.ShapeDtypeStruct((members, members + local_members), jnp.float32),
        compiler_params=pltpu.CompilerParams(vmem_limit_bytes=VMEM_LIMIT),
        name="products",
    )(everyone, predicted, obs_values, obs_variance[None, :], same)
    distance = 1
    while distance < slab_count:
        pairs = [(i, i ^ distance) for i in range(slab_count)]
        products = products + lax.ppermute(products, "slab", pairs)
        distance *= 2
    updated = pl.pallas_call(
        functools.partial(update_kernel, per_group),
        out_shape=jax.ShapeDtypeStruct(parameters.shape, jnp.float32),
        compiler_params=pltpu.CompilerParams(vmem_limit_bytes=VMEM_LIMIT),
        name="update",
    )(products[None], same, own_same, rank[None, :], rank[:, None], param_anomalies, parameters)
    return (field, updated)


def solution(mesh):
    in_specs = (
        P("ens", "slab", None),
        P(None, "slab", None),
        P("ens", None),
        P("slab"),
        P("ens", "slab"),
        P("slab"),
        P(),
    )
    out_specs = (P("ens", "slab", None), P("ens", None))
    return jax.shard_map(local, mesh=mesh, in_specs=in_specs, out_specs=out_specs, check_vma=False)
```

```python
import functools
import math

import jax
import jax.numpy as jnp
from jax import lax
from jax.experimental import pallas as pl
from jax.experimental.pallas import tpu as pltpu
from jax.sharding import PartitionSpec as P

STEPS = 4
GROUPS = 8
HALO = 2 * STEPS
LANES = 128
SUBLANES = 8
ROWS = 16
GROUP = 4
FOLD = 4
PICKED = 128
TILES = 2
FIELD_CALLS = 3
ALL_ROWS = ROWS + 2 * HALO
VMEM_LIMIT = 16 * 1024 * 1024
TALL_LIMIT = 58 * 1024 * 1024
COST_BYTES = 200000
ANYWHERE = pl.BlockSpec(memory_space=pltpu.HBM)
IN_VMEM = pl.BlockSpec(memory_space=pltpu.VMEM)
IN_SMEM = pl.BlockSpec(memory_space=pltpu.SMEM)


def hdot(left, right):
    return jnp.dot(left, right, precision=lax.Precision.HIGHEST, preferred_element_type=jnp.float32)


def limited(left, right):
    return jnp.minimum(jnp.maximum(left, jnp.minimum(right, 0.0)), jnp.maximum(right, 0.0))


def block_at(block):
    return pl.ds(pl.multiple_of(block * LANES, LANES), LANES)


def everywhere(coef, block, place):
    return coef[block, pl.ds(place, SUBLANES, stride=0), :]


def edge_lanes():
    lane = lax.broadcasted_iota(jnp.int32, (SUBLANES, LANES), 1)
    return lane == 0, lane == LANES - 1


def dealt(values, back=False):
    shape = (FOLD * LANES, FOLD * LANES)
    natural = lax.broadcasted_iota(jnp.int32, shape, 1 if back else 0)
    place = lax.broadcasted_iota(jnp.int32, shape, 0 if back else 1)
    moves = natural == FOLD * lax.rem(place, LANES) + lax.div(place, LANES)
    moves = jnp.where(moves, 1.0, 0.0).astype(jnp.bfloat16)
    products = []
    for _ in range(3):
        piece = values.astype(jnp.bfloat16)
        products.append(jnp.dot(piece, moves, preferred_element_type=jnp.float32))
        values = values - piece.astype(jnp.float32)
    return products[0] + (products[1] + products[2])


def stencil(line, speeds):
    d = [line[i + 1] - line[i] for i in range(GROUP + 3)]
    slope = [None] + [limited(d[i - 1], d[i]) for i in range(1, GROUP + 3)]
    twice = [None] + [d[i] + d[i] for i in range(1, GROUP + 2)]
    results = []
    for i in range(2, GROUP + 2):
        speed = speeds[i - 2]
        forward = twice[i - 1] - slope[i - 1]
        backward = twice[i] - slope[i + 1]
        flux = speed * (jnp.where(speed > 0.0, forward, backward) + slope[i])
        results.append((flux, d[i] - d[i - 1]))
    return results


def advance_tile(cell, places, part, parts, source, target, coef, params, blocks):
    start = part * FOLD
    before = lax.rem(part + parts - 1, parts) * FOLD
    after = lax.rem(part + 1, parts) * FOLD
    first, last = edge_lanes()
    own = [
        [source[cell + (i - 2) * blocks + start + p] for p in range(FOLD)] for i in range(GROUP + 4)
    ]
    along_rows = [
        stencil(
            [own[i][p] for i in range(GROUP + 4)],
            [everywhere(coef, start + p, places[i][0]) for i in range(GROUP)],
        )
        for p in range(FOLD)
    ]
    for i in range(GROUP):
        row = own[i + 2]
        here = cell + i * blocks
        left = [
            jnp.where(first, pltpu.roll(source[here + before + p], 1, 1), pltpu.roll(row[p], 1, 1))
            for p in (FOLD - 2, FOLD - 1)
        ]
        right = [
            jnp.where(
                last,
                pltpu.roll(source[here + after + p], LANES - 1, 1),
                pltpu.roll(row[p], LANES - 1, 1),
            )
            for p in (0, 1)
        ]
        along_columns = stencil(
            [*left, *row, *right], [everywhere(coef, start + p, places[i][1]) for p in range(FOLD)]
        )
        for p in range(FOLD):
            flux_x, lap_x = along_rows[p][i]
            flux_y, lap_y = along_columns[p]
            value = row[p] - 0.5 * (flux_x + flux_y)
            value = value + everywhere(coef, start + p, places[i][2]) * (lap_x + lap_y)
            value = value + params[:, block_at(start + p)] * everywhere(coef, start + p, places[i][3])
            target[here + start + p] = value


def advance_group(source, target, row, coef, params, blocks):
    cell = row * blocks
    places = [[coef_row(array, row + i) for array in range(4)] for i in range(GROUP)]
    parts = blocks // FOLD

    @pl.loop(0, parts // TILES)
    def _(some):
        for k in range(TILES):
            advance_tile(
                cell, places, some * TILES + k, parts, source, target, coef, params, blocks
            )


class Copies:
    def __init__(self, sems):
        self.sems, self.used = sems, 0

    def make(self, source, target):
        copy = pltpu.make_async_copy(source, target, self.sems.at[self.used])
        self.used += 1
        assert self.used <= self.sems.shape[0]
        return copy

    def start(self, source, target):
        copy = self.make(source, target)
        copy.start()
        return copy


def region(levels, level, row, blocks):
    return levels[level].at[pl.ds((HALO + row) * blocks, GROUP * blocks)]


def fill_rows(blocks, first_rows, tracer, mixed, staged, sems):
    def copy(block):
        return pltpu.make_async_copy(tracer.at[:, block_at(block)], staged.at[block], sems.at[block])

    @pl.loop(0, blocks)
    def _(block):
        copy(block).start()

    lines = len(first_rows) * GROUP * SUBLANES

    @pl.loop(0, blocks // FOLD)
    def _(part):
        for q in range(FOLD):
            block = part * FOLD + q
            copy(block).wait()
            for k, first_row in enumerate(first_rows):
                for row in range(GROUP):
                    line = part * lines + (k * GROUP + row) * SUBLANES
                    mixed[pl.ds(pl.multiple_of(line, SUBLANES), SUBLANES), block_at(q)] = staged[
                        block, pl.ds(first_row + row, SUBLANES, stride=ROWS), :
                    ]


def take_rows(blocks, mixed, outs):
    lines = len(outs) * GROUP * SUBLANES

    @pl.loop(0, blocks // FOLD)
    def _(part):
        for k, out in enumerate(outs):
            for row in range(GROUP):
                line = part * lines + (k * GROUP + row) * SUBLANES
                for p in range(FOLD):
                    out[row * blocks + part * FOLD + p] = mixed[
                        pl.ds(pl.multiple_of(line, SUBLANES), SUBLANES), block_at(p)
                    ]


def outer_rows_kernel(
    blocks, tracer, own_coef, place_of, up, down, up_coef, down_coef, edge, edge_sem, mixed, staged, sems
):
    copy = pltpu.make_async_copy(own_coef.at[place_of[0]], edge, edge_sem)
    copy.start()
    fill_rows(blocks, (0, ROWS - GROUP), tracer, mixed, staged, sems)
    copy.wait()
    parts = blocks // FOLD
    field_lines = parts * 2 * GROUP * SUBLANES
    width = FOLD * LANES
    for part in range(parts):
        mixed[field_lines + part * ROWS : field_lines + (part + 1) * ROWS, :] = edge[
            :, part * width : (part + 1) * width
        ]
    mixed[...] = dealt(mixed[...])
    take_rows(blocks, mixed, (down, up))
    for part in range(parts):
        line = field_lines + part * ROWS
        for p in range(FOLD):
            down_coef[part * FOLD + p] = mixed[line : line + HALO, block_at(p)]
            up_coef[part * FOLD + p] = mixed[line + ROWS - HALO : line + ROWS, block_at(p)]


def inner_rows_kernel(
    blocks, tracer, own_coef, params, outer, low, high, by_block, dealt_params, whole, coef_sem, mixed,
    staged, sems,
):
    copy = pltpu.make_async_copy(own_coef, whole, coef_sem)
    copy.start()
    fill_rows(blocks, (GROUP, ROWS - 2 * GROUP), tracer, mixed, staged, sems)
    copy.wait()
    parts = blocks // FOLD
    coef_lines = parts * 2 * GROUP * SUBLANES
    param_lines = coef_lines + parts * 4 * ROWS
    width = FOLD * LANES
    for part in range(parts):
        at = slice(part * width, (part + 1) * width)
        for array in range(4):
            line = coef_lines + (part * 4 + array) * ROWS
            mixed[line : line + ROWS, :] = whole[array, :, at]
        line = param_lines + part * SUBLANES
        mixed[line : line + SUBLANES, :] = params[:, at]
    mixed[...] = dealt(mixed[...])
    take_rows(blocks, mixed, (low, high))
    for part in range(parts):
        line = coef_lines + part * 4 * ROWS
        for p in range(FOLD):
            block = part * FOLD + p
            by_block[block] = mixed[line : line + 4 * ROWS, block_at(p)]
            dealt_params[:, block_at(block)] = mixed[
                param_lines + part * SUBLANES : param_lines + (part + 1) * SUBLANES, block_at(p)
            ]


def interior_kernel(blocks, own0, own1, own2, own3, own_coef, params, *rest):
    outs, (*levels, coef, sems) = rest[:5], rest[5:]
    copies = Copies(sems)
    waits = [
        copies.start(own, region(levels, 0, GROUP * i, blocks))
        for i, own in enumerate((own0, own1, own2, own3))
    ]
    waits.append(copies.start(own_coef, coef.at[:, 0 : 4 * ROWS]))
    for copy in waits:
        copy.wait()

    for level, start, count in ((0, 2, 3), (1, 4, 2), (2, 6, 1)):
        @pl.loop(0, count)
        def _(i):
            row = start + HALO + GROUP * i
            advance_group(levels[level], levels[level + 1], row, coef, params, blocks)

    waits = [
        copies.start(region(levels, level, row, blocks), out)
        for out, (level, row) in zip(outs, ((1, 2), (1, 10), (2, 4), (2, 8), (3, 6)))
    ]
    for copy in waits:
        copy.wait()


def edge_steps(outer, blocks, waits, sends, levels, coef, params):
    for level in range(STEPS):
        for copy in waits[level]:
            copy.wait()
        low, high = 2 * level - outer, ROWS + outer - GROUP - 2 * level

        @pl.loop(0, 2)
        def _(side):
            row = low + HALO + side * (high - low)
            advance_group(levels[level], levels[level + 1], row, coef, params, blocks)

        for copy in sends[2 * level : 2 * level + 2]:
            copy.start()


def coef_row(array, row):
    own = array * ROWS + row - HALO
    low = 4 * ROWS + 2 * HALO * array + row
    high = 4 * ROWS + 2 * HALO * array + row - ROWS
    return jnp.where(row < HALO, low, jnp.where(row < HALO + ROWS, own, high))


def load_coef(copies, own_coef, pair, other, place_of, coef):
    waits = [copies.start(own_coef, coef.at[:, 0 : 4 * ROWS])]
    for number, source in enumerate((pair.at[0], pair.at[1], other.at[0], other.at[1])):
        array = jnp.bitwise_xor(place_of[0], number)
        for side in range(2):
            first = 4 * ROWS + 2 * HALO * array + HALO * side
            waits.append(copies.start(source.at[side], coef.at[:, pl.ds(first, HALO)]))
    return waits


def middle_kernel(blocks, *refs):
    sources, refs = refs[:9], refs[9:]
    own_coef, pair, other, params, place_of = refs[:5]
    outs, (*levels, coef, sems) = refs[5:13], refs[13:]
    copies = Copies(sems)
    places = ((0, -4), (0, 0), (0, 12), (0, 16), (1, 2), (1, 10), (2, 4), (2, 8), (3, 6))
    waits = [[] for _ in range(STEPS)]
    for source, (level, row) in zip(sources, places):
        waits[level].append(copies.start(source, region(levels, level, row, blocks)))
    waits[0] += load_coef(copies, own_coef, pair, other, place_of, coef)
    places = [(k + 1, row) for k in range(STEPS) for row in (2 * k - 2, ROWS + 2 - GROUP - 2 * k)]
    sends = [
        copies.make(region(levels, level, row, blocks), out)
        for out, (level, row) in zip(outs, places)
    ]
    edge_steps(2, blocks, waits, sends, levels, coef, params)
    for copy in sends:
        copy.wait()


def last_kernel(blocks, *refs):
    sources, refs = refs[:12], refs[12:]
    own_coef, pair, other, params, place_of, cell_of, shift_of = refs[:7]
    low_out, high_out, predicted, *levels, coef, sems = refs[7:]
    copies = Copies(sems)
    places = (
        (0, -8), (0, -4), (0, 16), (0, 20),
        (1, -2), (1, 14), (2, 0), (2, 12), (3, 2), (3, 10), (4, 4), (4, 8),
    )
    waits = [[] for _ in range(STEPS + 1)]
    for source, (level, row) in zip(sources, places):
        waits[level].append(copies.start(source, region(levels, level, row, blocks)))
    waits[0] += load_coef(copies, own_coef, pair, other, place_of, coef)
    edge_steps(6, blocks, waits, (), levels, coef, params)
    for copy in waits[STEPS]:
        copy.wait()
    sends = [
        copies.start(region(levels, STEPS, row, blocks), out)
        for row, out in ((0, low_out), (ROWS - GROUP, high_out))
    ]
    lane = lax.broadcasted_iota(jnp.int32, (SUBLANES, LANES), 1)

    @pl.loop(0, predicted.shape[1] // LANES)
    def _(block):
        base = block * LANES

        def some(part, found):
            for i in range(PICKED):
                o = part * PICKED + i
                value = pltpu.roll(levels[STEPS][cell_of[base + o]], shift_of[base + o], 1)
                found = jnp.where(lane == o, value, found)
            return found

        empty = jnp.zeros((SUBLANES, LANES), jnp.float32)
        predicted[:, block_at(block)] = lax.fori_loop(0, LANES // PICKED, some, empty)

    for copy in sends:
        copy.wait()


def field_kernel(blocks, first_part, count, *refs):
    sources, refs = refs[: ROWS // GROUP], refs[-6:]
    out, cells, mixed, staged, sems, out_sems = refs
    copies = Copies(sems)
    width = count * FOLD
    waits = [
        copies.start(
            source.at[pl.ds(row * blocks + first_part * FOLD, width)],
            cells.at[pl.ds((i * GROUP + row) * width, width)],
        )
        for i, source in enumerate(sources)
        for row in range(GROUP)
    ]
    for copy in waits:
        copy.wait()
    lines = ROWS * SUBLANES

    def line_at(part, row):
        return pl.ds(pl.multiple_of(part * lines + row * SUBLANES, SUBLANES), SUBLANES)

    @pl.loop(0, count)
    def _(part):
        for row in range(ROWS):
            for p in range(FOLD):
                mixed[line_at(part, row), block_at(p)] = cells[row * width + part * FOLD + p]

    mixed[...] = dealt(mixed[...], back=True)

    def out_copy(block):
        return pltpu.make_async_copy(
            staged.at[block], out.at[:, block_at(first_part * FOLD + block)], out_sems.at[block]
        )

    @pl.loop(0, count)
    def _(part):
        for q in range(FOLD):
            block = part * FOLD + q
            for row in range(ROWS):
                staged[block, pl.ds(row, SUBLANES, stride=ROWS), :] = mixed[
                    line_at(part, row), block_at(q)
                ]
            out_copy(block).start()

    @pl.loop(0, width)
    def _(block):
        out_copy(block).wait()


def scratch(columns, *more):
    blocks = columns // LANES
    return [
        *[pltpu.VMEM((ALL_ROWS * blocks, SUBLANES, LANES), jnp.float32)] * (STEPS + 1),
        pltpu.VMEM((blocks, 4 * ALL_ROWS, LANES), jnp.float32),
        *more,
    ]


def kernel_call(body, name, outs, specs, out_specs, scratches, cost, operands, aliases={}):
    return pl.pallas_call(
        body,
        out_shape=tuple(jax.ShapeDtypeStruct(shape, jnp.float32) for shape in outs),
        in_specs=specs,
        out_specs=out_specs,
        scratch_shapes=scratches,
        compiler_params=pltpu.CompilerParams(vmem_limit_bytes=TALL_LIMIT),
        cost_estimate=pl.CostEstimate(flops=0, bytes_accessed=cost * COST_BYTES, transcendentals=0),
        input_output_aliases=aliases,
        name=name,
    )(*operands)


def row_groups(tracer, coefficients, params, place_of):
    members, rows, columns = tracer.shape
    if members != SUBLANES or rows != ROWS or columns % (FOLD * LANES):
        raise ValueError("block shape")
    blocks = columns // LANES
    parts = blocks // FOLD
    flat = tracer.reshape(members * rows, columns)
    dma = pltpu.SemaphoreType.DMA
    staged = [pltpu.VMEM((blocks, members * rows, LANES), jnp.float32), dma((blocks,))]

    def mixed(lines):
        return pltpu.VMEM((parts * lines, FOLD * LANES), jnp.float32)

    group, edge = (GROUP * blocks, members, LANES), (blocks, HALO, LANES)
    up, down, up_coef, down_coef = kernel_call(
        functools.partial(outer_rows_kernel, blocks), "outer_rows",
        [group, group, edge, edge], [ANYWHERE, ANYWHERE, IN_SMEM], (IN_VMEM,) * 4,
        [pltpu.VMEM((rows, columns), jnp.float32), dma, mixed(2 * GROUP * members + rows)] + staged, 3,
        [flat, coefficients, place_of],
    )
    low, high, by_block, dealt_params = kernel_call(
        functools.partial(inner_rows_kernel, blocks), "inner_rows",
        [group, group, (blocks, 4 * rows, LANES), params.shape],
        [ANYWHERE, ANYWHERE, IN_VMEM, ANYWHERE], (IN_VMEM,) * 4,
        [
            pltpu.VMEM((4, rows, columns), jnp.float32), dma,
            mixed(2 * GROUP * members + 4 * rows + members),
        ] + staged, 3,
        [flat, coefficients, params, up],
    )
    return (down, low, high, up), (up_coef, down_coef), by_block, dealt_params


def transport(shape, own, low0, high0, own_coef, pair, other, params, place_of, obs_index, halos):
    members, rows, columns = shape
    blocks = columns // LANES
    group = (GROUP * blocks, members, LANES)
    flat = (members * rows, columns)
    dma = pltpu.SemaphoreType.DMA
    inner = kernel_call(
        functools.partial(interior_kernel, blocks), "interior",
        [group] * 5, [ANYWHERE] * 5 + [IN_VMEM], (ANYWHERE,) * 5,
        scratch(columns, dma((16,))), 8, [*own, own_coef, params],
    )
    upper, lower, low0, high0, *_ = lax.optimization_barrier(
        (own[2], own[1], low0, high0, inner[0])
    )
    low1, high1 = halos(upper, lower)
    first = kernel_call(
        functools.partial(middle_kernel, blocks), "edge_first",
        [group] * 8, [ANYWHERE] * 12 + [IN_VMEM, IN_SMEM], (ANYWHERE,) * 8,
        scratch(columns, dma((29,))), 10,
        [low0, own[0], own[3], high0, *inner, own_coef, pair, other, params, place_of],
    )
    obs_row, obs_col = obs_index // columns, obs_index % columns
    width = FOLD * LANES
    obs_block = obs_col // width * FOLD + obs_col % FOLD
    cell_of = (HALO + obs_row) * blocks + obs_block
    lane_of = obs_col % width // FOLD
    shift_of = (jnp.arange(obs_index.shape[0], dtype=jnp.int32) - lane_of) % LANES
    low4, high4, predicted = kernel_call(
        functools.partial(last_kernel, blocks), "edge_last",
        [group, group, (members, obs_index.shape[0])],
        [ANYWHERE] * 15 + [IN_VMEM] + [IN_SMEM] * 3, (ANYWHERE, ANYWHERE, IN_VMEM),
        scratch(columns, dma((31,))), 15,
        [low1, low0, high0, high1, *first, own_coef, pair, other, params, place_of, cell_of, shift_of],
    )
    field, first_part, parts = None, 0, blocks // FOLD
    for i in range(FIELD_CALLS):
        count = parts * (i + 1) // FIELD_CALLS - first_part
        width = count * FOLD
        previous = [] if field is None else [field]
        (field,) = kernel_call(
            functools.partial(field_kernel, blocks, first_part, count), "field_%d" % i,
            [flat], [ANYWHERE] * (4 + len(previous)), (ANYWHERE,),
            [
                pltpu.VMEM((rows * width, members, LANES), jnp.float32),
                pltpu.VMEM((members * rows * count, FOLD * LANES), jnp.float32),
                pltpu.VMEM((width, members * rows, LANES), jnp.float32),
                dma((rows,)), dma((width,)),
            ],
            4, [low4, first[6], first[7], high4, *previous], {4: 0} if previous else {},
        )
        first_part += count
    return field.reshape(shape), predicted, inner[0]


def products_kernel(total_obs, per_group, spread, everyone, own, values, variance, same, out):
    weight = 1.0 / (variance[...] * total_obs)
    innovation = (values[...] - own[...]) * weight
    predicted = everyone[...]
    anomalies = (predicted - hdot(same[...], predicted) / per_group) * spread
    right = jnp.concatenate([anomalies * weight, innovation], axis=0)
    out[...] = lax.dot_general(
        anomalies,
        right,
        (((1,), (1,)), ((), ())),
        precision=lax.Precision.HIGHEST,
        preferred_element_type=jnp.float32,
    )


def update_kernel(per_group, summands, same, own_same, rank_row, rank_col, anomalies, own, out):
    members = same.shape[0]
    total = summands[0]
    for index in range(1, summands.shape[0]):
        total = total + summands[index]
    together = same[...]
    row = lax.broadcasted_iota(jnp.int32, (members, members), 0)
    col = lax.broadcasted_iota(jnp.int32, (members, members), 1)
    system = jnp.where(row == col, 1.0, 0.0) + together * total[:, 0:members]
    right = own_same[...] * total[:, members:]
    for pivot in range(per_group):
        pick = jnp.where(rank_row[...] == pivot, together, 0.0)
        pivot_system = hdot(pick, system)
        pivot_right = hdot(pick, right)
        pivot_value = jnp.sum(pick * pivot_system, axis=1, keepdims=True)
        factor = jnp.sum(pick * system, axis=1, keepdims=True)
        is_pivot = rank_col[...] == pivot
        scale = 1.0 / pivot_value
        scaled_system, scaled_right = pivot_system * scale, pivot_right * scale
        system = jnp.where(is_pivot, scaled_system, system - factor * scaled_system)
        right = jnp.where(is_pivot, scaled_right, right - factor * scaled_right)
    change = lax.dot_general(
        right,
        anomalies[...],
        (((0,), (0,)), ((), ())),
        precision=lax.Precision.HIGHEST,
        preferred_element_type=jnp.float32,
    )
    out[...] = own[...] + change


def local(tracer, coefficients, parameters, obs_index, obs_values, obs_variance, member_group):
    local_members, rows, columns = tracer.shape
    ens_pos = lax.axis_index("ens")
    ens_count = lax.axis_size("ens")
    slab_count = lax.axis_size("slab")
    if ens_count != 4 or coefficients.shape[0] != 4 or slab_count & (slab_count - 1):
        raise ValueError("mesh shape")
    forward = [(i, i + 1) for i in range(slab_count - 1)]
    backward = [(target, source) for source, target in forward]

    def over_ens(mine):
        pair = jnp.stack([mine, lax.ppermute(mine, "ens", [(i, i ^ 1) for i in range(ens_count)])])
        return pair, lax.ppermute(pair, "ens", [(i, i ^ 2) for i in range(ens_count)])

    def halos(upper, lower):
        return lax.ppermute(upper, "slab", forward), lax.ppermute(lower, "slab", backward)

    place_of = jnp.reshape(ens_pos, (1,))
    own, coef_edges, own_coef, dealt_params = row_groups(
        tracer, coefficients, parameters, place_of
    )
    low0, high0 = halos(own[3], own[0])

    edge_low, edge_high = halos(*coef_edges)
    pair, other = over_ens(jnp.stack([edge_low, edge_high]))

    members = member_group.shape[0]
    per_group = members // GROUPS
    spread = 1.0 / math.sqrt(per_group - 1)
    same_bool = member_group[:, None] == member_group[None, :]
    same = same_bool.astype(jnp.float32)
    earlier = jnp.arange(members)[None, :] < jnp.arange(members)[:, None]
    rank = jnp.sum((same_bool & earlier).astype(jnp.int32), axis=1)
    own_same = lax.dynamic_slice_in_dim(same, ens_pos * local_members, local_members, 1)
    field, predicted, first_done = transport(
        tracer.shape, own, low0, high0,
        own_coef, pair, other, dealt_params, place_of, obs_index, halos,
    )

    later, _ = lax.optimization_barrier((parameters, first_done))
    shared = jnp.concatenate(over_ens(later), axis=0)
    all_params = jnp.concatenate(
        [lax.dynamic_index_in_dim(shared, ens_pos ^ i, 0, False) for i in range(ens_count)], axis=0
    )
    param_anomalies = (all_params - hdot(same, all_params) / per_group) * spread
    everyone = lax.all_gather(predicted, "ens", axis=0, tiled=True)
    total_obs = obs_variance.shape[0] * slab_count
    products = pl.pallas_call(
        functools.partial(products_kernel, float(total_obs), per_group, spread),
        out_shape=jax.ShapeDtypeStruct((members, members + local_members), jnp.float32),
        compiler_params=pltpu.CompilerParams(vmem_limit_bytes=VMEM_LIMIT),
        name="products",
    )(everyone, predicted, obs_values, obs_variance[None, :], same)
    distance = 1
    while distance < slab_count:
        pairs = [(i, i ^ distance) for i in range(slab_count)]
        products = products + lax.ppermute(products, "slab", pairs)
        distance *= 2
    updated = pl.pallas_call(
        functools.partial(update_kernel, per_group),
        out_shape=jax.ShapeDtypeStruct(parameters.shape, jnp.float32),
        compiler_params=pltpu.CompilerParams(vmem_limit_bytes=VMEM_LIMIT),
        name="update",
    )(products[None], same, own_same, rank[None, :], rank[:, None], param_anomalies, parameters)
    return (field, updated)


def solution(mesh):
    in_specs = (
        P("ens", "slab", None),
        P(None, "slab", None),
        P("ens", None),
        P("slab"),
        P("ens", "slab"),
        P("slab"),
        P(),
    )
    out_specs = (P("ens", "slab", None), P("ens", None))
    return jax.shard_map(local, mesh=mesh, in_specs=in_specs, out_specs=out_specs, check_vma=False)
```

```python
import functools
import math

import jax
import jax.numpy as jnp
from jax import lax
from jax.experimental import pallas as pl
from jax.experimental.pallas import tpu as pltpu
from jax.sharding import PartitionSpec as P

STEPS = 4
GROUPS = 8
HALO = 2 * STEPS
LANES = 128
SUBLANES = 8
ROWS = 16
GROUP = 4
FOLD = 4
PICKED = 128
TILES = 4
FIELD_CALLS = 2
ALL_ROWS = ROWS + 2 * HALO
VMEM_LIMIT = 16 * 1024 * 1024
TALL_LIMIT = 58 * 1024 * 1024
COST_BYTES = 200000
ANYWHERE = pl.BlockSpec(memory_space=pltpu.HBM)
IN_VMEM = pl.BlockSpec(memory_space=pltpu.VMEM)
IN_SMEM = pl.BlockSpec(memory_space=pltpu.SMEM)


def hdot(left, right):
    return jnp.dot(left, right, precision=lax.Precision.HIGHEST, preferred_element_type=jnp.float32)


def limited(left, right):
    return jnp.minimum(jnp.maximum(left, jnp.minimum(right, 0.0)), jnp.maximum(right, 0.0))


def block_at(block):
    return pl.ds(pl.multiple_of(block * LANES, LANES), LANES)


def everywhere(coef, block, place):
    return coef[block, pl.ds(place, SUBLANES, stride=0), :]


def edge_lanes():
    lane = lax.broadcasted_iota(jnp.int32, (SUBLANES, LANES), 1)
    return lane == 0, lane == LANES - 1


def dealt(values, back=False):
    shape = (FOLD * LANES, FOLD * LANES)
    natural = lax.broadcasted_iota(jnp.int32, shape, 1 if back else 0)
    place = lax.broadcasted_iota(jnp.int32, shape, 0 if back else 1)
    moves = natural == FOLD * lax.rem(place, LANES) + lax.div(place, LANES)
    moves = jnp.where(moves, 1.0, 0.0).astype(jnp.bfloat16)
    products = []
    for _ in range(3):
        piece = values.astype(jnp.bfloat16)
        products.append(jnp.dot(piece, moves, preferred_element_type=jnp.float32))
        values = values - piece.astype(jnp.float32)
    return products[0] + (products[1] + products[2])


def stencil(line, speeds):
    d = [line[i + 1] - line[i] for i in range(GROUP + 3)]
    slope = [None] + [limited(d[i - 1], d[i]) for i in range(1, GROUP + 3)]
    twice = [None] + [d[i] + d[i] for i in range(1, GROUP + 2)]
    results = []
    for i in range(2, GROUP + 2):
        speed = speeds[i - 2]
        forward = twice[i - 1] - slope[i - 1]
        backward = twice[i] - slope[i + 1]
        flux = speed * (jnp.where(speed > 0.0, forward, backward) + slope[i])
        results.append((flux, d[i] - d[i - 1]))
    return results


def advance_tile(cell, places, part, parts, source, target, coef, params, blocks):
    start = part * FOLD
    before = lax.rem(part + parts - 1, parts) * FOLD
    after = lax.rem(part + 1, parts) * FOLD
    first, last = edge_lanes()
    own = [
        [source[cell + (i - 2) * blocks + start + p] for p in range(FOLD)] for i in range(GROUP + 4)
    ]
    along_rows = [
        stencil(
            [own[i][p] for i in range(GROUP + 4)],
            [everywhere(coef, start + p, places[i][0]) for i in range(GROUP)],
        )
        for p in range(FOLD)
    ]
    for i in range(GROUP):
        row = own[i + 2]
        here = cell + i * blocks
        left = [
            jnp.where(first, pltpu.roll(source[here + before + p], 1, 1), pltpu.roll(row[p], 1, 1))
            for p in (FOLD - 2, FOLD - 1)
        ]
        right = [
            jnp.where(
                last,
                pltpu.roll(source[here + after + p], LANES - 1, 1),
                pltpu.roll(row[p], LANES - 1, 1),
            )
            for p in (0, 1)
        ]
        along_columns = stencil(
            [*left, *row, *right], [everywhere(coef, start + p, places[i][1]) for p in range(FOLD)]
        )
        for p in range(FOLD):
            flux_x, lap_x = along_rows[p][i]
            flux_y, lap_y = along_columns[p]
            value = row[p] - 0.5 * (flux_x + flux_y)
            value = value + everywhere(coef, start + p, places[i][2]) * (lap_x + lap_y)
            value = value + params[:, block_at(start + p)] * everywhere(coef, start + p, places[i][3])
            target[here + start + p] = value


def advance_group(source, target, row, coef, params, blocks):
    cell = row * blocks
    places = [[coef_row(array, row + i) for array in range(4)] for i in range(GROUP)]
    parts = blocks // FOLD

    @pl.loop(0, parts // TILES)
    def _(some):
        for k in range(TILES):
            advance_tile(
                cell, places, some * TILES + k, parts, source, target, coef, params, blocks
            )


class Copies:
    def __init__(self, sems):
        self.sems, self.used = sems, 0

    def make(self, source, target):
        copy = pltpu.make_async_copy(source, target, self.sems.at[self.used])
        self.used += 1
        assert self.used <= self.sems.shape[0]
        return copy

    def start(self, source, target):
        copy = self.make(source, target)
        copy.start()
        return copy


def region(levels, level, row, blocks):
    return levels[level].at[pl.ds((HALO + row) * blocks, GROUP * blocks)]


def fill_rows(blocks, first_rows, tracer, mixed, staged, sems):
    def copy(block):
        return pltpu.make_async_copy(tracer.at[:, block_at(block)], staged.at[block], sems.at[block])

    @pl.loop(0, blocks)
    def _(block):
        copy(block).start()

    lines = len(first_rows) * GROUP * SUBLANES

    @pl.loop(0, blocks // FOLD)
    def _(part):
        for q in range(FOLD):
            block = part * FOLD + q
            copy(block).wait()
            for k, first_row in enumerate(first_rows):
                for row in range(GROUP):
                    line = part * lines + (k * GROUP + row) * SUBLANES
                    mixed[pl.ds(pl.multiple_of(line, SUBLANES), SUBLANES), block_at(q)] = staged[
                        block, pl.ds(first_row + row, SUBLANES, stride=ROWS), :
                    ]


def take_rows(blocks, mixed, outs):
    lines = len(outs) * GROUP * SUBLANES

    @pl.loop(0, blocks // FOLD)
    def _(part):
        for k, out in enumerate(outs):
            for row in range(GROUP):
                line = part * lines + (k * GROUP + row) * SUBLANES
                for p in range(FOLD):
                    out[row * blocks + part * FOLD + p] = mixed[
                        pl.ds(pl.multiple_of(line, SUBLANES), SUBLANES), block_at(p)
                    ]


def outer_rows_kernel(
    blocks, tracer, own_coef, place_of, up, down, up_coef, down_coef, edge, edge_sem, mixed, staged, sems
):
    copy = pltpu.make_async_copy(own_coef.at[place_of[0]], edge, edge_sem)
    copy.start()
    fill_rows(blocks, (0, ROWS - GROUP), tracer, mixed, staged, sems)
    copy.wait()
    parts = blocks // FOLD
    field_lines = parts * 2 * GROUP * SUBLANES
    width = FOLD * LANES
    for part in range(parts):
        mixed[field_lines + part * ROWS : field_lines + (part + 1) * ROWS, :] = edge[
            :, part * width : (part + 1) * width
        ]
    mixed[...] = dealt(mixed[...])
    take_rows(blocks, mixed, (down, up))
    for part in range(parts):
        line = field_lines + part * ROWS
        for p in range(FOLD):
            down_coef[part * FOLD + p] = mixed[line : line + HALO, block_at(p)]
            up_coef[part * FOLD + p] = mixed[line + ROWS - HALO : line + ROWS, block_at(p)]


def inner_rows_kernel(
    blocks, tracer, own_coef, params, outer, low, high, by_block, dealt_params, whole, coef_sem, mixed,
    staged, sems,
):
    copy = pltpu.make_async_copy(own_coef, whole, coef_sem)
    copy.start()
    fill_rows(blocks, (GROUP, ROWS - 2 * GROUP), tracer, mixed, staged, sems)
    copy.wait()
    parts = blocks // FOLD
    coef_lines = parts * 2 * GROUP * SUBLANES
    param_lines = coef_lines + parts * 4 * ROWS
    width = FOLD * LANES
    for part in range(parts):
        at = slice(part * width, (part + 1) * width)
        for array in range(4):
            line = coef_lines + (part * 4 + array) * ROWS
            mixed[line : line + ROWS, :] = whole[array, :, at]
        line = param_lines + part * SUBLANES
        mixed[line : line + SUBLANES, :] = params[:, at]
    mixed[...] = dealt(mixed[...])
    take_rows(blocks, mixed, (low, high))
    for part in range(parts):
        line = coef_lines + part * 4 * ROWS
        for p in range(FOLD):
            block = part * FOLD + p
            by_block[block] = mixed[line : line + 4 * ROWS, block_at(p)]
            dealt_params[:, block_at(block)] = mixed[
                param_lines + part * SUBLANES : param_lines + (part + 1) * SUBLANES, block_at(p)
            ]


def interior_kernel(blocks, own0, own1, own2, own3, own_coef, params, *rest):
    outs, (*levels, coef, sems) = rest[:5], rest[5:]
    copies = Copies(sems)
    waits = [
        copies.start(own, region(levels, 0, GROUP * i, blocks))
        for i, own in enumerate((own0, own1, own2, own3))
    ]
    waits.append(copies.start(own_coef, coef.at[:, 0 : 4 * ROWS]))
    for copy in waits:
        copy.wait()

    for level, start, count in ((0, 2, 3), (1, 4, 2), (2, 6, 1)):
        @pl.loop(0, count)
        def _(i):
            row = start + HALO + GROUP * i
            advance_group(levels[level], levels[level + 1], row, coef, params, blocks)

    waits = [
        copies.start(region(levels, level, row, blocks), out)
        for out, (level, row) in zip(outs, ((1, 2), (1, 10), (2, 4), (2, 8), (3, 6)))
    ]
    for copy in waits:
        copy.wait()


def edge_steps(outer, blocks, waits, sends, levels, coef, params):
    for level in range(STEPS):
        for copy in waits[level]:
            copy.wait()
        low, high = 2 * level - outer, ROWS + outer - GROUP - 2 * level

        @pl.loop(0, 2)
        def _(side):
            row = low + HALO + side * (high - low)
            advance_group(levels[level], levels[level + 1], row, coef, params, blocks)

        for copy in sends[2 * level : 2 * level + 2]:
            copy.start()


def coef_row(array, row):
    own = array * ROWS + row - HALO
    low = 4 * ROWS + 2 * HALO * array + row
    high = 4 * ROWS + 2 * HALO * array + row - ROWS
    return jnp.where(row < HALO, low, jnp.where(row < HALO + ROWS, own, high))


def load_coef(copies, own_coef, pair, other, place_of, coef):
    waits = [copies.start(own_coef, coef.at[:, 0 : 4 * ROWS])]
    for number, source in enumerate((pair.at[0], pair.at[1], other.at[0], other.at[1])):
        array = jnp.bitwise_xor(place_of[0], number)
        for side in range(2):
            first = 4 * ROWS + 2 * HALO * array + HALO * side
            waits.append(copies.start(source.at[side], coef.at[:, pl.ds(first, HALO)]))
    return waits


def middle_kernel(blocks, *refs):
    sources, refs = refs[:9], refs[9:]
    own_coef, pair, other, params, place_of = refs[:5]
    outs, (*levels, coef, sems) = refs[5:13], refs[13:]
    copies = Copies(sems)
    places = ((0, -4), (0, 0), (0, 12), (0, 16), (1, 2), (1, 10), (2, 4), (2, 8), (3, 6))
    waits = [[] for _ in range(STEPS)]
    for source, (level, row) in zip(sources, places):
        waits[level].append(copies.start(source, region(levels, level, row, blocks)))
    waits[0] += load_coef(copies, own_coef, pair, other, place_of, coef)
    places = [(k + 1, row) for k in range(STEPS) for row in (2 * k - 2, ROWS + 2 - GROUP - 2 * k)]
    sends = [
        copies.make(region(levels, level, row, blocks), out)
        for out, (level, row) in zip(outs, places)
    ]
    edge_steps(2, blocks, waits, sends, levels, coef, params)
    for copy in sends:
        copy.wait()


def last_kernel(blocks, *refs):
    sources, refs = refs[:12], refs[12:]
    own_coef, pair, other, params, place_of, cell_of, shift_of = refs[:7]
    low_out, high_out, predicted, *levels, coef, sems = refs[7:]
    copies = Copies(sems)
    places = (
        (0, -8), (0, -4), (0, 16), (0, 20),
        (1, -2), (1, 14), (2, 0), (2, 12), (3, 2), (3, 10), (4, 4), (4, 8),
    )
    waits = [[] for _ in range(STEPS + 1)]
    for source, (level, row) in zip(sources, places):
        waits[level].append(copies.start(source, region(levels, level, row, blocks)))
    waits[0] += load_coef(copies, own_coef, pair, other, place_of, coef)
    edge_steps(6, blocks, waits, (), levels, coef, params)
    for copy in waits[STEPS]:
        copy.wait()
    sends = [
        copies.start(region(levels, STEPS, row, blocks), out)
        for row, out in ((0, low_out), (ROWS - GROUP, high_out))
    ]
    lane = lax.broadcasted_iota(jnp.int32, (SUBLANES, LANES), 1)

    @pl.loop(0, predicted.shape[1] // LANES)
    def _(block):
        base = block * LANES

        def some(part, found):
            for i in range(PICKED):
                o = part * PICKED + i
                value = pltpu.roll(levels[STEPS][cell_of[base + o]], shift_of[base + o], 1)
                found = jnp.where(lane == o, value, found)
            return found

        empty = jnp.zeros((SUBLANES, LANES), jnp.float32)
        predicted[:, block_at(block)] = lax.fori_loop(0, LANES // PICKED, some, empty)

    for copy in sends:
        copy.wait()


def field_kernel(blocks, first_part, count, *refs):
    sources, refs = refs[: ROWS // GROUP], refs[-6:]
    out, cells, mixed, staged, sems, out_sems = refs
    copies = Copies(sems)
    width = count * FOLD
    waits = [
        copies.start(
            source.at[pl.ds(row * blocks + first_part * FOLD, width)],
            cells.at[pl.ds((i * GROUP + row) * width, width)],
        )
        for i, source in enumerate(sources)
        for row in range(GROUP)
    ]
    for copy in waits:
        copy.wait()
    lines = ROWS * SUBLANES

    def line_at(part, row):
        return pl.ds(pl.multiple_of(part * lines + row * SUBLANES, SUBLANES), SUBLANES)

    @pl.loop(0, count)
    def _(part):
        for row in range(ROWS):
            for p in range(FOLD):
                mixed[line_at(part, row), block_at(p)] = cells[row * width + part * FOLD + p]

    mixed[...] = dealt(mixed[...], back=True)

    def out_copy(block):
        return pltpu.make_async_copy(
            staged.at[block], out.at[:, block_at(first_part * FOLD + block)], out_sems.at[block]
        )

    @pl.loop(0, count)
    def _(part):
        for q in range(FOLD):
            block = part * FOLD + q
            for row in range(ROWS):
                staged[block, pl.ds(row, SUBLANES, stride=ROWS), :] = mixed[
                    line_at(part, row), block_at(q)
                ]
            out_copy(block).start()

    @pl.loop(0, width)
    def _(block):
        out_copy(block).wait()


def scratch(columns, *more):
    blocks = columns // LANES
    return [
        *[pltpu.VMEM((ALL_ROWS * blocks, SUBLANES, LANES), jnp.float32)] * (STEPS + 1),
        pltpu.VMEM((blocks, 4 * ALL_ROWS, LANES), jnp.float32),
        *more,
    ]


def kernel_call(body, name, outs, specs, out_specs, scratches, cost, operands, aliases={}):
    return pl.pallas_call(
        body,
        out_shape=tuple(jax.ShapeDtypeStruct(shape, jnp.float32) for shape in outs),
        in_specs=specs,
        out_specs=out_specs,
        scratch_shapes=scratches,
        compiler_params=pltpu.CompilerParams(vmem_limit_bytes=TALL_LIMIT),
        cost_estimate=pl.CostEstimate(flops=0, bytes_accessed=cost * COST_BYTES, transcendentals=0),
        input_output_aliases=aliases,
        name=name,
    )(*operands)


def row_groups(tracer, coefficients, params, place_of):
    members, rows, columns = tracer.shape
    if members != SUBLANES or rows != ROWS or columns % (FOLD * LANES):
        raise ValueError("block shape")
    blocks = columns // LANES
    parts = blocks // FOLD
    flat = tracer.reshape(members * rows, columns)
    dma = pltpu.SemaphoreType.DMA
    staged = [pltpu.VMEM((blocks, members * rows, LANES), jnp.float32), dma((blocks,))]

    def mixed(lines):
        return pltpu.VMEM((parts * lines, FOLD * LANES), jnp.float32)

    group, edge = (GROUP * blocks, members, LANES), (blocks, HALO, LANES)
    up, down, up_coef, down_coef = kernel_call(
        functools.partial(outer_rows_kernel, blocks), "outer_rows",
        [group, group, edge, edge], [ANYWHERE, ANYWHERE, IN_SMEM], (IN_VMEM,) * 4,
        [pltpu.VMEM((rows, columns), jnp.float32), dma, mixed(2 * GROUP * members + rows)] + staged, 3,
        [flat, coefficients, place_of],
    )
    low, high, by_block, dealt_params = kernel_call(
        functools.partial(inner_rows_kernel, blocks), "inner_rows",
        [group, group, (blocks, 4 * rows, LANES), params.shape],
        [ANYWHERE, ANYWHERE, IN_VMEM, ANYWHERE], (IN_VMEM,) * 4,
        [
            pltpu.VMEM((4, rows, columns), jnp.float32), dma,
            mixed(2 * GROUP * members + 4 * rows + members),
        ] + staged, 3,
        [flat, coefficients, params, up],
    )
    return (down, low, high, up), (up_coef, down_coef), by_block, dealt_params


def transport(shape, own, low0, high0, own_coef, pair, other, params, place_of, obs_index, halos, share_params):
    members, rows, columns = shape
    blocks = columns // LANES
    group = (GROUP * blocks, members, LANES)
    flat = (members * rows, columns)
    dma = pltpu.SemaphoreType.DMA
    inner = kernel_call(
        functools.partial(interior_kernel, blocks), "interior",
        [group] * 5, [ANYWHERE] * 5 + [IN_VMEM], (ANYWHERE,) * 5,
        scratch(columns, dma((16,))), 8, [*own, own_coef, params],
    )
    upper, lower, *_ = lax.optimization_barrier((own[2], own[1], inner[0], pair))
    low1, high1 = halos(upper, lower)
    first = kernel_call(
        functools.partial(middle_kernel, blocks), "edge_first",
        [group] * 8, [ANYWHERE] * 12 + [IN_VMEM, IN_SMEM], (ANYWHERE,) * 8,
        scratch(columns, dma((29,))), 10,
        [low0, own[0], own[3], high0, *inner, own_coef, pair, other, params, place_of],
    )
    high1, *all_params = lax.optimization_barrier((high1, *share_params(inner[0])))
    obs_row, obs_col = obs_index // columns, obs_index % columns
    width = FOLD * LANES
    obs_block = obs_col // width * FOLD + obs_col % FOLD
    cell_of = (HALO + obs_row) * blocks + obs_block
    lane_of = obs_col % width // FOLD
    shift_of = (jnp.arange(obs_index.shape[0], dtype=jnp.int32) - lane_of) % LANES
    low4, high4, predicted = kernel_call(
        functools.partial(last_kernel, blocks), "edge_last",
        [group, group, (members, obs_index.shape[0])],
        [ANYWHERE] * 15 + [IN_VMEM] + [IN_SMEM] * 3, (ANYWHERE, ANYWHERE, IN_VMEM),
        scratch(columns, dma((31,))), 15,
        [low1, low0, high0, high1, *first, own_coef, pair, other, params, place_of, cell_of, shift_of],
    )

    def write_field(index, field):
        parts = blocks // FOLD
        first_part = parts * index // FIELD_CALLS
        count = parts * (index + 1) // FIELD_CALLS - first_part
        width = count * FOLD
        previous = [] if field is None else [field]
        return kernel_call(
            functools.partial(field_kernel, blocks, first_part, count), "field_%d" % index,
            [flat], [ANYWHERE] * (4 + len(previous)), (ANYWHERE,),
            [
                pltpu.VMEM((rows * width, members, LANES), jnp.float32),
                pltpu.VMEM((members * rows * count, FOLD * LANES), jnp.float32),
                pltpu.VMEM((width, members * rows, LANES), jnp.float32),
                dma((rows,)), dma((width,)),
            ],
            4, [low4, first[6], first[7], high4, *previous], {4: 0} if previous else {},
        )[0]

    return write_field, predicted, all_params


def products_kernel(total_obs, per_group, spread, pair, other, values, variance, same, out):
    weight = 1.0 / (variance[...] * total_obs)
    predicted = jnp.concatenate([pair[0], pair[1], other[0], other[1]], axis=0)
    innovation = (values[...] - pair[0]) * weight
    anomalies = (predicted - hdot(same[...], predicted) / per_group) * spread
    right = jnp.concatenate([anomalies * weight, innovation], axis=0)
    out[...] = lax.dot_general(
        anomalies,
        right,
        (((1,), (1,)), ((), ())),
        precision=lax.Precision.HIGHEST,
        preferred_element_type=jnp.float32,
    )


def update_kernel(per_group, summands, same, own_same, rank_row, rank_col, anomalies, own, out):
    members = same.shape[0]
    total = summands[0]
    for index in range(1, summands.shape[0]):
        total = total + summands[index]
    together = same[...]
    row = lax.broadcasted_iota(jnp.int32, (members, members), 0)
    col = lax.broadcasted_iota(jnp.int32, (members, members), 1)
    system = jnp.where(row == col, 1.0, 0.0) + together * total[:, 0:members]
    right = own_same[...] * total[:, members:]
    for pivot in range(per_group):
        pick = jnp.where(rank_row[...] == pivot, together, 0.0)
        pivot_system = hdot(pick, system)
        pivot_right = hdot(pick, right)
        pivot_value = jnp.sum(pick * pivot_system, axis=1, keepdims=True)
        factor = jnp.sum(pick * system, axis=1, keepdims=True)
        is_pivot = rank_col[...] == pivot
        scale = 1.0 / pivot_value
        scaled_system, scaled_right = pivot_system * scale, pivot_right * scale
        system = jnp.where(is_pivot, scaled_system, system - factor * scaled_system)
        right = jnp.where(is_pivot, scaled_right, right - factor * scaled_right)
    change = lax.dot_general(
        right,
        anomalies[...],
        (((0,), (0,)), ((), ())),
        precision=lax.Precision.HIGHEST,
        preferred_element_type=jnp.float32,
    )
    out[...] = own[...] + change


def local(tracer, coefficients, parameters, obs_index, obs_values, obs_variance, member_group):
    local_members, rows, columns = tracer.shape
    ens_pos = lax.axis_index("ens")
    ens_count = lax.axis_size("ens")
    slab_count = lax.axis_size("slab")
    if ens_count != 4 or coefficients.shape[0] != 4 or slab_count & (slab_count - 1):
        raise ValueError("mesh shape")
    forward = [(i, i + 1) for i in range(slab_count - 1)]
    backward = [(target, source) for source, target in forward]

    def next_core(value):
        return lax.ppermute(value, "ens", [(i, i ^ 1) for i in range(ens_count)])

    def next_chip(value):
        return lax.ppermute(value, "ens", [(i, i ^ 2) for i in range(ens_count)])

    def over_ens(mine):
        pair = jnp.stack([mine, next_core(mine)])
        return pair, next_chip(pair)

    def halos(upper, lower):
        return lax.ppermute(upper, "slab", forward), lax.ppermute(lower, "slab", backward)

    place_of = jnp.reshape(ens_pos, (1,))
    own, coef_edges, own_coef, dealt_params = row_groups(
        tracer, coefficients, parameters, place_of
    )
    low0, high0 = halos(own[3], own[0])

    edge_low, edge_high = halos(*coef_edges)
    pair, other = over_ens(jnp.stack([edge_low, edge_high]))

    members = member_group.shape[0]
    per_group = members // GROUPS
    spread = 1.0 / math.sqrt(per_group - 1)
    blocks_of = member_group.reshape(ens_count, local_members)
    group_of = jnp.concatenate(
        [lax.dynamic_index_in_dim(blocks_of, ens_pos ^ i, 0, False) for i in range(ens_count)]
    )
    same_bool = group_of[:, None] == group_of[None, :]
    same = same_bool.astype(jnp.float32)
    earlier = jnp.arange(members)[None, :] < jnp.arange(members)[:, None]
    rank = jnp.sum((same_bool & earlier).astype(jnp.int32), axis=1)

    def share_params(after):
        later, _ = lax.optimization_barrier((parameters, after))
        return over_ens(later)

    write_field, predicted, all_params = transport(
        tracer.shape, own, low0, high0,
        own_coef, pair, other, dealt_params, place_of, obs_index, halos, share_params,
    )
    all_params = jnp.concatenate(all_params, axis=0).reshape(members, columns)
    param_anomalies = (all_params - hdot(same, all_params) / per_group) * spread

    near = jnp.stack([predicted, next_core(predicted)])
    field = write_field(0, None)
    near, field = lax.optimization_barrier((near, field))
    far = next_chip(near)
    field = write_field(1, field)
    far, field = lax.optimization_barrier((far, field))
    total_obs = obs_variance.shape[0] * slab_count
    products = pl.pallas_call(
        functools.partial(products_kernel, float(total_obs), per_group, spread),
        out_shape=jax.ShapeDtypeStruct((members, members + local_members), jnp.float32),
        compiler_params=pltpu.CompilerParams(vmem_limit_bytes=VMEM_LIMIT),
        name="products",
    )(near, far, obs_values, obs_variance[None, :], same)
    distance = 1
    while distance < slab_count:
        pairs = [(i, i ^ distance) for i in range(slab_count)]
        products = products + lax.ppermute(products, "slab", pairs)
        distance *= 2
    updated = pl.pallas_call(
        functools.partial(update_kernel, per_group),
        out_shape=jax.ShapeDtypeStruct(parameters.shape, jnp.float32),
        compiler_params=pltpu.CompilerParams(vmem_limit_bytes=VMEM_LIMIT),
        name="update",
    )(
        products[None], same, same[:, :local_members], rank[None, :], rank[:, None],
        param_anomalies, parameters,
    )
    return (field.reshape(tracer.shape), updated)


def solution(mesh):
    in_specs = (
        P("ens", "slab", None),
        P(None, "slab", None),
        P("ens", None),
        P("slab"),
        P("ens", "slab"),
        P("slab"),
        P(),
    )
    out_specs = (P("ens", "slab", None), P("ens", None))
    return jax.shard_map(local, mesh=mesh, in_specs=in_specs, out_specs=out_specs, check_vma=False)
```

```python
import functools
import math

import jax
import jax.numpy as jnp
from jax import lax
from jax.experimental import pallas as pl
from jax.experimental.pallas import tpu as pltpu
from jax.sharding import PartitionSpec as P

STEPS = 4
GROUPS = 8
HALO = 2 * STEPS
LANES = 128
SUBLANES = 8
ROWS = 16
GROUP = 4
FOLD = 4
PICKED = 128
TILES = 4
FIELD_CALLS = 2
ALL_ROWS = ROWS + 2 * HALO
VMEM_LIMIT = 16 * 1024 * 1024
TALL_LIMIT = 58 * 1024 * 1024
COST_BYTES = 200000
ANYWHERE = pl.BlockSpec(memory_space=pltpu.HBM)
IN_VMEM = pl.BlockSpec(memory_space=pltpu.VMEM)
IN_SMEM = pl.BlockSpec(memory_space=pltpu.SMEM)


def hdot(left, right):
    return jnp.dot(left, right, precision=lax.Precision.HIGHEST, preferred_element_type=jnp.float32)


def limited(left, right):
    return jnp.minimum(jnp.maximum(left, jnp.minimum(right, 0.0)), jnp.maximum(right, 0.0))


def block_at(block):
    return pl.ds(pl.multiple_of(block * LANES, LANES), LANES)


def everywhere(coef, block, place):
    return coef[block, pl.ds(place, SUBLANES, stride=0), :]


def edge_lanes():
    lane = lax.broadcasted_iota(jnp.int32, (SUBLANES, LANES), 1)
    return lane == 0, lane == LANES - 1


def dealt(values, back=False):
    shape = (FOLD * LANES, FOLD * LANES)
    natural = lax.broadcasted_iota(jnp.int32, shape, 1 if back else 0)
    place = lax.broadcasted_iota(jnp.int32, shape, 0 if back else 1)
    moves = natural == FOLD * lax.rem(place, LANES) + lax.div(place, LANES)
    moves = jnp.where(moves, 1.0, 0.0).astype(jnp.bfloat16)
    products = []
    for _ in range(3):
        piece = values.astype(jnp.bfloat16)
        products.append(jnp.dot(piece, moves, preferred_element_type=jnp.float32))
        values = values - piece.astype(jnp.float32)
    return products[0] + (products[1] + products[2])


def stencil(line, speeds):
    d = [line[i + 1] - line[i] for i in range(GROUP + 3)]
    slope = [None] + [limited(d[i - 1], d[i]) for i in range(1, GROUP + 3)]
    twice = [None] + [d[i] + d[i] for i in range(1, GROUP + 2)]
    results = []
    for i in range(2, GROUP + 2):
        speed = speeds[i - 2]
        forward = twice[i - 1] - slope[i - 1]
        backward = twice[i] - slope[i + 1]
        flux = speed * (jnp.where(speed > 0.0, forward, backward) + slope[i])
        results.append((flux, d[i] - d[i - 1]))
    return results


def advance_tile(cell, places, part, parts, source, target, coef, params, blocks):
    start = part * FOLD
    before = lax.rem(part + parts - 1, parts) * FOLD
    after = lax.rem(part + 1, parts) * FOLD
    first, last = edge_lanes()
    own = [
        [source[cell + (i - 2) * blocks + start + p] for p in range(FOLD)] for i in range(GROUP + 4)
    ]
    along_rows = [
        stencil(
            [own[i][p] for i in range(GROUP + 4)],
            [everywhere(coef, start + p, places[i][0]) for i in range(GROUP)],
        )
        for p in range(FOLD)
    ]
    for i in range(GROUP):
        row = own[i + 2]
        here = cell + i * blocks
        left = [
            jnp.where(first, pltpu.roll(source[here + before + p], 1, 1), pltpu.roll(row[p], 1, 1))
            for p in (FOLD - 2, FOLD - 1)
        ]
        right = [
            jnp.where(
                last,
                pltpu.roll(source[here + after + p], LANES - 1, 1),
                pltpu.roll(row[p], LANES - 1, 1),
            )
            for p in (0, 1)
        ]
        along_columns = stencil(
            [*left, *row, *right], [everywhere(coef, start + p, places[i][1]) for p in range(FOLD)]
        )
        for p in range(FOLD):
            flux_x, lap_x = along_rows[p][i]
            flux_y, lap_y = along_columns[p]
            value = row[p] - 0.5 * (flux_x + flux_y)
            value = value + everywhere(coef, start + p, places[i][2]) * (lap_x + lap_y)
            value = value + params[:, block_at(start + p)] * everywhere(coef, start + p, places[i][3])
            target[here + start + p] = value


def advance_group(source, target, row, coef, params, blocks):
    cell = row * blocks
    places = [[coef_row(array, row + i) for array in range(4)] for i in range(GROUP)]
    parts = blocks // FOLD

    @pl.loop(0, parts // TILES)
    def _(some):
        for k in range(TILES):
            advance_tile(
                cell, places, some * TILES + k, parts, source, target, coef, params, blocks
            )


class Copies:
    def __init__(self, sems):
        self.sems, self.used = sems, 0

    def make(self, source, target):
        copy = pltpu.make_async_copy(source, target, self.sems.at[self.used])
        self.used += 1
        assert self.used <= self.sems.shape[0]
        return copy

    def start(self, source, target):
        copy = self.make(source, target)
        copy.start()
        return copy


def region(levels, level, row, blocks):
    return levels[level].at[pl.ds((HALO + row) * blocks, GROUP * blocks)]


def fill_rows(blocks, first_rows, tracer, mixed, staged, sems):
    def copy(block):
        return pltpu.make_async_copy(tracer.at[:, block_at(block)], staged.at[block], sems.at[block])

    @pl.loop(0, blocks)
    def _(block):
        copy(block).start()

    lines = len(first_rows) * GROUP * SUBLANES

    @pl.loop(0, blocks // FOLD)
    def _(part):
        for q in range(FOLD):
            block = part * FOLD + q
            copy(block).wait()
            for k, first_row in enumerate(first_rows):
                for row in range(GROUP):
                    line = part * lines + (k * GROUP + row) * SUBLANES
                    mixed[pl.ds(pl.multiple_of(line, SUBLANES), SUBLANES), block_at(q)] = staged[
                        block, pl.ds(first_row + row, SUBLANES, stride=ROWS), :
                    ]


def take_rows(blocks, mixed, outs):
    lines = len(outs) * GROUP * SUBLANES

    @pl.loop(0, blocks // FOLD)
    def _(part):
        for k, out in enumerate(outs):
            for row in range(GROUP):
                line = part * lines + (k * GROUP + row) * SUBLANES
                for p in range(FOLD):
                    out[row * blocks + part * FOLD + p] = mixed[
                        pl.ds(pl.multiple_of(line, SUBLANES), SUBLANES), block_at(p)
                    ]


def outer_rows_kernel(
    blocks, tracer, own_coef, place_of, up, down, up_coef, down_coef, edge, edge_sem, mixed, staged, sems
):
    copy = pltpu.make_async_copy(own_coef.at[place_of[0]], edge, edge_sem)
    copy.start()
    fill_rows(blocks, (0, ROWS - GROUP), tracer, mixed, staged, sems)
    copy.wait()
    parts = blocks // FOLD
    field_lines = parts * 2 * GROUP * SUBLANES
    width = FOLD * LANES
    for part in range(parts):
        mixed[field_lines + part * ROWS : field_lines + (part + 1) * ROWS, :] = edge[
            :, part * width : (part + 1) * width
        ]
    mixed[...] = dealt(mixed[...])
    take_rows(blocks, mixed, (down, up))
    for part in range(parts):
        line = field_lines + part * ROWS
        for p in range(FOLD):
            down_coef[part * FOLD + p] = mixed[line : line + HALO, block_at(p)]
            up_coef[part * FOLD + p] = mixed[line + ROWS - HALO : line + ROWS, block_at(p)]


def inner_rows_kernel(
    blocks, tracer, own_coef, params, outer, low, high, by_block, dealt_params, whole, coef_sem, mixed,
    staged, sems,
):
    copy = pltpu.make_async_copy(own_coef, whole, coef_sem)
    copy.start()
    fill_rows(blocks, (GROUP, ROWS - 2 * GROUP), tracer, mixed, staged, sems)
    copy.wait()
    parts = blocks // FOLD
    coef_lines = parts * 2 * GROUP * SUBLANES
    param_lines = coef_lines + parts * 4 * ROWS
    width = FOLD * LANES
    for part in range(parts):
        at = slice(part * width, (part + 1) * width)
        for array in range(4):
            line = coef_lines + (part * 4 + array) * ROWS
            mixed[line : line + ROWS, :] = whole[array, :, at]
        line = param_lines + part * SUBLANES
        mixed[line : line + SUBLANES, :] = params[:, at]
    mixed[...] = dealt(mixed[...])
    take_rows(blocks, mixed, (low, high))
    for part in range(parts):
        line = coef_lines + part * 4 * ROWS
        for p in range(FOLD):
            block = part * FOLD + p
            by_block[block] = mixed[line : line + 4 * ROWS, block_at(p)]
            dealt_params[:, block_at(block)] = mixed[
                param_lines + part * SUBLANES : param_lines + (part + 1) * SUBLANES, block_at(p)
            ]


def interior_kernel(blocks, own0, own1, own2, own3, own_coef, params, *rest):
    outs, (*levels, coef, sems) = rest[:5], rest[5:]
    copies = Copies(sems)
    waits = [
        copies.start(own, region(levels, 0, GROUP * i, blocks))
        for i, own in enumerate((own0, own1, own2, own3))
    ]
    waits.append(copies.start(own_coef, coef.at[:, 0 : 4 * ROWS]))
    for copy in waits:
        copy.wait()

    for level, start, count in ((0, 2, 3), (1, 4, 2), (2, 6, 1)):
        @pl.loop(0, count)
        def _(i):
            row = start + HALO + GROUP * i
            advance_group(levels[level], levels[level + 1], row, coef, params, blocks)

    waits = [
        copies.start(region(levels, level, row, blocks), out)
        for out, (level, row) in zip(outs, ((1, 2), (1, 10), (2, 4), (2, 8), (3, 6)))
    ]
    for copy in waits:
        copy.wait()


def edge_steps(outer, blocks, waits, sends, levels, coef, params):
    for level in range(STEPS):
        for copy in waits[level]:
            copy.wait()
        low, high = 2 * level - outer, ROWS + outer - GROUP - 2 * level

        @pl.loop(0, 2)
        def _(side):
            row = low + HALO + side * (high - low)
            advance_group(levels[level], levels[level + 1], row, coef, params, blocks)

        for copy in sends[2 * level : 2 * level + 2]:
            copy.start()


def coef_row(array, row):
    own = array * ROWS + row - HALO
    low = 4 * ROWS + 2 * HALO * array + row
    high = 4 * ROWS + 2 * HALO * array + row - ROWS
    return jnp.where(row < HALO, low, jnp.where(row < HALO + ROWS, own, high))


def load_coef(copies, own_coef, pair, other, place_of, coef):
    waits = [copies.start(own_coef, coef.at[:, 0 : 4 * ROWS])]
    for number, source in enumerate((pair.at[0], pair.at[1], other.at[0], other.at[1])):
        array = jnp.bitwise_xor(place_of[0], number)
        for side in range(2):
            first = 4 * ROWS + 2 * HALO * array + HALO * side
            waits.append(copies.start(source.at[side], coef.at[:, pl.ds(first, HALO)]))
    return waits


def middle_kernel(blocks, *refs):
    sources, refs = refs[:9], refs[9:]
    own_coef, pair, other, params, place_of = refs[:5]
    outs, (*levels, coef, sems) = refs[5:13], refs[13:]
    copies = Copies(sems)
    places = ((0, -4), (0, 0), (0, 12), (0, 16), (1, 2), (1, 10), (2, 4), (2, 8), (3, 6))
    waits = [[] for _ in range(STEPS)]
    for source, (level, row) in zip(sources, places):
        waits[level].append(copies.start(source, region(levels, level, row, blocks)))
    waits[0] += load_coef(copies, own_coef, pair, other, place_of, coef)
    places = [(k + 1, row) for k in range(STEPS) for row in (2 * k - 2, ROWS + 2 - GROUP - 2 * k)]
    sends = [
        copies.make(region(levels, level, row, blocks), out)
        for out, (level, row) in zip(outs, places)
    ]
    edge_steps(2, blocks, waits, sends, levels, coef, params)
    for copy in sends:
        copy.wait()


def last_kernel(blocks, *refs):
    sources, refs = refs[:12], refs[12:]
    own_coef, pair, other, params, place_of, cell_of, shift_of = refs[:7]
    low_out, high_out, predicted, *levels, coef, sems = refs[7:]
    copies = Copies(sems)
    places = (
        (0, -8), (0, -4), (0, 16), (0, 20),
        (1, -2), (1, 14), (2, 0), (2, 12), (3, 2), (3, 10), (4, 4), (4, 8),
    )
    waits = [[] for _ in range(STEPS + 1)]
    for source, (level, row) in zip(sources, places):
        waits[level].append(copies.start(source, region(levels, level, row, blocks)))
    waits[0] += load_coef(copies, own_coef, pair, other, place_of, coef)
    edge_steps(6, blocks, waits, (), levels, coef, params)
    for copy in waits[STEPS]:
        copy.wait()
    sends = [
        copies.start(region(levels, STEPS, row, blocks), out)
        for row, out in ((0, low_out), (ROWS - GROUP, high_out))
    ]
    lane = lax.broadcasted_iota(jnp.int32, (SUBLANES, LANES), 1)

    @pl.loop(0, predicted.shape[1] // LANES)
    def _(block):
        base = block * LANES

        def some(part, found):
            for i in range(PICKED):
                o = part * PICKED + i
                value = pltpu.roll(levels[STEPS][cell_of[base + o]], shift_of[base + o], 1)
                found = jnp.where(lane == o, value, found)
            return found

        empty = jnp.zeros((SUBLANES, LANES), jnp.float32)
        predicted[:, block_at(block)] = lax.fori_loop(0, LANES // PICKED, some, empty)

    for copy in sends:
        copy.wait()


def field_kernel(blocks, first_part, count, *refs):
    sources, refs = refs[: ROWS // GROUP], refs[-6:]
    out, cells, mixed, staged, sems, out_sems = refs
    copies = Copies(sems)
    width = count * FOLD
    waits = [
        copies.start(
            source.at[pl.ds(row * blocks + first_part * FOLD, width)],
            cells.at[pl.ds((i * GROUP + row) * width, width)],
        )
        for i, source in enumerate(sources)
        for row in range(GROUP)
    ]
    for copy in waits:
        copy.wait()
    lines = ROWS * SUBLANES

    def line_at(part, row):
        return pl.ds(pl.multiple_of(part * lines + row * SUBLANES, SUBLANES), SUBLANES)

    @pl.loop(0, count)
    def _(part):
        for row in range(ROWS):
            for p in range(FOLD):
                mixed[line_at(part, row), block_at(p)] = cells[row * width + part * FOLD + p]

    mixed[...] = dealt(mixed[...], back=True)

    def out_copy(block):
        return pltpu.make_async_copy(
            staged.at[block], out.at[:, block_at(first_part * FOLD + block)], out_sems.at[block]
        )

    @pl.loop(0, count)
    def _(part):
        for q in range(FOLD):
            block = part * FOLD + q
            for row in range(ROWS):
                staged[block, pl.ds(row, SUBLANES, stride=ROWS), :] = mixed[
                    line_at(part, row), block_at(q)
                ]
            out_copy(block).start()

    @pl.loop(0, width)
    def _(block):
        out_copy(block).wait()


def scratch(columns, *more):
    blocks = columns // LANES
    return [
        *[pltpu.VMEM((ALL_ROWS * blocks, SUBLANES, LANES), jnp.float32)] * (STEPS + 1),
        pltpu.VMEM((blocks, 4 * ALL_ROWS, LANES), jnp.float32),
        *more,
    ]


def kernel_call(body, name, outs, specs, out_specs, scratches, cost, operands, aliases={}):
    return pl.pallas_call(
        body,
        out_shape=tuple(jax.ShapeDtypeStruct(shape, jnp.float32) for shape in outs),
        in_specs=specs,
        out_specs=out_specs,
        scratch_shapes=scratches,
        compiler_params=pltpu.CompilerParams(vmem_limit_bytes=TALL_LIMIT),
        cost_estimate=pl.CostEstimate(flops=0, bytes_accessed=cost * COST_BYTES, transcendentals=0),
        input_output_aliases=aliases,
        name=name,
    )(*operands)


def row_groups(tracer, coefficients, params, place_of):
    members, rows, columns = tracer.shape
    if members != SUBLANES or rows != ROWS or columns % (FOLD * LANES):
        raise ValueError("block shape")
    blocks = columns // LANES
    parts = blocks // FOLD
    flat = tracer.reshape(members * rows, columns)
    dma = pltpu.SemaphoreType.DMA
    staged = [pltpu.VMEM((blocks, members * rows, LANES), jnp.float32), dma((blocks,))]

    def mixed(lines):
        return pltpu.VMEM((parts * lines, FOLD * LANES), jnp.float32)

    group, edge = (GROUP * blocks, members, LANES), (blocks, HALO, LANES)
    up, down, up_coef, down_coef = kernel_call(
        functools.partial(outer_rows_kernel, blocks), "outer_rows",
        [group, group, edge, edge], [ANYWHERE, ANYWHERE, IN_SMEM], (IN_VMEM,) * 4,
        [pltpu.VMEM((rows, columns), jnp.float32), dma, mixed(2 * GROUP * members + rows)] + staged, 3,
        [flat, coefficients, place_of],
    )
    low, high, by_block, dealt_params = kernel_call(
        functools.partial(inner_rows_kernel, blocks), "inner_rows",
        [group, group, (blocks, 4 * rows, LANES), params.shape],
        [ANYWHERE, ANYWHERE, IN_VMEM, ANYWHERE], (IN_VMEM,) * 4,
        [
            pltpu.VMEM((4, rows, columns), jnp.float32), dma,
            mixed(2 * GROUP * members + 4 * rows + members),
        ] + staged, 3,
        [flat, coefficients, params, up],
    )
    return (down, low, high, up), (up_coef, down_coef), by_block, dealt_params


def transport(shape, own, low0, high0, own_coef, pair, other, params, place_of, obs_index, halos, share_params):
    members, rows, columns = shape
    blocks = columns // LANES
    group = (GROUP * blocks, members, LANES)
    flat = (members * rows, columns)
    dma = pltpu.SemaphoreType.DMA
    inner = kernel_call(
        functools.partial(interior_kernel, blocks), "interior",
        [group] * 5, [ANYWHERE] * 5 + [IN_VMEM], (ANYWHERE,) * 5,
        scratch(columns, dma((16,))), 8, [*own, own_coef, params],
    )
    upper, lower, low0, high0, *_ = lax.optimization_barrier(
        (own[2], own[1], low0, high0, inner[0])
    )
    low1, high1 = halos(upper, lower)
    first = kernel_call(
        functools.partial(middle_kernel, blocks), "edge_first",
        [group] * 8, [ANYWHERE] * 12 + [IN_VMEM, IN_SMEM], (ANYWHERE,) * 8,
        scratch(columns, dma((29,))), 10,
        [low0, own[0], own[3], high0, *inner, own_coef, pair, other, params, place_of],
    )
    high1, *all_params = lax.optimization_barrier((high1, *share_params(inner[0])))
    obs_row, obs_col = obs_index // columns, obs_index % columns
    width = FOLD * LANES
    obs_block = obs_col // width * FOLD + obs_col % FOLD
    cell_of = (HALO + obs_row) * blocks + obs_block
    lane_of = obs_col % width // FOLD
    shift_of = (jnp.arange(obs_index.shape[0], dtype=jnp.int32) - lane_of) % LANES
    low4, high4, predicted = kernel_call(
        functools.partial(last_kernel, blocks), "edge_last",
        [group, group, (members, obs_index.shape[0])],
        [ANYWHERE] * 15 + [IN_VMEM] + [IN_SMEM] * 3, (ANYWHERE, ANYWHERE, IN_VMEM),
        scratch(columns, dma((31,))), 15,
        [low1, low0, high0, high1, *first, own_coef, pair, other, params, place_of, cell_of, shift_of],
    )

    def write_field(index, field):
        parts = blocks // FOLD
        first_part = parts * index // FIELD_CALLS
        count = parts * (index + 1) // FIELD_CALLS - first_part
        width = count * FOLD
        previous = [] if field is None else [field]
        return kernel_call(
            functools.partial(field_kernel, blocks, first_part, count), "field_%d" % index,
            [flat], [ANYWHERE] * (4 + len(previous)), (ANYWHERE,),
            [
                pltpu.VMEM((rows * width, members, LANES), jnp.float32),
                pltpu.VMEM((members * rows * count, FOLD * LANES), jnp.float32),
                pltpu.VMEM((width, members * rows, LANES), jnp.float32),
                dma((rows,)), dma((width,)),
            ],
            4, [low4, first[6], first[7], high4, *previous], {4: 0} if previous else {},
        )[0]

    return write_field, predicted, all_params


def products_kernel(total_obs, per_group, spread, pair, other, values, variance, same, out):
    weight = 1.0 / (variance[...] * total_obs)
    predicted = jnp.concatenate([pair[0], pair[1], other[0], other[1]], axis=0)
    innovation = (values[...] - pair[0]) * weight
    anomalies = (predicted - hdot(same[...], predicted) / per_group) * spread
    right = jnp.concatenate([anomalies * weight, innovation], axis=0)
    out[...] = lax.dot_general(
        anomalies,
        right,
        (((1,), (1,)), ((), ())),
        precision=lax.Precision.HIGHEST,
        preferred_element_type=jnp.float32,
    )


def update_kernel(per_group, summands, same, own_same, rank_row, rank_col, anomalies, own, out):
    members = same.shape[0]
    total = summands[0]
    for index in range(1, summands.shape[0]):
        total = total + summands[index]
    together = same[...]
    row = lax.broadcasted_iota(jnp.int32, (members, members), 0)
    col = lax.broadcasted_iota(jnp.int32, (members, members), 1)
    system = jnp.where(row == col, 1.0, 0.0) + together * total[:, 0:members]
    right = own_same[...] * total[:, members:]
    for pivot in range(per_group):
        pick = jnp.where(rank_row[...] == pivot, together, 0.0)
        pivot_system = hdot(pick, system)
        pivot_right = hdot(pick, right)
        pivot_value = jnp.sum(pick * pivot_system, axis=1, keepdims=True)
        factor = jnp.sum(pick * system, axis=1, keepdims=True)
        is_pivot = rank_col[...] == pivot
        scale = 1.0 / pivot_value
        scaled_system, scaled_right = pivot_system * scale, pivot_right * scale
        system = jnp.where(is_pivot, scaled_system, system - factor * scaled_system)
        right = jnp.where(is_pivot, scaled_right, right - factor * scaled_right)
    change = lax.dot_general(
        right,
        anomalies[...],
        (((0,), (0,)), ((), ())),
        precision=lax.Precision.HIGHEST,
        preferred_element_type=jnp.float32,
    )
    out[...] = own[...] + change


def local(tracer, coefficients, parameters, obs_index, obs_values, obs_variance, member_group):
    local_members, rows, columns = tracer.shape
    ens_pos = lax.axis_index("ens")
    ens_count = lax.axis_size("ens")
    slab_count = lax.axis_size("slab")
    if ens_count != 4 or coefficients.shape[0] != 4 or slab_count & (slab_count - 1):
        raise ValueError("mesh shape")
    forward = [(i, i + 1) for i in range(slab_count - 1)]
    backward = [(target, source) for source, target in forward]

    def next_core(value):
        return lax.ppermute(value, "ens", [(i, i ^ 1) for i in range(ens_count)])

    def next_chip(value):
        return lax.ppermute(value, "ens", [(i, i ^ 2) for i in range(ens_count)])

    def over_ens(mine):
        pair = jnp.stack([mine, next_core(mine)])
        return pair, next_chip(pair)

    def halos(upper, lower):
        return lax.ppermute(upper, "slab", forward), lax.ppermute(lower, "slab", backward)

    place_of = jnp.reshape(ens_pos, (1,))
    own, coef_edges, own_coef, dealt_params = row_groups(
        tracer, coefficients, parameters, place_of
    )
    low0, high0 = halos(own[3], own[0])

    edge_low, edge_high = halos(*coef_edges)
    pair, other = over_ens(jnp.stack([edge_low, edge_high]))

    members = member_group.shape[0]
    per_group = members // GROUPS
    spread = 1.0 / math.sqrt(per_group - 1)
    blocks_of = member_group.reshape(ens_count, local_members)
    group_of = jnp.concatenate(
        [lax.dynamic_index_in_dim(blocks_of, ens_pos ^ i, 0, False) for i in range(ens_count)]
    )
    same_bool = group_of[:, None] == group_of[None, :]
    same = same_bool.astype(jnp.float32)
    earlier = jnp.arange(members)[None, :] < jnp.arange(members)[:, None]
    rank = jnp.sum((same_bool & earlier).astype(jnp.int32), axis=1)

    def share_params(after):
        later, _ = lax.optimization_barrier((parameters, after))
        return over_ens(later)

    write_field, predicted, all_params = transport(
        tracer.shape, own, low0, high0,
        own_coef, pair, other, dealt_params, place_of, obs_index, halos, share_params,
    )
    all_params = jnp.concatenate(all_params, axis=0).reshape(members, columns)
    param_anomalies = (all_params - hdot(same, all_params) / per_group) * spread

    near = jnp.stack([predicted, next_core(predicted)])
    field = write_field(0, None)
    near, field = lax.optimization_barrier((near, field))
    far = next_chip(near)
    total_obs = obs_variance.shape[0] * slab_count
    products = pl.pallas_call(
        functools.partial(products_kernel, float(total_obs), per_group, spread),
        out_shape=jax.ShapeDtypeStruct((members, members + local_members), jnp.float32),
        compiler_params=pltpu.CompilerParams(vmem_limit_bytes=VMEM_LIMIT),
        name="products",
    )(near, far, obs_values, obs_variance[None, :], same)
    distance = 1
    while distance < slab_count:
        pairs = [(i, i ^ distance) for i in range(slab_count)]
        arrived = lax.ppermute(products, "slab", pairs)
        if distance == 1:
            arrived, field = lax.optimization_barrier((arrived, write_field(1, field)))
        products = products + arrived
        distance *= 2
    updated = pl.pallas_call(
        functools.partial(update_kernel, per_group),
        out_shape=jax.ShapeDtypeStruct(parameters.shape, jnp.float32),
        compiler_params=pltpu.CompilerParams(vmem_limit_bytes=VMEM_LIMIT),
        name="update",
    )(
        products[None], same, same[:, :local_members], rank[None, :], rank[:, None],
        param_anomalies, parameters,
    )
    return (field.reshape(tracer.shape), updated)


def solution(mesh):
    in_specs = (
        P("ens", "slab", None),
        P(None, "slab", None),
        P("ens", None),
        P("slab"),
        P("ens", "slab"),
        P("slab"),
        P(),
    )
    out_specs = (P("ens", "slab", None), P("ens", None))
    return jax.shard_map(local, mesh=mesh, in_specs=in_specs, out_specs=out_specs, check_vma=False)
```

```python
import functools
import math

import jax
import jax.numpy as jnp
from jax import lax
from jax.experimental import pallas as pl
from jax.experimental.pallas import tpu as pltpu
from jax.sharding import PartitionSpec as P

STEPS = 4
GROUPS = 8
HALO = 2 * STEPS
LANES = 128
SUBLANES = 8
ROWS = 16
GROUP = 4
FOLD = 4
PICKED = 128
TILES = 4
FIELD_CALLS = 2
ALL_ROWS = ROWS + 2 * HALO
VMEM_LIMIT = 16 * 1024 * 1024
TALL_LIMIT = 58 * 1024 * 1024
COST_BYTES = 200000
ANYWHERE = pl.BlockSpec(memory_space=pltpu.HBM)
IN_VMEM = pl.BlockSpec(memory_space=pltpu.VMEM)
IN_SMEM = pl.BlockSpec(memory_space=pltpu.SMEM)


def hdot(left, right):
    return jnp.dot(left, right, precision=lax.Precision.HIGHEST, preferred_element_type=jnp.float32)


def limited(left, right):
    return jnp.minimum(jnp.maximum(left, jnp.minimum(right, 0.0)), jnp.maximum(right, 0.0))


def block_at(block):
    return pl.ds(pl.multiple_of(block * LANES, LANES), LANES)


def everywhere(coef, block, place):
    return coef[block, pl.ds(place, SUBLANES, stride=0), :]


def edge_lanes():
    lane = lax.broadcasted_iota(jnp.int32, (SUBLANES, LANES), 1)
    return lane == 0, lane == LANES - 1


def dealt(values, back=False):
    shape = (FOLD * LANES, FOLD * LANES)
    natural = lax.broadcasted_iota(jnp.int32, shape, 1 if back else 0)
    place = lax.broadcasted_iota(jnp.int32, shape, 0 if back else 1)
    moves = natural == FOLD * lax.rem(place, LANES) + lax.div(place, LANES)
    moves = jnp.where(moves, 1.0, 0.0).astype(jnp.bfloat16)
    products = []
    for _ in range(3):
        piece = values.astype(jnp.bfloat16)
        products.append(jnp.dot(piece, moves, preferred_element_type=jnp.float32))
        values = values - piece.astype(jnp.float32)
    return products[0] + (products[1] + products[2])


def stencil(line, speeds):
    d = [line[i + 1] - line[i] for i in range(GROUP + 3)]
    slope = [None] + [limited(d[i - 1], d[i]) for i in range(1, GROUP + 3)]
    twice = [None] + [d[i] + d[i] for i in range(1, GROUP + 2)]
    results = []
    for i in range(2, GROUP + 2):
        speed = speeds[i - 2]
        forward = twice[i - 1] - slope[i - 1]
        backward = twice[i] - slope[i + 1]
        flux = speed * (jnp.where(speed > 0.0, forward, backward) + slope[i])
        results.append((flux, d[i] - d[i - 1]))
    return results


def advance_tile(cell, places, part, parts, source, target, coef, params, blocks):
    start = part * FOLD
    before = lax.rem(part + parts - 1, parts) * FOLD
    after = lax.rem(part + 1, parts) * FOLD
    first, last = edge_lanes()
    own = [
        [source[cell + (i - 2) * blocks + start + p] for p in range(FOLD)] for i in range(GROUP + 4)
    ]
    along_rows = [
        stencil(
            [own[i][p] for i in range(GROUP + 4)],
            [everywhere(coef, start + p, places[i][0]) for i in range(GROUP)],
        )
        for p in range(FOLD)
    ]
    for i in range(GROUP):
        row = own[i + 2]
        here = cell + i * blocks
        left = [
            jnp.where(first, pltpu.roll(source[here + before + p], 1, 1), pltpu.roll(row[p], 1, 1))
            for p in (FOLD - 2, FOLD - 1)
        ]
        right = [
            jnp.where(
                last,
                pltpu.roll(source[here + after + p], LANES - 1, 1),
                pltpu.roll(row[p], LANES - 1, 1),
            )
            for p in (0, 1)
        ]
        along_columns = stencil(
            [*left, *row, *right], [everywhere(coef, start + p, places[i][1]) for p in range(FOLD)]
        )
        for p in range(FOLD):
            flux_x, lap_x = along_rows[p][i]
            flux_y, lap_y = along_columns[p]
            value = row[p] - 0.5 * (flux_x + flux_y)
            value = value + everywhere(coef, start + p, places[i][2]) * (lap_x + lap_y)
            value = value + params[:, block_at(start + p)] * everywhere(coef, start + p, places[i][3])
            target[here + start + p] = value


def advance_group(source, target, row, coef, params, blocks):
    cell = row * blocks
    places = [[coef_row(array, row + i) for array in range(4)] for i in range(GROUP)]
    parts = blocks // FOLD

    @pl.loop(0, parts // TILES)
    def _(some):
        for k in range(TILES):
            advance_tile(
                cell, places, some * TILES + k, parts, source, target, coef, params, blocks
            )


class Copies:
    def __init__(self, sems):
        self.sems, self.used = sems, 0

    def make(self, source, target):
        copy = pltpu.make_async_copy(source, target, self.sems.at[self.used])
        self.used += 1
        assert self.used <= self.sems.shape[0]
        return copy

    def start(self, source, target):
        copy = self.make(source, target)
        copy.start()
        return copy


def region(levels, level, row, blocks):
    return levels[level].at[pl.ds((HALO + row) * blocks, GROUP * blocks)]


def fill_rows(blocks, first_rows, tracer, mixed, staged, sems):
    def copy(block):
        return pltpu.make_async_copy(tracer.at[:, block_at(block)], staged.at[block], sems.at[block])

    @pl.loop(0, blocks)
    def _(block):
        copy(block).start()

    lines = len(first_rows) * GROUP * SUBLANES

    @pl.loop(0, blocks // FOLD)
    def _(part):
        for q in range(FOLD):
            block = part * FOLD + q
            copy(block).wait()
            for k, first_row in enumerate(first_rows):
                for row in range(GROUP):
                    line = part * lines + (k * GROUP + row) * SUBLANES
                    mixed[pl.ds(pl.multiple_of(line, SUBLANES), SUBLANES), block_at(q)] = staged[
                        block, pl.ds(first_row + row, SUBLANES, stride=ROWS), :
                    ]


def take_rows(blocks, mixed, outs):
    lines = len(outs) * GROUP * SUBLANES

    @pl.loop(0, blocks // FOLD)
    def _(part):
        for k, out in enumerate(outs):
            for row in range(GROUP):
                line = part * lines + (k * GROUP + row) * SUBLANES
                for p in range(FOLD):
                    out[row * blocks + part * FOLD + p] = mixed[
                        pl.ds(pl.multiple_of(line, SUBLANES), SUBLANES), block_at(p)
                    ]


def outer_rows_kernel(
    blocks, tracer, own_coef, place_of, up, down, up_coef, down_coef, edge, edge_sem, mixed, staged, sems
):
    copy = pltpu.make_async_copy(own_coef.at[place_of[0]], edge, edge_sem)
    copy.start()
    fill_rows(blocks, (0, ROWS - GROUP), tracer, mixed, staged, sems)
    copy.wait()
    parts = blocks // FOLD
    field_lines = parts * 2 * GROUP * SUBLANES
    width = FOLD * LANES
    for part in range(parts):
        mixed[field_lines + part * ROWS : field_lines + (part + 1) * ROWS, :] = edge[
            :, part * width : (part + 1) * width
        ]
    mixed[...] = dealt(mixed[...])
    take_rows(blocks, mixed, (down, up))
    for part in range(parts):
        line = field_lines + part * ROWS
        for p in range(FOLD):
            down_coef[part * FOLD + p] = mixed[line : line + HALO, block_at(p)]
            up_coef[part * FOLD + p] = mixed[line + ROWS - HALO : line + ROWS, block_at(p)]


def inner_rows_kernel(
    blocks, tracer, own_coef, params, outer, low, high, by_block, dealt_params, whole, coef_sem, mixed,
    staged, sems,
):
    copy = pltpu.make_async_copy(own_coef, whole, coef_sem)
    copy.start()
    fill_rows(blocks, (GROUP, ROWS - 2 * GROUP), tracer, mixed, staged, sems)
    copy.wait()
    parts = blocks // FOLD
    coef_lines = parts * 2 * GROUP * SUBLANES
    param_lines = coef_lines + parts * 4 * ROWS
    width = FOLD * LANES
    for part in range(parts):
        at = slice(part * width, (part + 1) * width)
        for array in range(4):
            line = coef_lines + (part * 4 + array) * ROWS
            mixed[line : line + ROWS, :] = whole[array, :, at]
        line = param_lines + part * SUBLANES
        mixed[line : line + SUBLANES, :] = params[:, at]
    mixed[...] = dealt(mixed[...])
    take_rows(blocks, mixed, (low, high))
    for part in range(parts):
        line = coef_lines + part * 4 * ROWS
        for p in range(FOLD):
            block = part * FOLD + p
            by_block[block] = mixed[line : line + 4 * ROWS, block_at(p)]
            dealt_params[:, block_at(block)] = mixed[
                param_lines + part * SUBLANES : param_lines + (part + 1) * SUBLANES, block_at(p)
            ]


def interior_kernel(blocks, own0, own1, own2, own3, own_coef, params, *rest):
    outs, (*levels, coef, sems) = rest[:5], rest[5:]
    copies = Copies(sems)
    waits = [
        copies.start(own, region(levels, 0, GROUP * i, blocks))
        for i, own in enumerate((own0, own1, own2, own3))
    ]
    waits.append(copies.start(own_coef, coef.at[:, 0 : 4 * ROWS]))
    for copy in waits:
        copy.wait()

    for level, start, count in ((0, 2, 3), (1, 4, 2), (2, 6, 1)):
        @pl.loop(0, count)
        def _(i):
            row = start + HALO + GROUP * i
            advance_group(levels[level], levels[level + 1], row, coef, params, blocks)

    waits = [
        copies.start(region(levels, level, row, blocks), out)
        for out, (level, row) in zip(outs, ((1, 2), (1, 10), (2, 4), (2, 8), (3, 6)))
    ]
    for copy in waits:
        copy.wait()


def edge_steps(outer, blocks, waits, sends, levels, coef, params):
    for level in range(STEPS):
        for copy in waits[level]:
            copy.wait()
        low, high = 2 * level - outer, ROWS + outer - GROUP - 2 * level

        @pl.loop(0, 2)
        def _(side):
            row = low + HALO + side * (high - low)
            advance_group(levels[level], levels[level + 1], row, coef, params, blocks)

        for copy in sends[2 * level : 2 * level + 2]:
            copy.start()


def coef_row(array, row):
    own = array * ROWS + row - HALO
    low = 4 * ROWS + 2 * HALO * array + row
    high = 4 * ROWS + 2 * HALO * array + row - ROWS
    return jnp.where(row < HALO, low, jnp.where(row < HALO + ROWS, own, high))


def load_coef(copies, own_coef, pair, other, place_of, coef):
    waits = [copies.start(own_coef, coef.at[:, 0 : 4 * ROWS])]
    for number, source in enumerate((pair.at[0], pair.at[1], other.at[0], other.at[1])):
        array = jnp.bitwise_xor(place_of[0], number)
        for side in range(2):
            first = 4 * ROWS + 2 * HALO * array + HALO * side
            waits.append(copies.start(source.at[side], coef.at[:, pl.ds(first, HALO)]))
    return waits


def middle_kernel(blocks, *refs):
    sources, refs = refs[:9], refs[9:]
    own_coef, pair, other, params, place_of = refs[:5]
    outs, (*levels, coef, sems) = refs[5:13], refs[13:]
    copies = Copies(sems)
    places = ((0, -4), (0, 0), (0, 12), (0, 16), (1, 2), (1, 10), (2, 4), (2, 8), (3, 6))
    waits = [[] for _ in range(STEPS)]
    for source, (level, row) in zip(sources, places):
        waits[level].append(copies.start(source, region(levels, level, row, blocks)))
    waits[0] += load_coef(copies, own_coef, pair, other, place_of, coef)
    places = [(k + 1, row) for k in range(STEPS) for row in (2 * k - 2, ROWS + 2 - GROUP - 2 * k)]
    sends = [
        copies.make(region(levels, level, row, blocks), out)
        for out, (level, row) in zip(outs, places)
    ]
    edge_steps(2, blocks, waits, sends, levels, coef, params)
    for copy in sends:
        copy.wait()


def last_kernel(blocks, *refs):
    sources, refs = refs[:12], refs[12:]
    own_coef, pair, other, params, place_of, cell_of, shift_of = refs[:7]
    low_out, high_out, predicted, *levels, coef, sems = refs[7:]
    copies = Copies(sems)
    places = (
        (0, -8), (0, -4), (0, 16), (0, 20),
        (1, -2), (1, 14), (2, 0), (2, 12), (3, 2), (3, 10), (4, 4), (4, 8),
    )
    waits = [[] for _ in range(STEPS + 1)]
    for source, (level, row) in zip(sources, places):
        waits[level].append(copies.start(source, region(levels, level, row, blocks)))
    waits[0] += load_coef(copies, own_coef, pair, other, place_of, coef)
    edge_steps(6, blocks, waits, (), levels, coef, params)
    for copy in waits[STEPS]:
        copy.wait()
    sends = [
        copies.start(region(levels, STEPS, row, blocks), out)
        for row, out in ((0, low_out), (ROWS - GROUP, high_out))
    ]
    lane = lax.broadcasted_iota(jnp.int32, (SUBLANES, LANES), 1)

    @pl.loop(0, predicted.shape[1] // LANES)
    def _(block):
        base = block * LANES

        def some(part, found):
            for i in range(PICKED):
                o = part * PICKED + i
                value = pltpu.roll(levels[STEPS][cell_of[base + o]], shift_of[base + o], 1)
                found = jnp.where(lane == o, value, found)
            return found

        empty = jnp.zeros((SUBLANES, LANES), jnp.float32)
        predicted[:, block_at(block)] = lax.fori_loop(0, LANES // PICKED, some, empty)

    for copy in sends:
        copy.wait()


def field_kernel(blocks, first_part, count, *refs):
    sources, refs = refs[: ROWS // GROUP], refs[-6:]
    out, cells, mixed, staged, sems, out_sems = refs
    copies = Copies(sems)
    width = count * FOLD
    waits = [
        copies.start(
            source.at[pl.ds(row * blocks + first_part * FOLD, width)],
            cells.at[pl.ds((i * GROUP + row) * width, width)],
        )
        for i, source in enumerate(sources)
        for row in range(GROUP)
    ]
    for copy in waits:
        copy.wait()
    lines = ROWS * SUBLANES

    def line_at(part, row):
        return pl.ds(pl.multiple_of(part * lines + row * SUBLANES, SUBLANES), SUBLANES)

    @pl.loop(0, count)
    def _(part):
        for row in range(ROWS):
            for p in range(FOLD):
                mixed[line_at(part, row), block_at(p)] = cells[row * width + part * FOLD + p]

    mixed[...] = dealt(mixed[...], back=True)

    def out_copy(block):
        return pltpu.make_async_copy(
            staged.at[block], out.at[:, block_at(first_part * FOLD + block)], out_sems.at[block]
        )

    @pl.loop(0, count)
    def _(part):
        for q in range(FOLD):
            block = part * FOLD + q
            for row in range(ROWS):
                staged[block, pl.ds(row, SUBLANES, stride=ROWS), :] = mixed[
                    line_at(part, row), block_at(q)
                ]
            out_copy(block).start()

    @pl.loop(0, width)
    def _(block):
        out_copy(block).wait()


def scratch(columns, *more):
    blocks = columns // LANES
    return [
        *[pltpu.VMEM((ALL_ROWS * blocks, SUBLANES, LANES), jnp.float32)] * (STEPS + 1),
        pltpu.VMEM((blocks, 4 * ALL_ROWS, LANES), jnp.float32),
        *more,
    ]


def kernel_call(body, name, outs, specs, out_specs, scratches, cost, operands, aliases={}):
    return pl.pallas_call(
        body,
        out_shape=tuple(jax.ShapeDtypeStruct(shape, jnp.float32) for shape in outs),
        in_specs=specs,
        out_specs=out_specs,
        scratch_shapes=scratches,
        compiler_params=pltpu.CompilerParams(vmem_limit_bytes=TALL_LIMIT),
        cost_estimate=pl.CostEstimate(flops=0, bytes_accessed=cost * COST_BYTES, transcendentals=0),
        input_output_aliases=aliases,
        name=name,
    )(*operands)


def row_groups(tracer, coefficients, params, place_of):
    members, rows, columns = tracer.shape
    if members != SUBLANES or rows != ROWS or columns % (FOLD * LANES):
        raise ValueError("block shape")
    blocks = columns // LANES
    parts = blocks // FOLD
    flat = tracer.reshape(members * rows, columns)
    dma = pltpu.SemaphoreType.DMA
    staged = [pltpu.VMEM((blocks, members * rows, LANES), jnp.float32), dma((blocks,))]

    def mixed(lines):
        return pltpu.VMEM((parts * lines, FOLD * LANES), jnp.float32)

    group, edge = (GROUP * blocks, members, LANES), (blocks, HALO, LANES)
    up, down, up_coef, down_coef = kernel_call(
        functools.partial(outer_rows_kernel, blocks), "outer_rows",
        [group, group, edge, edge], [ANYWHERE, ANYWHERE, IN_SMEM], (IN_VMEM,) * 4,
        [pltpu.VMEM((rows, columns), jnp.float32), dma, mixed(2 * GROUP * members + rows)] + staged, 3,
        [flat, coefficients, place_of],
    )
    low, high, by_block, dealt_params = kernel_call(
        functools.partial(inner_rows_kernel, blocks), "inner_rows",
        [group, group, (blocks, 4 * rows, LANES), params.shape],
        [ANYWHERE, ANYWHERE, IN_VMEM, ANYWHERE], (IN_VMEM,) * 4,
        [
            pltpu.VMEM((4, rows, columns), jnp.float32), dma,
            mixed(2 * GROUP * members + 4 * rows + members),
        ] + staged, 3,
        [flat, coefficients, params, up],
    )
    return (down, low, high, up), (up_coef, down_coef), by_block, dealt_params


def transport(shape, own, low0, high0, own_coef, pair, other, params, place_of, obs_index, halos, share_params):
    members, rows, columns = shape
    blocks = columns // LANES
    group = (GROUP * blocks, members, LANES)
    flat = (members * rows, columns)
    dma = pltpu.SemaphoreType.DMA
    inner = kernel_call(
        functools.partial(interior_kernel, blocks), "interior",
        [group] * 5, [ANYWHERE] * 5 + [IN_VMEM], (ANYWHERE,) * 5,
        scratch(columns, dma((16,))), 8, [*own, own_coef, params],
    )
    upper, lower, low0, high0, *_ = lax.optimization_barrier(
        (own[2], own[1], low0, high0, inner[0])
    )
    low1, high1 = halos(upper, lower)
    first = kernel_call(
        functools.partial(middle_kernel, blocks), "edge_first",
        [group] * 8, [ANYWHERE] * 12 + [IN_VMEM, IN_SMEM], (ANYWHERE,) * 8,
        scratch(columns, dma((29,))), 10,
        [low0, own[0], own[3], high0, *inner, own_coef, pair, other, params, place_of],
    )
    place_of, *all_params = lax.optimization_barrier((place_of, *share_params(inner[0])))
    obs_row, obs_col = obs_index // columns, obs_index % columns
    width = FOLD * LANES
    obs_block = obs_col // width * FOLD + obs_col % FOLD
    cell_of = (HALO + obs_row) * blocks + obs_block
    lane_of = obs_col % width // FOLD
    shift_of = (jnp.arange(obs_index.shape[0], dtype=jnp.int32) - lane_of) % LANES
    low4, high4, predicted = kernel_call(
        functools.partial(last_kernel, blocks), "edge_last",
        [group, group, (members, obs_index.shape[0])],
        [ANYWHERE] * 15 + [IN_VMEM] + [IN_SMEM] * 3, (ANYWHERE, ANYWHERE, IN_VMEM),
        scratch(columns, dma((31,))), 15,
        [low1, low0, high0, high1, *first, own_coef, pair, other, params, place_of, cell_of, shift_of],
    )

    def write_field(index, field):
        parts = blocks // FOLD
        first_part = parts * index // FIELD_CALLS
        count = parts * (index + 1) // FIELD_CALLS - first_part
        width = count * FOLD
        previous = [] if field is None else [field]
        return kernel_call(
            functools.partial(field_kernel, blocks, first_part, count), "field_%d" % index,
            [flat], [ANYWHERE] * (4 + len(previous)), (ANYWHERE,),
            [
                pltpu.VMEM((rows * width, members, LANES), jnp.float32),
                pltpu.VMEM((members * rows * count, FOLD * LANES), jnp.float32),
                pltpu.VMEM((width, members * rows, LANES), jnp.float32),
                dma((rows,)), dma((width,)),
            ],
            4, [low4, first[6], first[7], high4, *previous], {4: 0} if previous else {},
        )[0]

    return write_field, predicted, all_params


def products_kernel(
    total_obs, per_group, spread, own, second, third, fourth, values, variance, same, out
):
    weight = 1.0 / (variance[...] * total_obs)
    predicted = jnp.concatenate([own[...], second[...], third[...], fourth[...]], axis=0)
    innovation = (values[...] - own[...]) * weight
    anomalies = (predicted - hdot(same[...], predicted) / per_group) * spread
    right = jnp.concatenate([anomalies * weight, innovation], axis=0)
    out[...] = lax.dot_general(
        anomalies,
        right,
        (((1,), (1,)), ((), ())),
        precision=lax.Precision.HIGHEST,
        preferred_element_type=jnp.float32,
    )


def update_kernel(per_group, summands, same, own_same, rank_row, rank_col, anomalies, own, out):
    members = same.shape[0]
    total = summands[0]
    for index in range(1, summands.shape[0]):
        total = total + summands[index]
    together = same[...]
    row = lax.broadcasted_iota(jnp.int32, (members, members), 0)
    col = lax.broadcasted_iota(jnp.int32, (members, members), 1)
    system = jnp.where(row == col, 1.0, 0.0) + together * total[:, 0:members]
    right = own_same[...] * total[:, members:]
    for pivot in range(per_group):
        pick = jnp.where(rank_row[...] == pivot, together, 0.0)
        pivot_system = hdot(pick, system)
        pivot_right = hdot(pick, right)
        pivot_value = jnp.sum(pick * pivot_system, axis=1, keepdims=True)
        factor = jnp.sum(pick * system, axis=1, keepdims=True)
        is_pivot = rank_col[...] == pivot
        scale = 1.0 / pivot_value
        scaled_system, scaled_right = pivot_system * scale, pivot_right * scale
        system = jnp.where(is_pivot, scaled_system, system - factor * scaled_system)
        right = jnp.where(is_pivot, scaled_right, right - factor * scaled_right)
    change = lax.dot_general(
        right,
        anomalies[...],
        (((0,), (0,)), ((), ())),
        precision=lax.Precision.HIGHEST,
        preferred_element_type=jnp.float32,
    )
    out[...] = own[...] + change


def local(tracer, coefficients, parameters, obs_index, obs_values, obs_variance, member_group):
    local_members, rows, columns = tracer.shape
    ens_pos = lax.axis_index("ens")
    ens_count = lax.axis_size("ens")
    slab_count = lax.axis_size("slab")
    if ens_count != 4 or coefficients.shape[0] != 4 or slab_count & (slab_count - 1):
        raise ValueError("mesh shape")
    forward = [(i, i + 1) for i in range(slab_count - 1)]
    backward = [(target, source) for source, target in forward]

    def next_core(value):
        return lax.ppermute(value, "ens", [(i, i ^ 1) for i in range(ens_count)])

    def next_chip(value):
        return lax.ppermute(value, "ens", [(i, i ^ 2) for i in range(ens_count)])

    def over_ens(mine):
        pair = jnp.stack([mine, next_core(mine)])
        return pair, next_chip(pair)

    def halos(upper, lower):
        return lax.ppermute(upper, "slab", forward), lax.ppermute(lower, "slab", backward)

    place_of = jnp.reshape(ens_pos, (1,))
    own, coef_edges, own_coef, dealt_params = row_groups(
        tracer, coefficients, parameters, place_of
    )
    low0, high0 = halos(own[3], own[0])

    edge_low, edge_high = halos(*coef_edges)
    pair, other = over_ens(jnp.stack([edge_low, edge_high]))

    members = member_group.shape[0]
    per_group = members // GROUPS
    spread = 1.0 / math.sqrt(per_group - 1)
    blocks_of = member_group.reshape(ens_count, local_members)
    group_of = jnp.concatenate(
        [lax.dynamic_index_in_dim(blocks_of, ens_pos ^ i, 0, False) for i in range(ens_count)]
    )
    same_bool = group_of[:, None] == group_of[None, :]
    same = same_bool.astype(jnp.float32)
    earlier = jnp.arange(members)[None, :] < jnp.arange(members)[:, None]
    rank = jnp.sum((same_bool & earlier).astype(jnp.int32), axis=1)

    def share_params(after):
        later, _ = lax.optimization_barrier((parameters, after))
        return over_ens(later)

    write_field, predicted, all_params = transport(
        tracer.shape, own, low0, high0,
        own_coef, pair, other, dealt_params, place_of, obs_index, halos, share_params,
    )
    all_params = jnp.concatenate(all_params, axis=0).reshape(members, columns)
    param_anomalies = (all_params - hdot(same, all_params) / per_group) * spread

    others = [
        lax.ppermute(predicted, "ens", [(i, i ^ step) for i in range(ens_count)])
        for step in range(1, ens_count)
    ]
    *others, field = lax.optimization_barrier((*others, write_field(0, None)))
    total_obs = obs_variance.shape[0] * slab_count
    products = pl.pallas_call(
        functools.partial(products_kernel, float(total_obs), per_group, spread),
        out_shape=jax.ShapeDtypeStruct((members, members + local_members), jnp.float32),
        compiler_params=pltpu.CompilerParams(vmem_limit_bytes=VMEM_LIMIT),
        name="products",
    )(predicted, *others, obs_values, obs_variance[None, :], same)
    distance = 1
    while distance < slab_count:
        radix = 4 if slab_count // distance % 4 == 0 else 2
        arrived = [
            lax.ppermute(products, "slab", [(i, i ^ (step * distance)) for i in range(slab_count)])
            for step in range(1, radix)
        ]
        if distance == 1:
            *arrived, field = lax.optimization_barrier((*arrived, write_field(1, field)))
        products = products + arrived[0]
        if radix == 4:
            products = products + (arrived[1] + arrived[2])
        distance *= radix
    updated = pl.pallas_call(
        functools.partial(update_kernel, per_group),
        out_shape=jax.ShapeDtypeStruct(parameters.shape, jnp.float32),
        compiler_params=pltpu.CompilerParams(vmem_limit_bytes=VMEM_LIMIT),
        name="update",
    )(
        products[None], same, same[:, :local_members], rank[None, :], rank[:, None],
        param_anomalies, parameters,
    )
    return (field.reshape(tracer.shape), updated)


def solution(mesh):
    in_specs = (
        P("ens", "slab", None),
        P(None, "slab", None),
        P("ens", None),
        P("slab"),
        P("ens", "slab"),
        P("slab"),
        P(),
    )
    out_specs = (P("ens", "slab", None), P("ens", None))
    return jax.shard_map(local, mesh=mesh, in_specs=in_specs, out_specs=out_specs, check_vma=False)
```

```python
import functools
import math

import jax
import jax.numpy as jnp
from jax import lax
from jax.experimental import pallas as pl
from jax.experimental.pallas import tpu as pltpu
from jax.sharding import PartitionSpec as P

STEPS = 4
GROUPS = 8
HALO = 2 * STEPS
LANES = 128
SUBLANES = 8
ROWS = 16
GROUP = 4
FOLD = 4
PICKED = 128
TILES = 4
FIELD_CALLS = 2
ALL_ROWS = ROWS + 2 * HALO
VMEM_LIMIT = 16 * 1024 * 1024
TALL_LIMIT = 60 * 1024 * 1024
COST_BYTES = 200000
ANYWHERE = pl.BlockSpec(memory_space=pltpu.HBM)
IN_VMEM = pl.BlockSpec(memory_space=pltpu.VMEM)
IN_SMEM = pl.BlockSpec(memory_space=pltpu.SMEM)


def hdot(left, right):
    return jnp.dot(left, right, precision=lax.Precision.HIGHEST, preferred_element_type=jnp.float32)


def limited(left, right):
    return jnp.minimum(jnp.maximum(left, jnp.minimum(right, 0.0)), jnp.maximum(right, 0.0))


def block_at(block):
    return pl.ds(pl.multiple_of(block * LANES, LANES), LANES)


def everywhere(coef, block, place):
    return coef[block, pl.ds(place, SUBLANES, stride=0), :]


def edge_lanes():
    lane = lax.broadcasted_iota(jnp.int32, (SUBLANES, LANES), 1)
    return lane == 0, lane == LANES - 1


def dealt(values, back=False):
    shape = (FOLD * LANES, FOLD * LANES)
    natural = lax.broadcasted_iota(jnp.int32, shape, 1 if back else 0)
    place = lax.broadcasted_iota(jnp.int32, shape, 0 if back else 1)
    moves = natural == FOLD * lax.rem(place, LANES) + lax.div(place, LANES)
    moves = jnp.where(moves, 1.0, 0.0).astype(jnp.bfloat16)
    products = []
    for _ in range(3):
        piece = values.astype(jnp.bfloat16)
        products.append(jnp.dot(piece, moves, preferred_element_type=jnp.float32))
        values = values - piece.astype(jnp.float32)
    return products[0] + (products[1] + products[2])


def stencil(line, speeds):
    d = [line[i + 1] - line[i] for i in range(GROUP + 3)]
    slope = [None] + [limited(d[i - 1], d[i]) for i in range(1, GROUP + 3)]
    twice = [None] + [d[i] + d[i] for i in range(1, GROUP + 2)]
    results = []
    for i in range(2, GROUP + 2):
        speed = speeds[i - 2]
        forward = twice[i - 1] - slope[i - 1]
        backward = twice[i] - slope[i + 1]
        flux = speed * (jnp.where(speed > 0.0, forward, backward) + slope[i])
        results.append((flux, d[i] - d[i - 1]))
    return results


def advance_tile(cell, places, part, parts, source, target, coef, params, blocks):
    start = part * FOLD
    before = lax.rem(part + parts - 1, parts) * FOLD
    after = lax.rem(part + 1, parts) * FOLD
    first, last = edge_lanes()
    own = [
        [source[cell + (i - 2) * blocks + start + p] for p in range(FOLD)] for i in range(GROUP + 4)
    ]
    along_rows = [
        stencil(
            [own[i][p] for i in range(GROUP + 4)],
            [everywhere(coef, start + p, places[i][0]) for i in range(GROUP)],
        )
        for p in range(FOLD)
    ]
    for i in range(GROUP):
        row = own[i + 2]
        here = cell + i * blocks
        left = [
            jnp.where(first, pltpu.roll(source[here + before + p], 1, 1), pltpu.roll(row[p], 1, 1))
            for p in (FOLD - 2, FOLD - 1)
        ]
        right = [
            jnp.where(
                last,
                pltpu.roll(source[here + after + p], LANES - 1, 1),
                pltpu.roll(row[p], LANES - 1, 1),
            )
            for p in (0, 1)
        ]
        along_columns = stencil(
            [*left, *row, *right], [everywhere(coef, start + p, places[i][1]) for p in range(FOLD)]
        )
        for p in range(FOLD):
            flux_x, lap_x = along_rows[p][i]
            flux_y, lap_y = along_columns[p]
            value = row[p] - 0.5 * (flux_x + flux_y)
            value = value + everywhere(coef, start + p, places[i][2]) * (lap_x + lap_y)
            value = value + params[:, block_at(start + p)] * everywhere(coef, start + p, places[i][3])
            target[here + start + p] = value


def advance_group(source, target, row, coef, params, blocks):
    cell = row * blocks
    places = [[coef_row(array, row + i) for array in range(4)] for i in range(GROUP)]
    parts = blocks // FOLD

    @pl.loop(0, parts // TILES)
    def _(some):
        for k in range(TILES):
            advance_tile(
                cell, places, some * TILES + k, parts, source, target, coef, params, blocks
            )


class Copies:
    def __init__(self, sems):
        self.sems, self.used = sems, 0

    def make(self, source, target):
        copy = pltpu.make_async_copy(source, target, self.sems.at[self.used])
        self.used += 1
        assert self.used <= self.sems.shape[0]
        return copy

    def start(self, source, target):
        copy = self.make(source, target)
        copy.start()
        return copy


def region(levels, level, row, blocks):
    return levels[level].at[pl.ds((HALO + row) * blocks, GROUP * blocks)]


def fill_rows(blocks, first_rows, tracer, mixed, staged, sems):
    def copy(block):
        return pltpu.make_async_copy(tracer.at[:, block_at(block)], staged.at[block], sems.at[block])

    @pl.loop(0, blocks)
    def _(block):
        copy(block).start()

    lines = len(first_rows) * GROUP * SUBLANES

    @pl.loop(0, blocks // FOLD)
    def _(part):
        for q in range(FOLD):
            block = part * FOLD + q
            copy(block).wait()
            for k, first_row in enumerate(first_rows):
                for row in range(GROUP):
                    line = part * lines + (k * GROUP + row) * SUBLANES
                    mixed[pl.ds(pl.multiple_of(line, SUBLANES), SUBLANES), block_at(q)] = staged[
                        block, pl.ds(first_row + row, SUBLANES, stride=ROWS), :
                    ]


def take_rows(blocks, mixed, outs):
    lines = len(outs) * GROUP * SUBLANES

    @pl.loop(0, blocks // FOLD)
    def _(part):
        for k, out in enumerate(outs):
            for row in range(GROUP):
                line = part * lines + (k * GROUP + row) * SUBLANES
                for p in range(FOLD):
                    out[row * blocks + part * FOLD + p] = mixed[
                        pl.ds(pl.multiple_of(line, SUBLANES), SUBLANES), block_at(p)
                    ]


def outer_rows_kernel(
    blocks, tracer, own_coef, place_of, up, down, up_coef, down_coef, edge, edge_sem, mixed, staged, sems
):
    copy = pltpu.make_async_copy(own_coef.at[place_of[0]], edge, edge_sem)
    copy.start()
    fill_rows(blocks, (0, ROWS - GROUP), tracer, mixed, staged, sems)
    copy.wait()
    parts = blocks // FOLD
    field_lines = parts * 2 * GROUP * SUBLANES
    width = FOLD * LANES
    for part in range(parts):
        mixed[field_lines + part * ROWS : field_lines + (part + 1) * ROWS, :] = edge[
            :, part * width : (part + 1) * width
        ]
    mixed[...] = dealt(mixed[...])
    take_rows(blocks, mixed, (down, up))
    for part in range(parts):
        line = field_lines + part * ROWS
        for p in range(FOLD):
            down_coef[part * FOLD + p] = mixed[line : line + HALO, block_at(p)]
            up_coef[part * FOLD + p] = mixed[line + ROWS - HALO : line + ROWS, block_at(p)]


def inner_rows_kernel(
    blocks, tracer, own_coef, params, outer, low, high, by_block, dealt_params, whole, coef_sem, mixed,
    staged, sems,
):
    copy = pltpu.make_async_copy(own_coef, whole, coef_sem)
    copy.start()
    fill_rows(blocks, (GROUP, ROWS - 2 * GROUP), tracer, mixed, staged, sems)
    copy.wait()
    parts = blocks // FOLD
    coef_lines = parts * 2 * GROUP * SUBLANES
    param_lines = coef_lines + parts * 4 * ROWS
    width = FOLD * LANES
    for part in range(parts):
        at = slice(part * width, (part + 1) * width)
        for array in range(4):
            line = coef_lines + (part * 4 + array) * ROWS
            mixed[line : line + ROWS, :] = whole[array, :, at]
        line = param_lines + part * SUBLANES
        mixed[line : line + SUBLANES, :] = params[:, at]
    mixed[...] = dealt(mixed[...])
    take_rows(blocks, mixed, (low, high))
    for part in range(parts):
        line = coef_lines + part * 4 * ROWS
        for p in range(FOLD):
            block = part * FOLD + p
            by_block[block] = mixed[line : line + 4 * ROWS, block_at(p)]
            dealt_params[:, block_at(block)] = mixed[
                param_lines + part * SUBLANES : param_lines + (part + 1) * SUBLANES, block_at(p)
            ]


def interior_kernel(blocks, own0, own1, own2, own3, own_coef, params, *rest):
    outs, (*levels, coef, sems) = rest[:5], rest[5:]
    copies = Copies(sems)
    waits = [
        copies.start(own, region(levels, 0, GROUP * i, blocks))
        for i, own in enumerate((own0, own1, own2, own3))
    ]
    waits.append(copies.start(own_coef, coef.at[:, 0 : 4 * ROWS]))
    for copy in waits:
        copy.wait()

    for level, start, count in ((0, 2, 3), (1, 4, 2), (2, 6, 1)):
        @pl.loop(0, count)
        def _(i):
            row = start + HALO + GROUP * i
            advance_group(levels[level], levels[level + 1], row, coef, params, blocks)

    waits = [
        copies.start(region(levels, level, row, blocks), out)
        for out, (level, row) in zip(outs, ((1, 2), (1, 10), (2, 4), (2, 8), (3, 6)))
    ]
    for copy in waits:
        copy.wait()


def edge_steps(outer, blocks, waits, sends, levels, coef, params):
    for level in range(STEPS):
        for copy in waits[level]:
            copy.wait()
        low, high = 2 * level - outer, ROWS + outer - GROUP - 2 * level

        @pl.loop(0, 2)
        def _(side):
            row = low + HALO + side * (high - low)
            advance_group(levels[level], levels[level + 1], row, coef, params, blocks)

        for copy in sends[2 * level : 2 * level + 2]:
            copy.start()


def coef_row(array, row):
    own = array * ROWS + row - HALO
    low = 4 * ROWS + 2 * HALO * array + row
    high = 4 * ROWS + 2 * HALO * array + row - ROWS
    return jnp.where(row < HALO, low, jnp.where(row < HALO + ROWS, own, high))


def load_coef(copies, own_coef, pair, other, place_of, coef):
    waits = [copies.start(own_coef, coef.at[:, 0 : 4 * ROWS])]
    for number, source in enumerate((pair.at[0], pair.at[1], other.at[0], other.at[1])):
        array = jnp.bitwise_xor(place_of[0], number)
        for side in range(2):
            first = 4 * ROWS + 2 * HALO * array + HALO * side
            waits.append(copies.start(source.at[side], coef.at[:, pl.ds(first, HALO)]))
    return waits


def middle_kernel(blocks, *refs):
    sources, refs = refs[:9], refs[9:]
    own_coef, pair, other, params, place_of = refs[:5]
    outs, (*levels, coef, sems) = refs[5:13], refs[13:]
    copies = Copies(sems)
    places = ((0, -4), (0, 0), (0, 12), (0, 16), (1, 2), (1, 10), (2, 4), (2, 8), (3, 6))
    waits = [[] for _ in range(STEPS)]
    for source, (level, row) in zip(sources, places):
        waits[level].append(copies.start(source, region(levels, level, row, blocks)))
    waits[0] += load_coef(copies, own_coef, pair, other, place_of, coef)
    places = [(k + 1, row) for k in range(STEPS) for row in (2 * k - 2, ROWS + 2 - GROUP - 2 * k)]
    sends = [
        copies.make(region(levels, level, row, blocks), out)
        for out, (level, row) in zip(outs, places)
    ]
    edge_steps(2, blocks, waits, sends, levels, coef, params)
    for copy in sends:
        copy.wait()


def last_kernel(blocks, *refs):
    sources, refs = refs[:12], refs[12:]
    own_coef, pair, other, params, place_of, cell_of, shift_of = refs[:7]
    low_out, high_out, predicted, *levels, coef, sems = refs[7:]
    copies = Copies(sems)
    places = (
        (0, -8), (0, -4), (0, 16), (0, 20),
        (1, -2), (1, 14), (2, 0), (2, 12), (3, 2), (3, 10), (4, 4), (4, 8),
    )
    waits = [[] for _ in range(STEPS + 1)]
    for source, (level, row) in zip(sources, places):
        waits[level].append(copies.start(source, region(levels, level, row, blocks)))
    waits[0] += load_coef(copies, own_coef, pair, other, place_of, coef)
    edge_steps(6, blocks, waits, (), levels, coef, params)
    for copy in waits[STEPS]:
        copy.wait()
    sends = [
        copies.start(region(levels, STEPS, row, blocks), out)
        for row, out in ((0, low_out), (ROWS - GROUP, high_out))
    ]
    lane = lax.broadcasted_iota(jnp.int32, (SUBLANES, LANES), 1)

    @pl.loop(0, predicted.shape[1] // LANES)
    def _(block):
        base = block * LANES

        def some(part, found):
            for i in range(PICKED):
                o = part * PICKED + i
                value = pltpu.roll(levels[STEPS][cell_of[base + o]], shift_of[base + o], 1)
                found = jnp.where(lane == o, value, found)
            return found

        empty = jnp.zeros((SUBLANES, LANES), jnp.float32)
        predicted[:, block_at(block)] = lax.fori_loop(0, LANES // PICKED, some, empty)

    for copy in sends:
        copy.wait()


def field_kernel(blocks, first_part, count, *refs):
    sources, refs = refs[: ROWS // GROUP], refs[-6:]
    out, cells, mixed, staged, sems, out_sems = refs
    copies = Copies(sems)
    width = count * FOLD
    waits = [
        copies.start(
            source.at[pl.ds(row * blocks + first_part * FOLD, width)],
            cells.at[pl.ds((i * GROUP + row) * width, width)],
        )
        for i, source in enumerate(sources)
        for row in range(GROUP)
    ]
    for copy in waits:
        copy.wait()
    lines = ROWS * SUBLANES

    def line_at(part, row):
        return pl.ds(pl.multiple_of(part * lines + row * SUBLANES, SUBLANES), SUBLANES)

    @pl.loop(0, count)
    def _(part):
        for row in range(ROWS):
            for p in range(FOLD):
                mixed[line_at(part, row), block_at(p)] = cells[row * width + part * FOLD + p]

    mixed[...] = dealt(mixed[...], back=True)

    def out_copy(block):
        return pltpu.make_async_copy(
            staged.at[block], out.at[:, block_at(first_part * FOLD + block)], out_sems.at[block]
        )

    @pl.loop(0, count)
    def _(part):
        for q in range(FOLD):
            block = part * FOLD + q
            for row in range(ROWS):
                staged[block, pl.ds(row, SUBLANES, stride=ROWS), :] = mixed[
                    line_at(part, row), block_at(q)
                ]
            out_copy(block).start()

    @pl.loop(0, width)
    def _(block):
        out_copy(block).wait()


def scratch(columns, *more):
    blocks = columns // LANES
    return [
        *[pltpu.VMEM((ALL_ROWS * blocks, SUBLANES, LANES), jnp.float32)] * (STEPS + 1),
        pltpu.VMEM((blocks, 4 * ALL_ROWS, LANES), jnp.float32),
        *more,
    ]


def kernel_call(body, name, outs, specs, out_specs, scratches, cost, operands, aliases={}):
    return pl.pallas_call(
        body,
        out_shape=tuple(jax.ShapeDtypeStruct(shape, jnp.float32) for shape in outs),
        in_specs=specs,
        out_specs=out_specs,
        scratch_shapes=scratches,
        compiler_params=pltpu.CompilerParams(vmem_limit_bytes=TALL_LIMIT),
        cost_estimate=pl.CostEstimate(flops=0, bytes_accessed=cost * COST_BYTES, transcendentals=0),
        input_output_aliases=aliases,
        name=name,
    )(*operands)


def row_groups(tracer, coefficients, params, place_of):
    members, rows, columns = tracer.shape
    if members != SUBLANES or rows != ROWS or columns % (FOLD * LANES):
        raise ValueError("block shape")
    blocks = columns // LANES
    parts = blocks // FOLD
    flat = tracer.reshape(members * rows, columns)
    dma = pltpu.SemaphoreType.DMA
    staged = [pltpu.VMEM((blocks, members * rows, LANES), jnp.float32), dma((blocks,))]

    def mixed(lines):
        return pltpu.VMEM((parts * lines, FOLD * LANES), jnp.float32)

    group, edge = (GROUP * blocks, members, LANES), (blocks, HALO, LANES)
    up, down, up_coef, down_coef = kernel_call(
        functools.partial(outer_rows_kernel, blocks), "outer_rows",
        [group, group, edge, edge], [ANYWHERE, ANYWHERE, IN_SMEM], (IN_VMEM,) * 4,
        [pltpu.VMEM((rows, columns), jnp.float32), dma, mixed(2 * GROUP * members + rows)] + staged, 3,
        [flat, coefficients, place_of],
    )
    low, high, by_block, dealt_params = kernel_call(
        functools.partial(inner_rows_kernel, blocks), "inner_rows",
        [group, group, (blocks, 4 * rows, LANES), params.shape],
        [ANYWHERE, ANYWHERE, IN_VMEM, ANYWHERE], (IN_VMEM,) * 4,
        [
            pltpu.VMEM((4, rows, columns), jnp.float32), dma,
            mixed(2 * GROUP * members + 4 * rows + members),
        ] + staged, 3,
        [flat, coefficients, params, up],
    )
    return (down, low, high, up), (up_coef, down_coef), by_block, dealt_params


def transport(shape, own, low0, high0, own_coef, pair, other, params, place_of, obs_index, halos, share_params):
    members, rows, columns = shape
    blocks = columns // LANES
    group = (GROUP * blocks, members, LANES)
    flat = (members * rows, columns)
    dma = pltpu.SemaphoreType.DMA
    inner = kernel_call(
        functools.partial(interior_kernel, blocks), "interior",
        [group] * 5, [ANYWHERE] * 5 + [IN_VMEM], (ANYWHERE,) * 5,
        scratch(columns, dma((16,))), 8, [*own, own_coef, params],
    )
    upper, lower, low0, high0, *_ = lax.optimization_barrier(
        (own[2], own[1], low0, high0, inner[0])
    )
    low1, high1 = halos(upper, lower)
    first = kernel_call(
        functools.partial(middle_kernel, blocks), "edge_first",
        [group] * 8, [ANYWHERE] * 12 + [IN_VMEM, IN_SMEM], (ANYWHERE,) * 8,
        scratch(columns, dma((29,))), 10,
        [low0, own[0], own[3], high0, *inner, own_coef, pair, other, params, place_of],
    )
    *first, share_0, share_1 = lax.optimization_barrier((*first, *share_params(inner[0])))
    all_params = (share_0, share_1)
    obs_row, obs_col = obs_index // columns, obs_index % columns
    width = FOLD * LANES
    obs_block = obs_col // width * FOLD + obs_col % FOLD
    cell_of = (HALO + obs_row) * blocks + obs_block
    lane_of = obs_col % width // FOLD
    shift_of = (jnp.arange(obs_index.shape[0], dtype=jnp.int32) - lane_of) % LANES
    low4, high4, predicted = kernel_call(
        functools.partial(last_kernel, blocks), "edge_last",
        [group, group, (members, obs_index.shape[0])],
        [ANYWHERE] * 15 + [IN_VMEM] + [IN_SMEM] * 3, (ANYWHERE, ANYWHERE, IN_VMEM),
        scratch(columns, dma((31,))), 15,
        [low1, low0, high0, high1, *first, own_coef, pair, other, params, place_of, cell_of, shift_of],
    )

    def write_field(index, field):
        parts = blocks // FOLD
        first_part = parts * index // FIELD_CALLS
        count = parts * (index + 1) // FIELD_CALLS - first_part
        width = count * FOLD
        previous = [] if field is None else [field]
        return kernel_call(
            functools.partial(field_kernel, blocks, first_part, count), "field_%d" % index,
            [flat], [ANYWHERE] * (4 + len(previous)), (ANYWHERE,),
            [
                pltpu.VMEM((rows * width, members, LANES), jnp.float32),
                pltpu.VMEM((members * rows * count, FOLD * LANES), jnp.float32),
                pltpu.VMEM((width, members * rows, LANES), jnp.float32),
                dma((rows,)), dma((width,)),
            ],
            4, [low4, first[6], first[7], high4, *previous], {4: 0} if previous else {},
        )[0]

    return write_field, predicted, all_params


def products_kernel(
    total_obs, per_group, spread, own, second, third, fourth, values, variance, same, out
):
    weight = 1.0 / (variance[...] * total_obs)
    predicted = jnp.concatenate([own[...], second[...], third[...], fourth[...]], axis=0)
    innovation = (values[...] - own[...]) * weight
    anomalies = (predicted - hdot(same[...], predicted) / per_group) * spread
    right = jnp.concatenate([anomalies * weight, innovation], axis=0)
    out[...] = lax.dot_general(
        anomalies,
        right,
        (((1,), (1,)), ((), ())),
        precision=lax.Precision.HIGHEST,
        preferred_element_type=jnp.float32,
    )


def update_kernel(per_group, summands, same, own_same, rank_row, rank_col, anomalies, own, out):
    members = same.shape[0]
    total = summands[0]
    for index in range(1, summands.shape[0]):
        total = total + summands[index]
    together = same[...]
    row = lax.broadcasted_iota(jnp.int32, (members, members), 0)
    col = lax.broadcasted_iota(jnp.int32, (members, members), 1)
    system = jnp.where(row == col, 1.0, 0.0) + together * total[:, 0:members]
    right = own_same[...] * total[:, members:]
    for pivot in range(per_group):
        pick = jnp.where(rank_row[...] == pivot, together, 0.0)
        pivot_system = hdot(pick, system)
        pivot_right = hdot(pick, right)
        pivot_value = jnp.sum(pick * pivot_system, axis=1, keepdims=True)
        factor = jnp.sum(pick * system, axis=1, keepdims=True)
        is_pivot = rank_col[...] == pivot
        scale = 1.0 / pivot_value
        scaled_system, scaled_right = pivot_system * scale, pivot_right * scale
        system = jnp.where(is_pivot, scaled_system, system - factor * scaled_system)
        right = jnp.where(is_pivot, scaled_right, right - factor * scaled_right)
    change = lax.dot_general(
        right,
        anomalies[...],
        (((0,), (0,)), ((), ())),
        precision=lax.Precision.HIGHEST,
        preferred_element_type=jnp.float32,
    )
    out[...] = own[...] + change


def local(tracer, coefficients, parameters, obs_index, obs_values, obs_variance, member_group):
    local_members, rows, columns = tracer.shape
    ens_pos = lax.axis_index("ens")
    ens_count = lax.axis_size("ens")
    slab_count = lax.axis_size("slab")
    if ens_count != 4 or coefficients.shape[0] != 4 or slab_count & (slab_count - 1):
        raise ValueError("mesh shape")
    forward = [(i, i + 1) for i in range(slab_count - 1)]
    backward = [(target, source) for source, target in forward]

    def next_core(value):
        return lax.ppermute(value, "ens", [(i, i ^ 1) for i in range(ens_count)])

    def next_chip(value):
        return lax.ppermute(value, "ens", [(i, i ^ 2) for i in range(ens_count)])

    def over_ens(mine):
        pair = jnp.stack([mine, next_core(mine)])
        return pair, next_chip(pair)

    def halos(upper, lower):
        return lax.ppermute(upper, "slab", forward), lax.ppermute(lower, "slab", backward)

    place_of = jnp.reshape(ens_pos, (1,))
    own, coef_edges, own_coef, dealt_params = row_groups(
        tracer, coefficients, parameters, place_of
    )
    low0, high0 = halos(own[3], own[0])

    edge_low, edge_high = halos(*coef_edges)
    pair, other = over_ens(jnp.stack([edge_low, edge_high]))

    members = member_group.shape[0]
    per_group = members // GROUPS
    spread = 1.0 / math.sqrt(per_group - 1)
    blocks_of = member_group.reshape(ens_count, local_members)
    group_of = jnp.concatenate(
        [lax.dynamic_index_in_dim(blocks_of, ens_pos ^ i, 0, False) for i in range(ens_count)]
    )
    same_bool = group_of[:, None] == group_of[None, :]
    same = same_bool.astype(jnp.float32)
    earlier = jnp.arange(members)[None, :] < jnp.arange(members)[:, None]
    rank = jnp.sum((same_bool & earlier).astype(jnp.int32), axis=1)

    def share_params(after):
        later, _ = lax.optimization_barrier((parameters, after))
        return over_ens(later)

    write_field, predicted, all_params = transport(
        tracer.shape, own, low0, high0,
        own_coef, pair, other, dealt_params, place_of, obs_index, halos, share_params,
    )
    all_params = jnp.concatenate(all_params, axis=0).reshape(members, columns)
    param_anomalies = (all_params - hdot(same, all_params) / per_group) * spread

    others = [
        lax.ppermute(predicted, "ens", [(i, i ^ step) for i in range(ens_count)])
        for step in range(1, ens_count)
    ]
    *others, field = lax.optimization_barrier((*others, write_field(0, None)))
    total_obs = obs_variance.shape[0] * slab_count
    products = pl.pallas_call(
        functools.partial(products_kernel, float(total_obs), per_group, spread),
        out_shape=jax.ShapeDtypeStruct((members, members + local_members), jnp.float32),
        compiler_params=pltpu.CompilerParams(vmem_limit_bytes=VMEM_LIMIT),
        name="products",
    )(predicted, *others, obs_values, obs_variance[None, :], same)
    distance = 1
    while distance < slab_count:
        radix = 4 if slab_count // distance % 4 == 0 else 2
        arrived = [
            lax.ppermute(products, "slab", [(i, i ^ (step * distance)) for i in range(slab_count)])
            for step in range(1, radix)
        ]
        if distance == 1:
            *arrived, field = lax.optimization_barrier((*arrived, write_field(1, field)))
        products = products + arrived[0]
        if radix == 4:
            products = products + (arrived[1] + arrived[2])
        distance *= radix
    updated = pl.pallas_call(
        functools.partial(update_kernel, per_group),
        out_shape=jax.ShapeDtypeStruct(parameters.shape, jnp.float32),
        compiler_params=pltpu.CompilerParams(vmem_limit_bytes=VMEM_LIMIT),
        name="update",
    )(
        products[None], same, same[:, :local_members], rank[None, :], rank[:, None],
        param_anomalies, parameters,
    )
    return (field.reshape(tracer.shape), updated)


def solution(mesh):
    in_specs = (
        P("ens", "slab", None),
        P(None, "slab", None),
        P("ens", None),
        P("slab"),
        P("ens", "slab"),
        P("slab"),
        P(),
    )
    out_specs = (P("ens", "slab", None), P("ens", None))
    return jax.shard_map(local, mesh=mesh, in_specs=in_specs, out_specs=out_specs, check_vma=False)
```

```python
import functools
import math

import jax
import jax.numpy as jnp
from jax import lax
from jax.experimental import pallas as pl
from jax.experimental.pallas import tpu as pltpu
from jax.sharding import PartitionSpec as P

STEPS = 4
GROUPS = 8
HALO = 2 * STEPS
LANES = 128
SUBLANES = 8
ROWS = 16
GROUP = 4
FOLD = 4
CHAINS = 4
TILES = 4
FIELD_CALLS = 2
ALL_ROWS = ROWS + 2 * HALO
VMEM_LIMIT = 16 * 1024 * 1024
TALL_LIMIT = 60 * 1024 * 1024
COST_BYTES = 200000
ANYWHERE = pl.BlockSpec(memory_space=pltpu.HBM)
IN_VMEM = pl.BlockSpec(memory_space=pltpu.VMEM)
IN_SMEM = pl.BlockSpec(memory_space=pltpu.SMEM)


def hdot(left, right):
    return jnp.dot(left, right, precision=lax.Precision.HIGHEST, preferred_element_type=jnp.float32)


def limited(left, right):
    return jnp.minimum(jnp.maximum(left, jnp.minimum(right, 0.0)), jnp.maximum(right, 0.0))


def block_at(block):
    return pl.ds(pl.multiple_of(block * LANES, LANES), LANES)


def everywhere(coef, block, place):
    return coef[block, pl.ds(place, SUBLANES, stride=0), :]


def edge_lanes():
    lane = lax.broadcasted_iota(jnp.int32, (SUBLANES, LANES), 1)
    return lane == 0, lane == LANES - 1


def dealt(values, back=False):
    shape = (FOLD * LANES, FOLD * LANES)
    natural = lax.broadcasted_iota(jnp.int32, shape, 1 if back else 0)
    place = lax.broadcasted_iota(jnp.int32, shape, 0 if back else 1)
    moves = natural == FOLD * lax.rem(place, LANES) + lax.div(place, LANES)
    moves = jnp.where(moves, 1.0, 0.0).astype(jnp.bfloat16)
    products = []
    for _ in range(3):
        piece = values.astype(jnp.bfloat16)
        products.append(jnp.dot(piece, moves, preferred_element_type=jnp.float32))
        values = values - piece.astype(jnp.float32)
    return products[0] + (products[1] + products[2])


def stencil(line, speeds):
    d = [line[i + 1] - line[i] for i in range(GROUP + 3)]
    slope = [None] + [limited(d[i - 1], d[i]) for i in range(1, GROUP + 3)]
    twice = [None] + [d[i] + d[i] for i in range(1, GROUP + 2)]
    results = []
    for i in range(2, GROUP + 2):
        speed = speeds[i - 2]
        forward = twice[i - 1] - slope[i - 1]
        backward = twice[i] - slope[i + 1]
        flux = speed * (jnp.where(speed > 0.0, forward, backward) + slope[i])
        results.append((flux, d[i] - d[i - 1]))
    return results


def advance_tile(cell, places, part, parts, source, target, coef, params, blocks):
    start = part * FOLD
    before = lax.rem(part + parts - 1, parts) * FOLD
    after = lax.rem(part + 1, parts) * FOLD
    first, last = edge_lanes()
    own = [
        [source[cell + (i - 2) * blocks + start + p] for p in range(FOLD)] for i in range(GROUP + 4)
    ]
    along_rows = [
        stencil(
            [own[i][p] for i in range(GROUP + 4)],
            [everywhere(coef, start + p, places[i][0]) for i in range(GROUP)],
        )
        for p in range(FOLD)
    ]
    for i in range(GROUP):
        row = own[i + 2]
        here = cell + i * blocks
        left = [
            jnp.where(first, pltpu.roll(source[here + before + p], 1, 1), pltpu.roll(row[p], 1, 1))
            for p in (FOLD - 2, FOLD - 1)
        ]
        right = [
            jnp.where(
                last,
                pltpu.roll(source[here + after + p], LANES - 1, 1),
                pltpu.roll(row[p], LANES - 1, 1),
            )
            for p in (0, 1)
        ]
        along_columns = stencil(
            [*left, *row, *right], [everywhere(coef, start + p, places[i][1]) for p in range(FOLD)]
        )
        for p in range(FOLD):
            flux_x, lap_x = along_rows[p][i]
            flux_y, lap_y = along_columns[p]
            value = row[p] - 0.5 * (flux_x + flux_y)
            value = value + everywhere(coef, start + p, places[i][2]) * (lap_x + lap_y)
            value = value + params[:, block_at(start + p)] * everywhere(coef, start + p, places[i][3])
            target[here + start + p] = value


def advance_group(source, target, row, coef, params, blocks):
    cell = row * blocks
    places = [[coef_row(array, row + i) for array in range(4)] for i in range(GROUP)]
    parts = blocks // FOLD

    @pl.loop(0, parts // TILES)
    def _(some):
        for k in range(TILES):
            advance_tile(
                cell, places, some * TILES + k, parts, source, target, coef, params, blocks
            )


class Copies:
    def __init__(self, sems):
        self.sems, self.used = sems, 0

    def make(self, source, target):
        copy = pltpu.make_async_copy(source, target, self.sems.at[self.used])
        self.used += 1
        assert self.used <= self.sems.shape[0]
        return copy

    def start(self, source, target):
        copy = self.make(source, target)
        copy.start()
        return copy


def region(levels, level, row, blocks):
    return levels[level].at[pl.ds((HALO + row) * blocks, GROUP * blocks)]


def fill_rows(blocks, first_rows, tracer, mixed, staged, sems):
    def copy(block):
        return pltpu.make_async_copy(tracer.at[:, block_at(block)], staged.at[block], sems.at[block])

    @pl.loop(0, blocks)
    def _(block):
        copy(block).start()

    lines = len(first_rows) * GROUP * SUBLANES

    @pl.loop(0, blocks // FOLD)
    def _(part):
        for q in range(FOLD):
            block = part * FOLD + q
            copy(block).wait()
            for k, first_row in enumerate(first_rows):
                for row in range(GROUP):
                    line = part * lines + (k * GROUP + row) * SUBLANES
                    mixed[pl.ds(pl.multiple_of(line, SUBLANES), SUBLANES), block_at(q)] = staged[
                        block, pl.ds(first_row + row, SUBLANES, stride=ROWS), :
                    ]


def take_rows(blocks, mixed, outs):
    lines = len(outs) * GROUP * SUBLANES

    @pl.loop(0, blocks // FOLD)
    def _(part):
        for k, out in enumerate(outs):
            for row in range(GROUP):
                line = part * lines + (k * GROUP + row) * SUBLANES
                for p in range(FOLD):
                    out[row * blocks + part * FOLD + p] = mixed[
                        pl.ds(pl.multiple_of(line, SUBLANES), SUBLANES), block_at(p)
                    ]


def outer_rows_kernel(
    blocks, tracer, own_coef, place_of, up, down, up_coef, down_coef, edge, edge_sem, mixed, staged, sems
):
    copy = pltpu.make_async_copy(own_coef.at[place_of[0]], edge, edge_sem)
    copy.start()
    fill_rows(blocks, (0, ROWS - GROUP), tracer, mixed, staged, sems)
    copy.wait()
    parts = blocks // FOLD
    field_lines = parts * 2 * GROUP * SUBLANES
    width = FOLD * LANES
    for part in range(parts):
        mixed[field_lines + part * ROWS : field_lines + (part + 1) * ROWS, :] = edge[
            :, part * width : (part + 1) * width
        ]
    mixed[...] = dealt(mixed[...])
    take_rows(blocks, mixed, (down, up))
    for part in range(parts):
        line = field_lines + part * ROWS
        for p in range(FOLD):
            down_coef[part * FOLD + p] = mixed[line : line + HALO, block_at(p)]
            up_coef[part * FOLD + p] = mixed[line + ROWS - HALO : line + ROWS, block_at(p)]


def inner_rows_kernel(
    blocks, tracer, own_coef, params, outer, low, high, by_block, dealt_params, whole, coef_sem, mixed,
    staged, sems,
):
    copy = pltpu.make_async_copy(own_coef, whole, coef_sem)
    copy.start()
    fill_rows(blocks, (GROUP, ROWS - 2 * GROUP), tracer, mixed, staged, sems)
    copy.wait()
    parts = blocks // FOLD
    coef_lines = parts * 2 * GROUP * SUBLANES
    param_lines = coef_lines + parts * 4 * ROWS
    width = FOLD * LANES
    for part in range(parts):
        at = slice(part * width, (part + 1) * width)
        for array in range(4):
            line = coef_lines + (part * 4 + array) * ROWS
            mixed[line : line + ROWS, :] = whole[array, :, at]
        line = param_lines + part * SUBLANES
        mixed[line : line + SUBLANES, :] = params[:, at]
    mixed[...] = dealt(mixed[...])
    take_rows(blocks, mixed, (low, high))
    for part in range(parts):
        line = coef_lines + part * 4 * ROWS
        for p in range(FOLD):
            block = part * FOLD + p
            by_block[block] = mixed[line : line + 4 * ROWS, block_at(p)]
            dealt_params[:, block_at(block)] = mixed[
                param_lines + part * SUBLANES : param_lines + (part + 1) * SUBLANES, block_at(p)
            ]


def interior_kernel(blocks, own0, own1, own2, own3, own_coef, params, *rest):
    outs, (*levels, coef, sems) = rest[:5], rest[5:]
    copies = Copies(sems)
    waits = [
        copies.start(own, region(levels, 0, GROUP * i, blocks))
        for i, own in enumerate((own0, own1, own2, own3))
    ]
    waits.append(copies.start(own_coef, coef.at[:, 0 : 4 * ROWS]))
    for copy in waits:
        copy.wait()

    for level, start, count in ((0, 2, 3), (1, 4, 2), (2, 6, 1)):
        @pl.loop(0, count)
        def _(i):
            row = start + HALO + GROUP * i
            advance_group(levels[level], levels[level + 1], row, coef, params, blocks)

    waits = [
        copies.start(region(levels, level, row, blocks), out)
        for out, (level, row) in zip(outs, ((1, 2), (1, 10), (2, 4), (2, 8), (3, 6)))
    ]
    for copy in waits:
        copy.wait()


def edge_steps(outer, blocks, waits, sends, levels, coef, params):
    for level in range(STEPS):
        for copy in waits[level]:
            copy.wait()
        low, high = 2 * level - outer, ROWS + outer - GROUP - 2 * level

        @pl.loop(0, 2)
        def _(side):
            row = low + HALO + side * (high - low)
            advance_group(levels[level], levels[level + 1], row, coef, params, blocks)

        for copy in sends[2 * level : 2 * level + 2]:
            copy.start()


def coef_row(array, row):
    own = array * ROWS + row - HALO
    low = 4 * ROWS + 2 * HALO * array + row
    high = 4 * ROWS + 2 * HALO * array + row - ROWS
    return jnp.where(row < HALO, low, jnp.where(row < HALO + ROWS, own, high))


def load_coef(copies, own_coef, pair, other, place_of, coef):
    waits = [copies.start(own_coef, coef.at[:, 0 : 4 * ROWS])]
    for number, source in enumerate((pair.at[0], pair.at[1], other.at[0], other.at[1])):
        array = jnp.bitwise_xor(place_of[0], number)
        for side in range(2):
            first = 4 * ROWS + 2 * HALO * array + HALO * side
            waits.append(copies.start(source.at[side], coef.at[:, pl.ds(first, HALO)]))
    return waits


def middle_kernel(blocks, *refs):
    sources, refs = refs[:9], refs[9:]
    own_coef, pair, other, params, place_of = refs[:5]
    outs, (*levels, coef, sems) = refs[5:13], refs[13:]
    copies = Copies(sems)
    places = ((0, -4), (0, 0), (0, 12), (0, 16), (1, 2), (1, 10), (2, 4), (2, 8), (3, 6))
    waits = [[] for _ in range(STEPS)]
    for source, (level, row) in zip(sources, places):
        waits[level].append(copies.start(source, region(levels, level, row, blocks)))
    waits[0] += load_coef(copies, own_coef, pair, other, place_of, coef)
    places = [(k + 1, row) for k in range(STEPS) for row in (2 * k - 2, ROWS + 2 - GROUP - 2 * k)]
    sends = [
        copies.make(region(levels, level, row, blocks), out)
        for out, (level, row) in zip(outs, places)
    ]
    edge_steps(2, blocks, waits, sends, levels, coef, params)
    for copy in sends:
        copy.wait()


def last_kernel(blocks, *refs):
    sources, refs = refs[:12], refs[12:]
    own_coef, pair, other, params, place_of, cell_of, shift_of = refs[:7]
    low_out, high_out, predicted, *levels, coef, sems = refs[7:]
    copies = Copies(sems)
    places = (
        (0, -8), (0, -4), (0, 16), (0, 20),
        (1, -2), (1, 14), (2, 0), (2, 12), (3, 2), (3, 10), (4, 4), (4, 8),
    )
    waits = [[] for _ in range(STEPS + 1)]
    for source, (level, row) in zip(sources, places):
        waits[level].append(copies.start(source, region(levels, level, row, blocks)))
    waits[0] += load_coef(copies, own_coef, pair, other, place_of, coef)
    edge_steps(6, blocks, waits, (), levels, coef, params)
    for copy in waits[STEPS]:
        copy.wait()
    sends = [
        copies.start(region(levels, STEPS, row, blocks), out)
        for row, out in ((0, low_out), (ROWS - GROUP, high_out))
    ]
    lane = lax.broadcasted_iota(jnp.int32, (SUBLANES, LANES), 1)

    @pl.loop(0, predicted.shape[1] // LANES)
    def _(block):
        base = block * LANES

        found = [jnp.zeros((SUBLANES, LANES), jnp.float32)] * CHAINS
        for o in range(LANES):
            value = pltpu.roll(levels[STEPS][cell_of[base + o]], shift_of[base + o], 1)
            found[o % CHAINS] = jnp.where(lane == o, value, found[o % CHAINS])
        picked = found[0]
        for k in range(1, CHAINS):
            picked = jnp.where(lax.rem(lane, CHAINS) == k, found[k], picked)
        predicted[:, block_at(block)] = picked

    for copy in sends:
        copy.wait()


def field_kernel(blocks, first_part, count, *refs):
    sources, refs = refs[: ROWS // GROUP], refs[-6:]
    out, cells, mixed, staged, sems, out_sems = refs
    copies = Copies(sems)
    width = count * FOLD
    waits = [
        copies.start(
            source.at[pl.ds(row * blocks + first_part * FOLD, width)],
            cells.at[pl.ds((i * GROUP + row) * width, width)],
        )
        for i, source in enumerate(sources)
        for row in range(GROUP)
    ]
    for copy in waits:
        copy.wait()
    lines = ROWS * SUBLANES

    def line_at(part, row):
        return pl.ds(pl.multiple_of(part * lines + row * SUBLANES, SUBLANES), SUBLANES)

    @pl.loop(0, count)
    def _(part):
        for row in range(ROWS):
            for p in range(FOLD):
                mixed[line_at(part, row), block_at(p)] = cells[row * width + part * FOLD + p]

    mixed[...] = dealt(mixed[...], back=True)

    def out_copy(block):
        return pltpu.make_async_copy(
            staged.at[block], out.at[:, block_at(first_part * FOLD + block)], out_sems.at[block]
        )

    @pl.loop(0, count)
    def _(part):
        for q in range(FOLD):
            block = part * FOLD + q
            for row in range(ROWS):
                staged[block, pl.ds(row, SUBLANES, stride=ROWS), :] = mixed[
                    line_at(part, row), block_at(q)
                ]
            out_copy(block).start()

    @pl.loop(0, width)
    def _(block):
        out_copy(block).wait()


def scratch(columns, *more):
    blocks = columns // LANES
    return [
        *[pltpu.VMEM((ALL_ROWS * blocks, SUBLANES, LANES), jnp.float32)] * (STEPS + 1),
        pltpu.VMEM((blocks, 4 * ALL_ROWS, LANES), jnp.float32),
        *more,
    ]


def kernel_call(body, name, outs, specs, out_specs, scratches, cost, operands, aliases={}):
    return pl.pallas_call(
        body,
        out_shape=tuple(jax.ShapeDtypeStruct(shape, jnp.float32) for shape in outs),
        in_specs=specs,
        out_specs=out_specs,
        scratch_shapes=scratches,
        compiler_params=pltpu.CompilerParams(vmem_limit_bytes=TALL_LIMIT),
        cost_estimate=pl.CostEstimate(flops=0, bytes_accessed=cost * COST_BYTES, transcendentals=0),
        input_output_aliases=aliases,
        name=name,
    )(*operands)


def row_groups(tracer, coefficients, params, place_of):
    members, rows, columns = tracer.shape
    if members != SUBLANES or rows != ROWS or columns % (FOLD * LANES):
        raise ValueError("block shape")
    blocks = columns // LANES
    parts = blocks // FOLD
    flat = tracer.reshape(members * rows, columns)
    dma = pltpu.SemaphoreType.DMA
    staged = [pltpu.VMEM((blocks, members * rows, LANES), jnp.float32), dma((blocks,))]

    def mixed(lines):
        return pltpu.VMEM((parts * lines, FOLD * LANES), jnp.float32)

    group, edge = (GROUP * blocks, members, LANES), (blocks, HALO, LANES)
    up, down, up_coef, down_coef = kernel_call(
        functools.partial(outer_rows_kernel, blocks), "outer_rows",
        [group, group, edge, edge], [ANYWHERE, ANYWHERE, IN_SMEM], (IN_VMEM,) * 4,
        [pltpu.VMEM((rows, columns), jnp.float32), dma, mixed(2 * GROUP * members + rows)] + staged, 3,
        [flat, coefficients, place_of],
    )
    low, high, by_block, dealt_params = kernel_call(
        functools.partial(inner_rows_kernel, blocks), "inner_rows",
        [group, group, (blocks, 4 * rows, LANES), params.shape],
        [ANYWHERE, ANYWHERE, IN_VMEM, ANYWHERE], (IN_VMEM,) * 4,
        [
            pltpu.VMEM((4, rows, columns), jnp.float32), dma,
            mixed(2 * GROUP * members + 4 * rows + members),
        ] + staged, 3,
        [flat, coefficients, params, up],
    )
    return (down, low, high, up), (up_coef, down_coef), by_block, dealt_params


def transport(shape, own, low0, high0, own_coef, pair, other, params, place_of, obs_index, halos, share_params):
    members, rows, columns = shape
    blocks = columns // LANES
    group = (GROUP * blocks, members, LANES)
    flat = (members * rows, columns)
    dma = pltpu.SemaphoreType.DMA
    inner = kernel_call(
        functools.partial(interior_kernel, blocks), "interior",
        [group] * 5, [ANYWHERE] * 5 + [IN_VMEM], (ANYWHERE,) * 5,
        scratch(columns, dma((16,))), 8, [*own, own_coef, params],
    )
    upper, lower, low0, high0, *_ = lax.optimization_barrier(
        (own[2], own[1], low0, high0, inner[0])
    )
    low1, high1 = halos(upper, lower)
    first = kernel_call(
        functools.partial(middle_kernel, blocks), "edge_first",
        [group] * 8, [ANYWHERE] * 12 + [IN_VMEM, IN_SMEM], (ANYWHERE,) * 8,
        scratch(columns, dma((29,))), 10,
        [low0, own[0], own[3], high0, *inner, own_coef, pair, other, params, place_of],
    )
    *first, share_0, share_1 = lax.optimization_barrier((*first, *share_params(inner[0])))
    all_params = (share_0, share_1)
    obs_row, obs_col = obs_index // columns, obs_index % columns
    width = FOLD * LANES
    obs_block = obs_col // width * FOLD + obs_col % FOLD
    cell_of = (HALO + obs_row) * blocks + obs_block
    lane_of = obs_col % width // FOLD
    shift_of = (jnp.arange(obs_index.shape[0], dtype=jnp.int32) - lane_of) % LANES
    low4, high4, predicted = kernel_call(
        functools.partial(last_kernel, blocks), "edge_last",
        [group, group, (members, obs_index.shape[0])],
        [ANYWHERE] * 15 + [IN_VMEM] + [IN_SMEM] * 3, (ANYWHERE, ANYWHERE, IN_VMEM),
        scratch(columns, dma((31,))), 15,
        [low1, low0, high0, high1, *first, own_coef, pair, other, params, place_of, cell_of, shift_of],
    )

    def write_field(index, field):
        parts = blocks // FOLD
        first_part = parts * index // FIELD_CALLS
        count = parts * (index + 1) // FIELD_CALLS - first_part
        width = count * FOLD
        previous = [] if field is None else [field]
        return kernel_call(
            functools.partial(field_kernel, blocks, first_part, count), "field_%d" % index,
            [flat], [ANYWHERE] * (4 + len(previous)), (ANYWHERE,),
            [
                pltpu.VMEM((rows * width, members, LANES), jnp.float32),
                pltpu.VMEM((members * rows * count, FOLD * LANES), jnp.float32),
                pltpu.VMEM((width, members * rows, LANES), jnp.float32),
                dma((rows,)), dma((width,)),
            ],
            4, [low4, first[6], first[7], high4, *previous], {4: 0} if previous else {},
        )[0]

    return write_field, predicted, all_params


def products_kernel(
    total_obs, per_group, spread, own, second, third, fourth, values, variance, same, out
):
    weight = 1.0 / (variance[...] * total_obs)
    predicted = jnp.concatenate([own[...], second[...], third[...], fourth[...]], axis=0)
    innovation = (values[...] - own[...]) * weight
    anomalies = (predicted - hdot(same[...], predicted) / per_group) * spread
    right = jnp.concatenate([anomalies * weight, innovation], axis=0)
    out[...] = lax.dot_general(
        anomalies,
        right,
        (((1,), (1,)), ((), ())),
        precision=lax.Precision.HIGHEST,
        preferred_element_type=jnp.float32,
    )


def update_kernel(per_group, summands, same, own_same, rank_row, rank_col, anomalies, own, out):
    members = same.shape[0]
    total = summands[0]
    for index in range(1, summands.shape[0]):
        total = total + summands[index]
    together = same[...]
    row = lax.broadcasted_iota(jnp.int32, (members, members), 0)
    col = lax.broadcasted_iota(jnp.int32, (members, members), 1)
    system = jnp.where(row == col, 1.0, 0.0) + together * total[:, 0:members]
    right = own_same[...] * total[:, members:]
    for pivot in range(per_group):
        pick = jnp.where(rank_row[...] == pivot, together, 0.0)
        pivot_system = hdot(pick, system)
        pivot_right = hdot(pick, right)
        pivot_value = jnp.sum(pick * pivot_system, axis=1, keepdims=True)
        factor = jnp.sum(pick * system, axis=1, keepdims=True)
        is_pivot = rank_col[...] == pivot
        scale = 1.0 / pivot_value
        scaled_system, scaled_right = pivot_system * scale, pivot_right * scale
        system = jnp.where(is_pivot, scaled_system, system - factor * scaled_system)
        right = jnp.where(is_pivot, scaled_right, right - factor * scaled_right)
    change = lax.dot_general(
        right,
        anomalies[...],
        (((0,), (0,)), ((), ())),
        precision=lax.Precision.HIGHEST,
        preferred_element_type=jnp.float32,
    )
    out[...] = own[...] + change


def local(tracer, coefficients, parameters, obs_index, obs_values, obs_variance, member_group):
    local_members, rows, columns = tracer.shape
    ens_pos = lax.axis_index("ens")
    ens_count = lax.axis_size("ens")
    slab_count = lax.axis_size("slab")
    if ens_count != 4 or coefficients.shape[0] != 4 or slab_count & (slab_count - 1):
        raise ValueError("mesh shape")
    forward = [(i, i + 1) for i in range(slab_count - 1)]
    backward = [(target, source) for source, target in forward]

    def next_core(value):
        return lax.ppermute(value, "ens", [(i, i ^ 1) for i in range(ens_count)])

    def next_chip(value):
        return lax.ppermute(value, "ens", [(i, i ^ 2) for i in range(ens_count)])

    def over_ens(mine):
        pair = jnp.stack([mine, next_core(mine)])
        return pair, next_chip(pair)

    def halos(upper, lower):
        return lax.ppermute(upper, "slab", forward), lax.ppermute(lower, "slab", backward)

    place_of = jnp.reshape(ens_pos, (1,))
    own, coef_edges, own_coef, dealt_params = row_groups(
        tracer, coefficients, parameters, place_of
    )
    low0, high0 = halos(own[3], own[0])

    edge_low, edge_high = halos(*coef_edges)
    pair, other = over_ens(jnp.stack([edge_low, edge_high]))

    members = member_group.shape[0]
    per_group = members // GROUPS
    spread = 1.0 / math.sqrt(per_group - 1)
    blocks_of = member_group.reshape(ens_count, local_members)
    group_of = jnp.concatenate(
        [lax.dynamic_index_in_dim(blocks_of, ens_pos ^ i, 0, False) for i in range(ens_count)]
    )
    same_bool = group_of[:, None] == group_of[None, :]
    same = same_bool.astype(jnp.float32)
    earlier = jnp.arange(members)[None, :] < jnp.arange(members)[:, None]
    rank = jnp.sum((same_bool & earlier).astype(jnp.int32), axis=1)

    def share_params(after):
        later, _ = lax.optimization_barrier((parameters, after))
        return over_ens(later)

    write_field, predicted, all_params = transport(
        tracer.shape, own, low0, high0,
        own_coef, pair, other, dealt_params, place_of, obs_index, halos, share_params,
    )
    all_params = jnp.concatenate(all_params, axis=0).reshape(members, columns)
    param_anomalies = (all_params - hdot(same, all_params) / per_group) * spread

    others = [
        lax.ppermute(predicted, "ens", [(i, i ^ step) for i in range(ens_count)])
        for step in range(1, ens_count)
    ]
    *others, field = lax.optimization_barrier((*others, write_field(0, None)))
    total_obs = obs_variance.shape[0] * slab_count
    products = pl.pallas_call(
        functools.partial(products_kernel, float(total_obs), per_group, spread),
        out_shape=jax.ShapeDtypeStruct((members, members + local_members), jnp.float32),
        compiler_params=pltpu.CompilerParams(vmem_limit_bytes=VMEM_LIMIT),
        name="products",
    )(predicted, *others, obs_values, obs_variance[None, :], same)
    distance = 1
    while distance < slab_count:
        radix = 4 if slab_count // distance % 4 == 0 else 2
        arrived = [
            lax.ppermute(products, "slab", [(i, i ^ (step * distance)) for i in range(slab_count)])
            for step in range(1, radix)
        ]
        if distance == 1:
            *arrived, field = lax.optimization_barrier((*arrived, write_field(1, field)))
        products = products + arrived[0]
        if radix == 4:
            products = products + (arrived[1] + arrived[2])
        distance *= radix
    updated = pl.pallas_call(
        functools.partial(update_kernel, per_group),
        out_shape=jax.ShapeDtypeStruct(parameters.shape, jnp.float32),
        compiler_params=pltpu.CompilerParams(vmem_limit_bytes=VMEM_LIMIT),
        name="update",
    )(
        products[None], same, same[:, :local_members], rank[None, :], rank[:, None],
        param_anomalies, parameters,
    )
    return (field.reshape(tracer.shape), updated)


def solution(mesh):
    in_specs = (
        P("ens", "slab", None),
        P(None, "slab", None),
        P("ens", None),
        P("slab"),
        P("ens", "slab"),
        P("slab"),
        P(),
    )
    out_specs = (P("ens", "slab", None), P("ens", None))
    return jax.shard_map(local, mesh=mesh, in_specs=in_specs, out_specs=out_specs, check_vma=False)
```
